128 devices in a mesh: attn: 16 (over y, z), ffn: 8 (over x, core).
Axes of the slice: x: 4, y: 4, z: 4, core: 2. Of those that a mesh axis runs over, the one named last changes fastest.
Arguments:
- query: bfloat16 [512, 8192], P(('attn', 'ffn')), may hold values from -64 to 64
- cached_key_rows: bfloat16 [512, 2048, 256], P(('attn', 'ffn')), may hold values from -4 to 4
- cached_value_rows: bfloat16 [512, 2048, 256], P(('attn', 'ffn')), may hold values from -6 to 6
- request_cache_length: int32 [512], P(('attn', 'ffn')), may hold values from 2 to 2048, as said below
- request_tenant_index: int32 [512], P(('attn', 'ffn')), may hold values from 0 to 7
- residual: bfloat16 [512, 7168], P(None, 'attn'), may hold values from -64 to 64
- feedforward_norm_gain: bfloat16 [7168], P('attn'), may hold values from 0.099609375 to 1.8984375
- attention_output_weight: bfloat16 [8192, 7168], P(None, 'attn'), may hold values from -0.25 to 0.25
- gate_up_weight: bfloat16 [7168, 2, 18432], P('attn', None, 'ffn'), may hold values from -0.09375 to 0.09375
- down_projection_weight: bfloat16 [8, 16, 144, 7168], P('ffn', 'attn'), may hold values from -0.046875 to 0.046875
- adapter_down_maps: bfloat16 [8, 16, 144, 128], P('ffn', 'attn'), may hold values from -0.046875 to 0.046875
- adapter_up_maps: bfloat16 [128, 7168], replicated, may hold values from -1.5 to 1.5
Outputs:
- ffn_out: bfloat16 [512, 7168], P(('attn', 'ffn'))
The draws below stay inside these ranges and needn't reach their ends.
Inputs may be any that keep to these rules, and one draw needn't show every extreme that they name: `request_cache_length`: every request has at least two live slots, and some request fills all 2048 slots.
All inputs are finite; a program needn't handle non-finite values.
Results may differ from the reference program's by a relative error of at most 0.01.
Values may be sent and summed in bfloat16 or wider, within the bound.
A program may use at most 128 MiB of HBM per device.

```python
import jax
import jax.numpy as jnp
from jax import lax

MODEL_WIDTH = 7168
FEEDFWD_HIDDEN = 18432
HQ = 32
HD = 256
CACHE = 2048
TENANT_COUNT = 8
ADAPTER_RANK = 16
TOKENS = 512
C = 8192
BLOCK_HIDDEN = 144
N_ATTN = 16
N_FFN = 8


def first_keys(key):
    base_product = jax.random.normal(jax.random.fold_in(key, 101), (TOKENS, HD), jnp.float32)
    return jnp.clip(base_product, -4.0, 4.0)


def draw_cached_key_rows(key, part):
    first = first_keys(key)
    key = jax.random.fold_in(key, 3)
    base_product = jnp.clip(jax.random.normal(key, (TOKENS, CACHE, HD), jnp.float32), -4.0, 4.0)
    base_product = base_product.at[:, 0, :].set(first)
    return base_product.astype(jnp.bfloat16)


def draw_query(key, part):
    key = jax.random.fold_in(key, 5)
    values = jnp.clip(2.0 * jax.random.normal(key, (TOKENS, HQ, HD), jnp.float32), -8.0, 8.0)
    return values.reshape(TOKENS, HQ * HD).astype(jnp.bfloat16)


def draw_request_cache_length(key, part):
    key = jax.random.fold_in(key, 9)
    first_key, second_key = jax.random.split(key)
    lengths = jax.random.randint(first_key, (TOKENS,), 2, CACHE + 1, jnp.int32)
    chosen = jax.random.randint(second_key, (), 0, TOKENS, jnp.int32)
    return lengths.at[chosen].set(CACHE)


def draw_residual(key, part):
    key = jax.random.fold_in(key, 7)
    key_a, key_b, key_c = jax.random.split(key, 3)
    ramp = 3.0 ** (jnp.arange(MODEL_WIDTH, dtype=jnp.float32) / MODEL_WIDTH)
    row_scale = jnp.exp(jax.random.uniform(key_b, (TOKENS, 1), jnp.float32, -1.15, 1.15))
    col_scale = ramp[None, :] * jnp.exp(jax.random.uniform(key_c, (1, MODEL_WIDTH), jnp.float32, -1.15, 1.15)) / 1.7
    values = jax.random.normal(key_a, (TOKENS, MODEL_WIDTH), jnp.float32)
    return jnp.clip(values * row_scale * col_scale, -64.0, 64.0).astype(jnp.bfloat16)


def place_ends(result, own_key, low, largest):
    index_at = [jax.random.randint(jax.random.fold_in(own_key, axis), (), 0, length) for axis, length in enumerate(result.shape)]
    main_axis = result.shape.index(max(result.shape))
    beside = index_at[:main_axis] + [(index_at[main_axis] + 1) % result.shape[main_axis]] + index_at[main_axis + 1:]
    return result.at[tuple(index_at)].set(low).at[tuple(beside)].set(largest)


def spiked(drawn, stream_key, source, target, blocks, factor):
    owner, partner = [(jnp.arange(drawn.shape[dim]) // (drawn.shape[dim] // blocks)).reshape([-1 if axis == dim else 1 for axis in range(drawn.ndim)]) for dim in (source, target)]
    chosen = jax.random.permutation(stream_key, blocks)[partner]
    strong = (owner == chosen) | (owner == (partner + blocks // 2) % blocks)
    return jnp.where(strong, factor * drawn, drawn)


def steps_of(rng, extent, cuts, low, top_value):
    level = 1.0
    for position, parts in cuts:
        steps = jax.random.uniform(jax.random.fold_in(jax.random.fold_in(rng, 6), position), (parts,), jnp.float32, low / len(cuts), top_value / len(cuts))
        level = level * jnp.repeat(jnp.exp(steps), extent[position] // parts).reshape((-1,) + (1,) * (len(extent) - 1 - position))
    return level


def centred(rng, dims, width, reach, shards=(), held_as=jnp.bfloat16):
    values = width * jax.random.normal(rng, dims, jnp.float32)
    if shards:
        values = values * steps_of(rng, dims, shards, -0.22, 0.18)
    return jnp.clip(values, -reach, reach).astype(held_as)


def bell_draw_with(key, dims, width, most, cuts, heavy, held_as=jnp.bfloat16):
    values = width * jax.random.normal(key, dims, jnp.float32)
    if cuts:
        values = values * steps_of(key, dims, cuts, -0.22, 0.18)
    return jnp.clip(spiked(values, jax.random.fold_in(key, 3), *heavy), -most, most).astype(held_as)


def setup_inputs(seed: int = 0) -> dict:
    streams_of = jax.random.split(jax.random.key(seed), 13)
    query = draw_query(jax.random.fold_in(streams_of[12], 71), 0)
    cached_key_rows = draw_cached_key_rows(jax.random.fold_in(streams_of[12], 71), 0)
    cached_value_rows = centred(streams_of[2], (TOKENS, CACHE, HD), 1.0, 6.0, ((0, 128),))
    request_cache_length = draw_request_cache_length(jax.random.fold_in(streams_of[12], 71), 0)
    request_tenant_index = place_ends(jax.random.randint(streams_of[4], (TOKENS,), 0, TENANT_COUNT), jax.random.fold_in(streams_of[4], 1), 0, TENANT_COUNT - 1).astype(jnp.int32)
    residual = draw_residual(jax.random.fold_in(streams_of[12], 71), 0)
    feedforward_norm_gain = jnp.clip(1.0 + 0.18 * jax.random.normal(streams_of[6], (MODEL_WIDTH,), jnp.float32), 0.099609375, 1.8984375).astype(jnp.bfloat16)
    attention_output_weight = centred(streams_of[7], (C, MODEL_WIDTH), (C // 16) ** -0.5, 0.25, ((1, 16),))
    gate_up_weight = bell_draw_with(streams_of[8], (MODEL_WIDTH, 2, FEEDFWD_HIDDEN), MODEL_WIDTH ** -0.5, 0.09375, ((0, 16), (2, 8)), (0, 2, 16, 2.0))
    down_projection_weight = centred(streams_of[9], (N_FFN, N_ATTN, BLOCK_HIDDEN, MODEL_WIDTH), FEEDFWD_HIDDEN ** -0.5, 0.046875, ((0, 8), (1, 16)))
    adapter_down_maps = centred(streams_of[10], (N_FFN, N_ATTN, BLOCK_HIDDEN, TENANT_COUNT * ADAPTER_RANK), FEEDFWD_HIDDEN ** -0.5, 0.046875, ((0, 8), (1, 16)))
    adapter_up_maps = centred(streams_of[11], (TENANT_COUNT * ADAPTER_RANK, MODEL_WIDTH), ADAPTER_RANK ** -0.5, 1.5)
    return {"query": query, "cached_key_rows": cached_key_rows, "cached_value_rows": cached_value_rows, "request_cache_length": request_cache_length, "request_tenant_index": request_tenant_index, "residual": residual, "feedforward_norm_gain": feedforward_norm_gain, "attention_output_weight": attention_output_weight, "gate_up_weight": gate_up_weight, "down_projection_weight": down_projection_weight, "adapter_down_maps": adapter_down_maps, "adapter_up_maps": adapter_up_maps}


def attend_one(args):
    queries, keys, values, length = args
    heads = queries.reshape(HQ, HD)
    scores = jnp.dot(heads, keys.T, preferred_element_type=jnp.float32) * HD ** (-0.5)
    live = (jnp.arange(CACHE, dtype=jnp.int32) < length)[None, :]
    masked = jnp.where(live, scores, -jnp.inf)
    top = lax.optimization_barrier(jnp.max(masked, axis=1, keepdims=True))
    expo = jnp.where(live, jnp.exp(scores - top), jnp.float32(0.0))
    probs = (expo / lax.optimization_barrier(jnp.sum(expo, axis=1, keepdims=True))).astype(jnp.bfloat16)
    context = jnp.dot(probs, values, preferred_element_type=jnp.float32).astype(jnp.bfloat16)
    return context.reshape(HQ * HD)

def reference(query, cached_key_rows, cached_value_rows, request_cache_length, request_tenant_index, residual, feedforward_norm_gain, attention_output_weight, gate_up_weight, down_projection_weight, adapter_down_maps, adapter_up_maps):
    context = lax.map(attend_one, (query, cached_key_rows, cached_value_rows, request_cache_length))
    y_full = residual.astype(jnp.float32) + jnp.dot(context, attention_output_weight, preferred_element_type=jnp.float32)
    inverse = lax.rsqrt(lax.optimization_barrier(jnp.sum(y_full * y_full, axis=1)) / MODEL_WIDTH + 1e-06)
    normed = (y_full * feedforward_norm_gain.astype(jnp.float32)[None, :]).astype(jnp.bfloat16)
    both = jnp.dot(normed, gate_up_weight.reshape(MODEL_WIDTH, 2 * FEEDFWD_HIDDEN), preferred_element_type=jnp.float32)
    gate = both[:, :FEEDFWD_HIDDEN] * inverse[:, None]
    up_part = both[:, FEEDFWD_HIDDEN:] * inverse[:, None]
    hidden_state = (jax.nn.silu(gate) * up_part).astype(jnp.bfloat16)
    base_product = jnp.dot(hidden_state, down_projection_weight.reshape(FEEDFWD_HIDDEN, MODEL_WIDTH), preferred_element_type=jnp.float32)
    lowrank_state = jnp.dot(hidden_state, adapter_down_maps.reshape(FEEDFWD_HIDDEN, TENANT_COUNT * ADAPTER_RANK), preferred_element_type=jnp.float32)
    owners = (jnp.arange(TENANT_COUNT * ADAPTER_RANK, dtype=jnp.int32) // ADAPTER_RANK)[None, :]
    selected_adapter = jnp.where(owners == request_tenant_index[:, None], lowrank_state, jnp.float32(0.0)).astype(jnp.bfloat16)
    combined_output = base_product + jnp.dot(selected_adapter, adapter_up_maps, preferred_element_type=jnp.float32)
    return combined_output.astype(jnp.bfloat16)
```

```python
import functools

import jax
import jax.numpy as jnp
from jax import lax
from jax.experimental import pallas as pl
from jax.experimental.pallas import tpu as pltpu
from jax.sharding import PartitionSpec as P

MODEL_WIDTH = 7168
HQ = 32
HD = 256
TENANT_COUNT = 8
ADAPTER_RANK = 16
MESH = pl.DeviceIdType.MESH
BLOCK = 144
PAIR = 2 * BLOCK
HALF = 256
WIDE = MODEL_WIDTH + TENANT_COUNT * ADAPTER_RANK
FLOW = WIDE // 3
PIECE = 640
NT = (((1,), (1,)), ((), ()))
F32 = jnp.float32
BF16 = jnp.bfloat16


def attend(query, cached_key_rows, cached_value_rows, request_cache_length):
    count = query.shape[0]
    heads = query.reshape(count, HQ, HD)
    scores = jnp.einsum(
        "rhd,rld->rhl", heads, cached_key_rows, preferred_element_type=jnp.float32
    ) * HD ** (-0.5)
    slots = lax.broadcasted_iota(jnp.int32, (count, 1, cached_key_rows.shape[1]), 2)
    live = slots < request_cache_length[:, None, None]
    masked = jnp.where(live, scores, -jnp.inf)
    top = jnp.max(masked, axis=2, keepdims=True)
    expo = jnp.where(live, jnp.exp(scores - top), jnp.float32(0.0))
    probs = (expo / jnp.sum(expo, axis=2, keepdims=True)).astype(jnp.bfloat16)
    context = jnp.einsum(
        "rhl,rld->rhd", probs, cached_value_rows, preferred_element_type=jnp.float32
    )
    return context.astype(jnp.bfloat16).reshape(count, HQ * HD)


def position():
    a = lax.axis_index("attn")
    f = lax.axis_index("ffn")
    return {"y": a // 4, "z": lax.rem(a, 4), "x": f // 2, "c": lax.rem(f, 2)}


def device_at(pos, **steps):
    y = lax.rem(pos["y"] + steps.get("y", 0), 4)
    z = lax.rem(pos["z"] + steps.get("z", 0), 4)
    x = lax.rem(pos["x"] + steps.get("x", 0), 4)
    c = lax.rem(pos["c"] + steps.get("c", 0), 2)
    return (y * 4 + z, x * 2 + c)


def send(src, dst, send_sem, recv_sem, where):
    return pltpu.make_async_remote_copy(
        src_ref=src, dst_ref=dst, send_sem=send_sem, recv_sem=recv_sem,
        device_id=where, device_id_type=MESH,
    )


FLOWS = (("x", "y", "z"), ("y", "z", "x"), ("z", "x", "y"))


def feed_kernel(
    z_ref, w_ref, inv_ref, wd_ref, al_ref, up_ref, tenant_ref, out_ref,
    wt, part, got_a, got_b, summed, got_c, hid, wd, hb, ht,
    rows1, got1, rows2, got2, wide, rows3, got3, acc,
    ssem, rsem, csem, cssem, crsem, essem, ersem,
):
    pos = position()
    partners = [device_at(pos, c=1)]
    for axis in ("x", "y", "z"):
        partners += [device_at(pos, **{axis: d}) for d in (1, 2, 3)]
    barrier = pltpu.get_barrier_semaphore()
    for partner in partners:
        pl.semaphore_signal(barrier, inc=1, device_id=partner, device_id_type=MESH)
    pl.semaphore_wait(barrier, len(partners))

    peer = device_at(pos, c=1)
    w_out = send(wd_ref, wd.at[BLOCK:, :MODEL_WIDTH], cssem.at[0], crsem.at[0], peer)
    a_out = send(al_ref, wd.at[BLOCK:, MODEL_WIDTH:], cssem.at[1], crsem.at[1], peer)
    w_own = pltpu.make_async_copy(wd_ref, wd.at[:BLOCK, :MODEL_WIDTH], csem.at[0])
    a_own = pltpu.make_async_copy(al_ref, wd.at[:BLOCK, MODEL_WIDTH:], csem.at[1])
    for copy in (w_out, a_out, w_own, a_own):
        copy.start()

    for s in range(2):
        for tile in range(18):
            turned = w_ref[s, :, tile * 128:(tile + 1) * 128].T
            at = 0
            while at < 128:
                n = tile * 128 + at
                block, k = n // BLOCK, n % BLOCK
                count = min(128 - at, BLOCK - k)
                row = block * PAIR + s * BLOCK + k
                wt[row:row + count, :] = turned[at:at + count, :]
                at += count

    first = ("y", "z")
    me1 = [pos["y"], pos["z"]]
    me2 = [pos["z"], pos["y"]]

    def compute(h, p, lo, hi):
        def body(q, carry):
            a = p * 4 + q if h == 0 else q * 4 + p
            lhs = wt[pl.ds(pl.multiple_of(a * PAIR, PAIR), PAIR), :]
            r = lax.dot_general(
                lhs, z_ref[h * HALF:(h + 1) * HALF, :], NT, preferred_element_type=F32
            )
            part[h, p, q] = r.astype(BF16)
            return carry

        lax.fori_loop(lo, hi, body, 0)

    step = [[lax.rem(me1[h] + d, 4) for d in range(4)] for h in range(2)]
    one = [[None, None], [None, None]]
    two = [[None, None], [None, None]]
    three = [[None] * 3, [None] * 3]
    for h in range(2):
        for side in range(2):
            compute(h, step[h][2], 2 * side, 2 * side + 2)
            one[h][side] = send(
                part.at[h, step[h][2], 2 * side:2 * side + 2], got_a.at[h, side],
                ssem.at[h, side], rsem.at[h, side],
                device_at(pos, **{first[h]: 1 if side == 0 else 3}),
            )
            one[h][side].start()
    for h in range(2):
        compute(h, step[h][1], 0, 4)
        compute(h, step[h][3], 0, 4)
    for h in range(2):
        for side in range(2):
            to = 1 if side == 0 else 3
            p = step[h][to]
            one[h][side].wait_recv()

            def join(i, carry, h=h, side=side, p=p):
                q = 2 * side + i
                part[h, p, q] = (
                    part[h, p, q].astype(F32) + got_a[h, side, i].astype(F32)
                ).astype(BF16)
                return carry

            lax.fori_loop(0, 2, join, 0)
            two[h][side] = send(
                part.at[h, p], got_b.at[h, side], ssem.at[h, 2 + side], rsem.at[h, 2 + side],
                device_at(pos, **{first[h]: to}),
            )
            two[h][side].start()
    for h in range(2):
        compute(h, step[h][0], 0, 4)
    for h in range(2):
        for side in range(2):
            two[h][side].wait_recv()
        p = step[h][0]

        def total(q, h=h, p=p):
            return (
                part[h, p, q].astype(F32) + got_b[h, 0, q].astype(F32)
                + got_b[h, 1, q].astype(F32)
            )

        for d in (2, 1, 3):
            q = lax.rem(me2[h] + d, 4)
            summed[h, d - 1] = total(q).astype(BF16)
            three[h][d - 1] = send(
                summed.at[h, d - 1], got_c.at[h, d - 1], ssem.at[h, 3 + d], rsem.at[h, 3 + d],
                device_at(pos, **{first[1 - h]: d}),
            )
            three[h][d - 1].start()
    for h in range(2):
        for d in range(3):
            three[h][d].wait_recv()
        p, q = step[h][0], me2[h]
        both = (
            part[h, p, q].astype(F32) + got_b[h, 0, q].astype(F32) + got_b[h, 1, q].astype(F32)
            + got_c[h, 0].astype(F32) + got_c[h, 1].astype(F32) + got_c[h, 2].astype(F32)
        ) * inv_ref[:, h * HALF:(h + 1) * HALF]
        gate, up = both[:BLOCK], both[BLOCK:]
        hid[h] = (gate / (1.0 + jnp.exp(-gate)) * up).astype(BF16)

    c = pos["c"]
    h_out = send(hid.at[1 - c], hb.at[BLOCK:], cssem.at[2], crsem.at[2], peer)
    h_out.start()
    hb[:BLOCK, :] = hid[c]
    for copy in (w_out, a_out, h_out):
        copy.wait_recv()
    w_own.wait()
    a_own.wait()

    row = lax.broadcasted_iota(jnp.int32, (HALF, HALF), 0)
    col = lax.broadcasted_iota(jnp.int32, (HALF, HALF), 1)
    place = {"x": 64, "y": 16, "z": 4}
    for k, axes in enumerate(FLOWS):
        source = lax.rem(row, 4)
        for n, axis in enumerate(axes):
            source = source + lax.rem(row // (64, 16, 4)[n], 4) * place[axis]
        turn = (source == col).astype(BF16)
        ht[k] = lax.dot_general(turn, hb[...], NT, preferred_element_type=F32).astype(BF16)

    out1 = [[None] * 3 for _ in FLOWS]
    out2 = [[None] * 3 for _ in FLOWS]
    out3 = [[None] * 3 for _ in FLOWS]
    for k, axes in enumerate(FLOWS):
        def tile_of(start, width, k=k):
            r = jnp.dot(
                ht[k], wd[:, pl.ds(k * FLOW + start, width)], preferred_element_type=F32
            )
            rows1[k, :, pl.ds(start, width)] = r.astype(BF16)

        def body(i, carry, tile_of=tile_of):
            tile_of(pl.multiple_of(i * 256, 256), 256)
            return carry

        lax.fori_loop(0, 9, body, 0)
        tile_of(2304, 128)
        for d in (2, 1, 3):
            b = lax.rem(pos[axes[0]] + d, 4)
            out1[k][d - 1] = send(
                rows1.at[k, pl.ds(pl.multiple_of(b * 64, 64), 64)], got1.at[k, d - 1],
                essem.at[k, d - 1], ersem.at[k, d - 1], device_at(pos, **{axes[0]: d}),
            )
            out1[k][d - 1].start()
    for k, axes in enumerate(FLOWS):
        for d in range(3):
            out1[k][d].wait_recv()
        mine = pos[axes[0]] * 64

        def add1(i, carry, k=k, mine=mine):
            at = pl.multiple_of(i * 16, 16)
            r = rows1[k, pl.ds(pl.multiple_of(mine + at, 16), 16), :].astype(F32)
            for d in range(3):
                r = r + got1[k, d, pl.ds(at, 16), :].astype(F32)
            rows2[k, i] = r.astype(BF16)
            return carry

        lax.fori_loop(0, 4, add1, 0)
        for d in (2, 1, 3):
            b = lax.rem(pos[axes[1]] + d, 4)
            out2[k][d - 1] = send(
                rows2.at[k, b], got2.at[k, d - 1],
                essem.at[k, 2 + d], ersem.at[k, 2 + d], device_at(pos, **{axes[1]: d}),
            )
            out2[k][d - 1].start()
    wide[:, FLOW:] = jnp.zeros((16, 4 * PIECE - FLOW), F32)
    for k, axes in enumerate(FLOWS):
        for d in range(3):
            out2[k][d].wait_recv()
        r = rows2[k, pos[axes[1]]].astype(F32)
        for d in range(3):
            r = r + got2[k, d].astype(F32)
        wide[:, :FLOW] = r
        for to in range(4):
            rows3[k, to] = jnp.concatenate(
                [wide[4 * to:4 * to + 4, n * PIECE:(n + 1) * PIECE] for n in range(4)], axis=0
            ).astype(BF16)
        for d in (2, 1, 3):
            b = lax.rem(pos[axes[2]] + d, 4)
            out3[k][d - 1] = send(
                rows3.at[k, b], got3.at[k, d - 1],
                essem.at[k, 5 + d], ersem.at[k, 5 + d], device_at(pos, **{axes[2]: d}),
            )
            out3[k][d - 1].start()
    acc[...] = jnp.zeros(acc.shape, F32)
    for k, axes in enumerate(FLOWS):
        for d in range(3):
            out3[k][d].wait_recv()
        r = rows3[k, pos[axes[2]]].astype(F32)
        for d in range(3):
            r = r + got3[k, d].astype(F32)
        for n in range(4):
            width = min(PIECE, FLOW - n * PIECE)
            start = k * FLOW + n * PIECE
            acc[0:4, start:start + width] = r[4 * n:4 * n + 4, :width]

    low = acc[:, MODEL_WIDTH:]
    who = lax.broadcasted_iota(jnp.int32, low.shape, 0)
    owner = lax.broadcasted_iota(jnp.int32, low.shape, 1) // ADAPTER_RANK
    tenant = jnp.where(
        who == 0, tenant_ref[0],
        jnp.where(who == 1, tenant_ref[1], jnp.where(who == 2, tenant_ref[2], tenant_ref[3])),
    )
    picked = jnp.where(owner == tenant, low, 0.0).astype(BF16)
    for n in range(7):
        cols = slice(n * 1024, (n + 1) * 1024)
        r = acc[:, cols] + jnp.dot(picked, up_ref[:, cols], preferred_element_type=F32)
        out_ref[:, cols] = r[0:4].astype(BF16)

    for copy in (w_out, a_out, h_out):
        copy.wait_send()
    for group in (one, two, three, out1, out2, out3):
        for copies in group:
            for copy in copies:
                copy.wait_send()


def feed(z, w, inv, wd, al, up, tenant):
    vmem = pl.BlockSpec(memory_space=pltpu.VMEM)
    hbm = pl.BlockSpec(memory_space=pl.ANY)
    smem = pl.BlockSpec(memory_space=pltpu.SMEM)
    dma = pltpu.SemaphoreType.DMA
    return pl.pallas_call(
        feed_kernel,
        out_shape=jax.ShapeDtypeStruct((4, MODEL_WIDTH), BF16),
        in_specs=[vmem, vmem, vmem, hbm, hbm, vmem, smem],
        out_specs=vmem,
        scratch_shapes=[
            pltpu.VMEM((16 * PAIR, 448), BF16),
            pltpu.VMEM((2, 4, 4, PAIR, HALF), BF16),
            pltpu.VMEM((2, 2, 2, PAIR, HALF), BF16),
            pltpu.VMEM((2, 2, 4, PAIR, HALF), BF16),
            pltpu.VMEM((2, 3, PAIR, HALF), BF16),
            pltpu.VMEM((2, 3, PAIR, HALF), BF16),
            pltpu.VMEM((2, BLOCK, HALF), BF16),
            pltpu.VMEM((PAIR, WIDE), BF16),
            pltpu.VMEM((PAIR, HALF), BF16),
            pltpu.VMEM((3, HALF, PAIR), BF16),
            pltpu.VMEM((3, HALF, FLOW), BF16),
            pltpu.VMEM((3, 3, 64, FLOW), BF16),
            pltpu.VMEM((3, 4, 16, FLOW), BF16),
            pltpu.VMEM((3, 3, 16, FLOW), BF16),
            pltpu.VMEM((16, 4 * PIECE), F32),
            pltpu.VMEM((3, 4, 16, PIECE), BF16),
            pltpu.VMEM((3, 3, 16, PIECE), BF16),
            pltpu.VMEM((8, WIDE), F32),
            dma((2, 7)), dma((2, 7)), dma((2,)), dma((3,)), dma((3,)),
            dma((3, 9)), dma((3, 9)),
        ],
        compiler_params=pltpu.CompilerParams(
            collective_id=1, has_side_effects=True, vmem_limit_bytes=56 << 20
        ),
    )(z, w, inv, wd, al, up, tenant)


def local(
    query,
    cached_key_rows,
    cached_value_rows,
    request_cache_length,
    request_tenant_index,
    residual,
    feedforward_norm_gain,
    attention_output_weight,
    gate_up_weight,
    down_projection_weight,
    adapter_down_maps,
    adapter_up_maps,
):
    context = attend(query, cached_key_rows, cached_value_rows, request_cache_length)
    gathered = lax.all_gather(context, "attn", axis=0, tiled=True)
    projected = jnp.dot(gathered, attention_output_weight, preferred_element_type=F32)
    f = lax.axis_index("ffn")
    mine = lax.dynamic_index_in_dim(
        residual.reshape(16, 8, 4, 448), f, axis=1, keepdims=False
    ).reshape(64, 448)
    stream = mine.astype(F32) + projected
    squares = lax.psum(jnp.sum(stream * stream, axis=1), "attn")
    inverse = lax.rsqrt(squares / MODEL_WIDTH + 1e-06)
    normed = (stream * feedforward_norm_gain.astype(F32)[None, :]).astype(BF16)
    z = lax.all_gather(normed, "ffn", axis=0)
    z = z.reshape(4, 2, 64, 448).transpose(1, 0, 2, 3).reshape(512, 448)
    inv = lax.all_gather(inverse, "ffn", axis=0)
    inv = inv.reshape(4, 2, 64).transpose(1, 0, 2).reshape(1, 512)
    w = jnp.transpose(gate_up_weight, (1, 0, 2))
    return feed(
        z, w, inv, down_projection_weight.reshape(BLOCK, MODEL_WIDTH),
        adapter_down_maps.reshape(BLOCK, TENANT_COUNT * ADAPTER_RANK),
        adapter_up_maps, request_tenant_index,
    )


def solution(mesh):
    in_specs = (
        P(("attn", "ffn"), None),
        P(("attn", "ffn"), None, None),
        P(("attn", "ffn"), None, None),
        P(("attn", "ffn")),
        P(("attn", "ffn")),
        P(None, "attn"),
        P("attn"),
        P(None, "attn"),
        P("attn", None, "ffn"),
        P("ffn", "attn", None, None),
        P("ffn", "attn", None, None),
        P(),
    )
    out_specs = P(("attn", "ffn"), None)
    return jax.shard_map(local, mesh=mesh, in_specs=in_specs, out_specs=out_specs, check_vma=False)
```

```python
import jax
import jax.numpy as jnp
from jax import lax
from jax.experimental import pallas as pl
from jax.experimental.pallas import tpu as pltpu
from jax.sharding import PartitionSpec as P

MODEL_WIDTH = 7168
HQ = 32
HD = 256
TENANT_COUNT = 8
ADAPTER_RANK = 16
MESH = pl.DeviceIdType.MESH
BLOCK = 144
PAIR = 2 * BLOCK
HALF = 256
WIDE = MODEL_WIDTH + TENANT_COUNT * ADAPTER_RANK
FLOW = WIDE // 3
PIECE = 640
NT = (((1,), (1,)), ((), ()))
F32 = jnp.float32
BF16 = jnp.bfloat16


def attend(query, cached_key_rows, cached_value_rows, request_cache_length):
    count = query.shape[0]
    heads = query.reshape(count, HQ, HD)
    scores = jnp.einsum(
        "rhd,rld->rhl", heads, cached_key_rows, preferred_element_type=jnp.float32
    ) * HD ** (-0.5)
    slots = lax.broadcasted_iota(jnp.int32, (count, 1, cached_key_rows.shape[1]), 2)
    live = slots < request_cache_length[:, None, None]
    masked = jnp.where(live, scores, -jnp.inf)
    top = jnp.max(masked, axis=2, keepdims=True)
    expo = jnp.where(live, jnp.exp(scores - top), jnp.float32(0.0))
    probs = (expo / jnp.sum(expo, axis=2, keepdims=True)).astype(jnp.bfloat16)
    context = jnp.einsum(
        "rhl,rld->rhd", probs, cached_value_rows, preferred_element_type=jnp.float32
    )
    return context.astype(jnp.bfloat16).reshape(count, HQ * HD)


def position():
    a = lax.axis_index("attn")
    f = lax.axis_index("ffn")
    return {"y": a // 4, "z": lax.rem(a, 4), "x": f // 2, "c": lax.rem(f, 2)}


def device_at(pos, **steps):
    y = lax.rem(pos["y"] + steps.get("y", 0), 4)
    z = lax.rem(pos["z"] + steps.get("z", 0), 4)
    x = lax.rem(pos["x"] + steps.get("x", 0), 4)
    c = lax.rem(pos["c"] + steps.get("c", 0), 2)
    return (y * 4 + z, x * 2 + c)


def send(src, dst, send_sem, recv_sem, where):
    return pltpu.make_async_remote_copy(
        src_ref=src, dst_ref=dst, send_sem=send_sem, recv_sem=recv_sem,
        device_id=where, device_id_type=MESH,
    )


FLOWS = (("x", "y", "z"), ("y", "z", "x"), ("z", "x", "y"))


def feed_kernel(
    ctx_ref, wo_ref, res_ref, gain_ref, w_ref, wd_ref, al_ref, up_ref, tenant_ref, out_ref,
    ctx_all, wo, res, z, sq, iv, wraw, up,
    wt, part, got_a, got_b, summed, got_c, hid, wd, hb, ht,
    rows1, got1, rows2, got2, wide, rows3, got3, acc,
    lsem, asem, arsem, qsem, qrsem, zsem, zrsem, isem, irsem,
    ssem, rsem, cssem, crsem, essem, ersem,
):
    pos = position()
    c = pos["c"]
    y_me, z_me, x_me = pos["y"], pos["z"], pos["x"]
    peer = device_at(pos, c=1)
    plane = [(dy, dz) for dy in range(4) for dz in range(4) if dy or dz]
    line = [(dx, dc) for dx in range(4) for dc in range(2) if dx or dc]
    partners = [device_at(pos, y=dy, z=dz) for dy, dz in plane]
    partners += [device_at(pos, x=dx, c=dc) for dx, dc in line]
    barrier = pltpu.get_barrier_semaphore()
    for partner in partners:
        pl.semaphore_signal(barrier, inc=1, device_id=partner, device_id_type=MESH)

    loads = [
        pltpu.make_async_copy(w_ref, wraw, lsem.at[0]),
        pltpu.make_async_copy(wo_ref, wo, lsem.at[1]),
        pltpu.make_async_copy(res_ref, res, lsem.at[2]),
        pltpu.make_async_copy(wd_ref, wd.at[:BLOCK, :MODEL_WIDTH], lsem.at[3]),
        pltpu.make_async_copy(al_ref, wd.at[:BLOCK, MODEL_WIDTH:], lsem.at[4]),
        pltpu.make_async_copy(up_ref, up, lsem.at[5]),
    ]
    for copy in loads:
        copy.start()
    load_w, load_wo, load_res, load_wd, load_al, load_up = loads
    ctx_all[y_me, z_me] = ctx_ref[...]
    pl.semaphore_wait(barrier, len(partners))

    near, far = [], []
    for d in (2, 1, 3):
        for h, axis in enumerate(("y", "z")):
            view = ctx_all.at[y_me, z_me, :, h * 1024:(h + 1) * 1024]
            copy = send(
                view, view, asem.at[h, d - 1], arsem.at[h, d - 1], device_at(pos, **{axis: d})
            )
            copy.start()
            near.append(copy)

    w_out = send(wd_ref, wd.at[BLOCK:, :MODEL_WIDTH], cssem.at[0], crsem.at[0], peer)
    a_out = send(al_ref, wd.at[BLOCK:, MODEL_WIDTH:], cssem.at[1], crsem.at[1], peer)
    w_out.start()
    a_out.start()

    def turn_tiles(lo, hi):
        for tile in range(lo, hi):
            for s in range(2):
                turned = wraw[s, :, tile * 128:(tile + 1) * 128].T
                at = 0
                while at < 128:
                    n = tile * 128 + at
                    block, k = n // BLOCK, n % BLOCK
                    count = min(128 - at, BLOCK - k)
                    row = block * PAIR + s * BLOCK + k
                    wt[row:row + count, :] = turned[at:at + count, :]
                    at += count

    load_w.wait()
    turn_tiles(0, 4)
    for copy in near:
        copy.wait_recv()
    for d in (2, 1, 3):
        for h, axis in enumerate(("z", "y")):
            if h == 0:
                view = ctx_all.at[:, z_me, :, :1024]
            else:
                view = ctx_all.at[y_me, :, :, 1024:]
            copy = send(
                view, view, asem.at[h, 2 + d], arsem.at[h, 2 + d], device_at(pos, **{axis: d})
            )
            copy.start()
            far.append(copy)
    turn_tiles(4, 18)
    load_res.wait()
    load_wo.wait()

    row = lax.broadcasted_iota(jnp.int32, (128, 512), 0)
    col = lax.broadcasted_iota(jnp.int32, (128, 512), 1)
    f = x_me * 2 + c
    chosen = (col == (row // 8) * 32 + f * 4 + lax.rem(row, 4)).astype(BF16)
    stream = lax.dot_general(chosen, res[...], NT, preferred_element_type=F32)

    for copy in far:
        copy.wait_recv()
    quarter = lax.rem(lax.broadcasted_iota(jnp.int32, (HALF, 448), 0), 16) // 4
    projected = jnp.zeros((HALF, 448), F32)
    for q in range(4):
        r = lax.dot_general(
            ctx_all[...].reshape(HALF, 2048), wo[:, q * 2048:(q + 1) * 2048], NT,
            preferred_element_type=F32,
        )
        projected = jnp.where(quarter == q, r, projected)
    projected = projected.reshape(16, 16, 448)
    projected = projected[:, :8] + projected[:, 8:]
    projected = (projected + pltpu.roll(projected, 4, 1)).reshape(128, 448)
    stream = stream + projected
    normed = (stream * gain_ref[...].astype(F32)).astype(BF16)
    row = lax.broadcasted_iota(jnp.int32, (64, 128), 0)
    col = lax.broadcasted_iota(jnp.int32, (64, 128), 1)
    pick = (col == (row // 4) * 8 + lax.rem(row, 4)).astype(BF16)
    z[c, x_me] = jnp.dot(pick, normed, preferred_element_type=F32).astype(BF16)
    along, across = [], []
    for d in (2, 1, 3):
        view = z.at[c, x_me]
        copy = send(view, view, zsem.at[d - 1], zrsem.at[d - 1], device_at(pos, x=d))
        copy.start()
        along.append((d, copy))
    for d in (0, 1, 3, 2):
        if d:
            dict(along)[d].wait_recv()
        view = z.at[c, lax.rem(x_me + 4 - d, 4)]
        copy = send(view, view, zsem.at[3 + d], zrsem.at[3 + d], peer)
        copy.start()
        across.append(copy)

    squares = jnp.sum(stream * stream, axis=1, keepdims=True)
    row = lax.broadcasted_iota(jnp.int32, (128, 128), 0)
    col = lax.rem(lax.broadcasted_iota(jnp.int32, (128, 128), 1), 64)
    spread = jnp.where(row == (col // 4) * 8 + lax.rem(col, 4), squares, 0.0)
    sq[y_me, z_me] = jnp.broadcast_to(jnp.sum(spread, axis=0, keepdims=True), (8, 128))
    sums = []
    for n, (dy, dz) in enumerate(plane):
        view = sq.at[y_me, z_me]
        copy = send(view, view, qsem.at[n], qrsem.at[n], device_at(pos, y=dy, z=dz))
        copy.start()
        sums.append(copy)
    for copy in across:
        copy.wait_recv()

    first = ("y", "z")
    me1 = [pos["y"], pos["z"]]
    me2 = [pos["z"], pos["y"]]

    def compute(h, p, lo, hi):
        def body(q, carry):
            a = p * 4 + q if h == 0 else q * 4 + p
            lhs = wt[pl.ds(pl.multiple_of(a * PAIR, PAIR), PAIR), :]
            r = lax.dot_general(
                lhs, z[h].reshape(HALF, 448), NT, preferred_element_type=F32
            )
            part[h, p, q] = r.astype(BF16)
            return carry

        lax.fori_loop(lo, hi, body, 0)

    step = [[lax.rem(me1[h] + d, 4) for d in range(4)] for h in range(2)]
    one = [[None, None], [None, None]]
    two = [[None, None], [None, None]]
    three = [[None] * 3, [None] * 3]
    for h in range(2):
        for side in range(2):
            compute(h, step[h][2], 2 * side, 2 * side + 2)
            one[h][side] = send(
                part.at[h, step[h][2], 2 * side:2 * side + 2], got_a.at[h, side],
                ssem.at[h, side], rsem.at[h, side],
                device_at(pos, **{first[h]: 1 if side == 0 else 3}),
            )
            one[h][side].start()
    for h in range(2):
        compute(h, step[h][1], 0, 4)
        compute(h, step[h][3], 0, 4)
    for copy in sums:
        copy.wait_recv()
    squares = jnp.sum(sq[...].reshape(16, 8, 128), axis=0)
    iv[c, x_me] = lax.rsqrt(squares / MODEL_WIDTH + 1e-06)
    scales = []
    for n, (dx, dc) in enumerate(line):
        view = iv.at[c, x_me]
        copy = send(view, view, isem.at[n], irsem.at[n], device_at(pos, x=dx, c=dc))
        copy.start()
        scales.append(copy)
    for h in range(2):
        for side in range(2):
            to = 1 if side == 0 else 3
            p = step[h][to]
            one[h][side].wait_recv()

            def join(i, carry, h=h, side=side, p=p):
                q = 2 * side + i
                part[h, p, q] = (
                    part[h, p, q].astype(F32) + got_a[h, side, i].astype(F32)
                ).astype(BF16)
                return carry

            lax.fori_loop(0, 2, join, 0)
            two[h][side] = send(
                part.at[h, p], got_b.at[h, side], ssem.at[h, 2 + side], rsem.at[h, 2 + side],
                device_at(pos, **{first[h]: to}),
            )
            two[h][side].start()
    for h in range(2):
        compute(h, step[h][0], 0, 4)
    for h in range(2):
        for side in range(2):
            two[h][side].wait_recv()
        p = step[h][0]

        def total(q, h=h, p=p):
            return (
                part[h, p, q].astype(F32) + got_b[h, 0, q].astype(F32)
                + got_b[h, 1, q].astype(F32)
            )

        for d in (2, 1, 3):
            q = lax.rem(me2[h] + d, 4)
            summed[h, d - 1] = total(q).astype(BF16)
            three[h][d - 1] = send(
                summed.at[h, d - 1], got_c.at[h, d - 1], ssem.at[h, 3 + d], rsem.at[h, 3 + d],
                device_at(pos, **{first[1 - h]: d}),
            )
            three[h][d - 1].start()
    for copy in scales:
        copy.wait_recv()
    left = lax.broadcasted_iota(jnp.int32, (1, 128), 1) < 64
    for h in range(2):
        inverse = jnp.concatenate(
            [jnp.where(left, iv[h, 2 * n, :1], iv[h, 2 * n + 1, :1]) for n in range(2)], axis=1
        )
        for d in range(3):
            three[h][d].wait_recv()
        p, q = step[h][0], me2[h]
        both = (
            part[h, p, q].astype(F32) + got_b[h, 0, q].astype(F32) + got_b[h, 1, q].astype(F32)
            + got_c[h, 0].astype(F32) + got_c[h, 1].astype(F32) + got_c[h, 2].astype(F32)
        ) * inverse
        gate, lift = both[:BLOCK], both[BLOCK:]
        hid[h] = (gate / (1.0 + jnp.exp(-gate)) * lift).astype(BF16)

    h_out = send(hid.at[1 - c], hb.at[BLOCK:], cssem.at[2], crsem.at[2], peer)
    h_out.start()
    hb[:BLOCK, :] = hid[c]
    for copy in (w_out, a_out, h_out):
        copy.wait_recv()
    load_wd.wait()
    load_al.wait()

    row = lax.broadcasted_iota(jnp.int32, (HALF, HALF), 0)
    col = lax.broadcasted_iota(jnp.int32, (HALF, HALF), 1)
    place = {"x": 64, "y": 16, "z": 4}
    for k, axes in enumerate(FLOWS):
        source = lax.rem(row, 4)
        for n, axis in enumerate(axes):
            source = source + lax.rem(row // (64, 16, 4)[n], 4) * place[axis]
        turn = (source == col).astype(BF16)
        ht[k] = lax.dot_general(turn, hb[...], NT, preferred_element_type=F32).astype(BF16)

    out1 = [[None] * 3 for _ in FLOWS]
    out2 = [[None] * 3 for _ in FLOWS]
    out3 = [[None] * 3 for _ in FLOWS]
    for k, axes in enumerate(FLOWS):
        def tile_of(start, width, k=k):
            r = jnp.dot(
                ht[k], wd[:, pl.ds(k * FLOW + start, width)], preferred_element_type=F32
            )
            rows1[k, :, pl.ds(start, width)] = r.astype(BF16)

        def body(i, carry, tile_of=tile_of):
            tile_of(pl.multiple_of(i * 256, 256), 256)
            return carry

        lax.fori_loop(0, 9, body, 0)
        tile_of(2304, 128)
        for d in (2, 1, 3):
            b = lax.rem(pos[axes[0]] + d, 4)
            out1[k][d - 1] = send(
                rows1.at[k, pl.ds(pl.multiple_of(b * 64, 64), 64)], got1.at[k, d - 1],
                essem.at[k, d - 1], ersem.at[k, d - 1], device_at(pos, **{axes[0]: d}),
            )
            out1[k][d - 1].start()
    for k, axes in enumerate(FLOWS):
        for d in range(3):
            out1[k][d].wait_recv()
        mine = pos[axes[0]] * 64

        def add1(i, carry, k=k, mine=mine):
            at = pl.multiple_of(i * 16, 16)
            r = rows1[k, pl.ds(pl.multiple_of(mine + at, 16), 16), :].astype(F32)
            for d in range(3):
                r = r + got1[k, d, pl.ds(at, 16), :].astype(F32)
            rows2[k, i] = r.astype(BF16)
            return carry

        lax.fori_loop(0, 4, add1, 0)
        for d in (2, 1, 3):
            b = lax.rem(pos[axes[1]] + d, 4)
            out2[k][d - 1] = send(
                rows2.at[k, b], got2.at[k, d - 1],
                essem.at[k, 2 + d], ersem.at[k, 2 + d], device_at(pos, **{axes[1]: d}),
            )
            out2[k][d - 1].start()
    wide[:, FLOW:] = jnp.zeros((16, 4 * PIECE - FLOW), F32)
    for k, axes in enumerate(FLOWS):
        for d in range(3):
            out2[k][d].wait_recv()
        r = rows2[k, pos[axes[1]]].astype(F32)
        for d in range(3):
            r = r + got2[k, d].astype(F32)
        wide[:, :FLOW] = r
        for to in range(4):
            rows3[k, to] = jnp.concatenate(
                [wide[4 * to:4 * to + 4, n * PIECE:(n + 1) * PIECE] for n in range(4)], axis=0
            ).astype(BF16)
        for d in (2, 1, 3):
            b = lax.rem(pos[axes[2]] + d, 4)
            out3[k][d - 1] = send(
                rows3.at[k, b], got3.at[k, d - 1],
                essem.at[k, 5 + d], ersem.at[k, 5 + d], device_at(pos, **{axes[2]: d}),
            )
            out3[k][d - 1].start()
    acc[...] = jnp.zeros(acc.shape, F32)
    for k, axes in enumerate(FLOWS):
        for d in range(3):
            out3[k][d].wait_recv()
        r = rows3[k, pos[axes[2]]].astype(F32)
        for d in range(3):
            r = r + got3[k, d].astype(F32)
        for n in range(4):
            width = min(PIECE, FLOW - n * PIECE)
            start = k * FLOW + n * PIECE
            acc[0:4, start:start + width] = r[4 * n:4 * n + 4, :width]

    low = acc[:, MODEL_WIDTH:]
    who = lax.broadcasted_iota(jnp.int32, low.shape, 0)
    owner = lax.broadcasted_iota(jnp.int32, low.shape, 1) // ADAPTER_RANK
    tenant = jnp.where(
        who == 0, tenant_ref[0],
        jnp.where(who == 1, tenant_ref[1], jnp.where(who == 2, tenant_ref[2], tenant_ref[3])),
    )
    load_up.wait()
    picked = jnp.where(owner == tenant, low, 0.0).astype(BF16)
    for n in range(7):
        cols = slice(n * 1024, (n + 1) * 1024)
        r = acc[:, cols] + jnp.dot(picked, up[:, cols], preferred_element_type=F32)
        out_ref[:, cols] = r[0:4].astype(BF16)

    along = [copy for _, copy in along]
    for copies in ((w_out, a_out, h_out), near, far, along, across, sums, scales):
        for copy in copies:
            copy.wait_send()
    for group in (one, two, three, out1, out2, out3):
        for copies in group:
            for copy in copies:
                copy.wait_send()


def feed(ctx, wo, res, gain, w, wd, al, up, tenant):
    vmem = pl.BlockSpec(memory_space=pltpu.VMEM)
    hbm = pl.BlockSpec(memory_space=pl.ANY)
    smem = pl.BlockSpec(memory_space=pltpu.SMEM)
    dma = pltpu.SemaphoreType.DMA
    return pl.pallas_call(
        feed_kernel,
        out_shape=jax.ShapeDtypeStruct((4, MODEL_WIDTH), BF16),
        in_specs=[vmem, hbm, hbm, vmem, hbm, hbm, hbm, hbm, smem],
        out_specs=vmem,
        scratch_shapes=[
            pltpu.VMEM((4, 4, 16, 2048), BF16),
            pltpu.VMEM((448, 8192), BF16),
            pltpu.VMEM((448, 512), BF16),
            pltpu.VMEM((2, 4, 64, 448), BF16),
            pltpu.VMEM((4, 4, 8, 128), F32),
            pltpu.VMEM((2, 4, 8, 128), F32),
            pltpu.VMEM((2, 448, 2304), BF16),
            pltpu.VMEM((128, MODEL_WIDTH), BF16),
            pltpu.VMEM((16 * PAIR, 448), BF16),
            pltpu.VMEM((2, 4, 4, PAIR, HALF), BF16),
            pltpu.VMEM((2, 2, 2, PAIR, HALF), BF16),
            pltpu.VMEM((2, 2, 4, PAIR, HALF), BF16),
            pltpu.VMEM((2, 3, PAIR, HALF), BF16),
            pltpu.VMEM((2, 3, PAIR, HALF), BF16),
            pltpu.VMEM((2, BLOCK, HALF), BF16),
            pltpu.VMEM((PAIR, WIDE), BF16),
            pltpu.VMEM((PAIR, HALF), BF16),
            pltpu.VMEM((3, HALF, PAIR), BF16),
            pltpu.VMEM((3, HALF, FLOW), BF16),
            pltpu.VMEM((3, 3, 64, FLOW), BF16),
            pltpu.VMEM((3, 4, 16, FLOW), BF16),
            pltpu.VMEM((3, 3, 16, FLOW), BF16),
            pltpu.VMEM((16, 4 * PIECE), F32),
            pltpu.VMEM((3, 4, 16, PIECE), BF16),
            pltpu.VMEM((3, 3, 16, PIECE), BF16),
            pltpu.VMEM((8, WIDE), F32),
            dma((6,)), dma((2, 6)), dma((2, 6)), dma((15,)), dma((15,)),
            dma((7,)), dma((7,)), dma((7,)), dma((7,)),
            dma((2, 7)), dma((2, 7)), dma((3,)), dma((3,)),
            dma((3, 9)), dma((3, 9)),
        ],
        compiler_params=pltpu.CompilerParams(
            collective_id=1, has_side_effects=True, vmem_limit_bytes=58 << 20
        ),
    )(ctx, wo, res, gain, w, wd, al, up, tenant)


def local(
    query,
    cached_key_rows,
    cached_value_rows,
    request_cache_length,
    request_tenant_index,
    residual,
    feedforward_norm_gain,
    attention_output_weight,
    gate_up_weight,
    down_projection_weight,
    adapter_down_maps,
    adapter_up_maps,
):
    context = attend(query, cached_key_rows, cached_value_rows, request_cache_length)
    context = context.reshape(4, 4, 2048).transpose(1, 0, 2).reshape(16, 2048)
    return feed(
        context, attention_output_weight.T, residual.T, feedforward_norm_gain.reshape(1, -1),
        jnp.transpose(gate_up_weight, (1, 0, 2)),
        down_projection_weight.reshape(BLOCK, MODEL_WIDTH),
        adapter_down_maps.reshape(BLOCK, TENANT_COUNT * ADAPTER_RANK),
        adapter_up_maps, request_tenant_index,
    )


def solution(mesh):
    in_specs = (
        P(("attn", "ffn"), None),
        P(("attn", "ffn"), None, None),
        P(("attn", "ffn"), None, None),
        P(("attn", "ffn")),
        P(("attn", "ffn")),
        P(None, "attn"),
        P("attn"),
        P(None, "attn"),
        P("attn", None, "ffn"),
        P("ffn", "attn", None, None),
        P("ffn", "attn", None, None),
        P(),
    )
    out_specs = P(("attn", "ffn"), None)
    return jax.shard_map(local, mesh=mesh, in_specs=in_specs, out_specs=out_specs, check_vma=False)
```

```python
import functools

import jax
import jax.numpy as jnp
from jax import lax
from jax.experimental import pallas as pl
from jax.experimental.pallas import tpu as pltpu
from jax.sharding import PartitionSpec as P

MODEL_WIDTH = 7168
HQ = 32
HD = 256
CACHE = 2048
TENANT_COUNT = 8
ADAPTER_RANK = 16
MESH = pl.DeviceIdType.MESH
BLOCK = 144
PAIR = 2 * BLOCK
HALF = 256
WIDE = MODEL_WIDTH + TENANT_COUNT * ADAPTER_RANK
FLOW = WIDE // 3
PIECE = 640
NT = (((1,), (1,)), ((), ()))
F32 = jnp.float32
BF16 = jnp.bfloat16


def position():
    a = lax.axis_index("attn")
    f = lax.axis_index("ffn")
    return {"y": a // 4, "z": lax.rem(a, 4), "x": f // 2, "c": lax.rem(f, 2)}


def device_at(pos, **steps):
    y = lax.rem(pos["y"] + steps.get("y", 0), 4)
    z = lax.rem(pos["z"] + steps.get("z", 0), 4)
    x = lax.rem(pos["x"] + steps.get("x", 0), 4)
    c = lax.rem(pos["c"] + steps.get("c", 0), 2)
    return (y * 4 + z, x * 2 + c)


def send_to(sent, src, dst, send_sem, recv_sem, where):
    copy = pltpu.make_async_remote_copy(
        src_ref=src, dst_ref=dst, send_sem=send_sem, recv_sem=recv_sem,
        device_id=where, device_id_type=MESH,
    )
    copy.start()
    sent.append(copy)
    return copy


FLOWS = (("x", "y", "z"), ("y", "z", "x"), ("z", "x", "y"))


def feed_kernel(
    q_ref, key_ref, value_ref, length_ref,
    wo_ref, res_ref, gain_ref, w_ref, wd_ref, al_ref, up_ref, tenant_ref, out_ref,
    keys, values, heads, ctx_all, wo, res, z, sq, iv, wraw, up,
    wt, part, got_a, got_b, summed, got_c, hid, wd, hb, ht,
    rows1, got1, rows2, got2, wide, rows3, got3, acc,
    kvsem, lsem, asem, arsem, qsem, qrsem, zsem, zrsem, isem, irsem,
    ssem, rsem, cssem, crsem, essem, ersem,
):
    pos = position()
    sent = []
    send = functools.partial(send_to, sent)
    c = pos["c"]
    y_me, z_me, x_me = pos["y"], pos["z"], pos["x"]
    peer = device_at(pos, c=1)
    plane = [(dy, dz) for dy in range(4) for dz in range(4) if dy or dz]
    line = [(dx, dc) for dx in range(4) for dc in range(2) if dx or dc]
    partners = [device_at(pos, y=dy, z=dz) for dy, dz in plane]
    partners += [device_at(pos, x=dx, c=dc) for dx, dc in line]
    barrier = pltpu.get_barrier_semaphore()
    for partner in partners:
        pl.semaphore_signal(barrier, inc=1, device_id=partner, device_id_type=MESH)

    streams = []
    for j in range(4):
        streams.append((
            pltpu.make_async_copy(key_ref.at[j], keys.at[j], kvsem.at[0, j]),
            pltpu.make_async_copy(value_ref.at[j], values.at[j], kvsem.at[1, j]),
        ))
        for copy in streams[j]:
            copy.start()
    loads = [
        pltpu.make_async_copy(w_ref, wraw, lsem.at[0]),
        pltpu.make_async_copy(wo_ref, wo, lsem.at[1]),
        pltpu.make_async_copy(res_ref, res, lsem.at[2]),
        pltpu.make_async_copy(wd_ref, wd.at[:BLOCK, :MODEL_WIDTH], lsem.at[3]),
        pltpu.make_async_copy(al_ref, wd.at[:BLOCK, MODEL_WIDTH:], lsem.at[4]),
        pltpu.make_async_copy(up_ref, up, lsem.at[5]),
    ]
    for copy in loads:
        copy.start()
    load_w, load_wo, load_res, load_wd, load_al, load_up = loads

    row = lax.broadcasted_iota(jnp.int32, (128, 128), 0)
    col = lax.broadcasted_iota(jnp.int32, (128, 128), 1)
    turn = (col == lax.rem(row, HQ) * 4 + row // HQ).astype(BF16)
    queries = jnp.dot(
        turn, q_ref[...].reshape(128, HD), preferred_element_type=F32
    ).astype(BF16)
    slots = lax.broadcasted_iota(jnp.int32, (HQ, CACHE), 1)
    for j in range(4):
        streams[j][0].wait()
        scores = lax.dot_general(
            queries[j * HQ:(j + 1) * HQ], keys[j], NT, preferred_element_type=F32
        ) * HD ** (-0.5)
        scores = jnp.where(slots < length_ref[j], scores, -jnp.inf)
        expo = jnp.exp(scores - jnp.max(scores, axis=1, keepdims=True))
        probs = (expo * (1.0 / jnp.sum(expo, axis=1, keepdims=True))).astype(BF16)
        streams[j][1].wait()
        heads[j * HQ:(j + 1) * HQ, :] = jnp.dot(
            probs, values[j], preferred_element_type=F32
        ).astype(BF16)
    head = lax.rem(row // 4, 4) * 8 + row // 16
    turn = (col == lax.rem(row, 4) * HQ + head).astype(BF16)
    context = jnp.dot(turn, heads[...], preferred_element_type=F32).astype(BF16)
    for n in range(8):
        ctx_all[y_me, z_me, :, n * HD:(n + 1) * HD] = context[n * 16:(n + 1) * 16]
    pl.semaphore_wait(barrier, len(partners))

    near, far = [], []
    for d in (2, 1, 3):
        for h, axis in enumerate(("y", "z")):
            view = ctx_all.at[y_me, z_me, :, h * 1024:(h + 1) * 1024]
            copy = send(
                view, view, asem.at[h, d - 1], arsem.at[h, d - 1], device_at(pos, **{axis: d})
            )
            near.append(copy)

    w_out = send(wd_ref, wd.at[BLOCK:, :MODEL_WIDTH], cssem.at[0], crsem.at[0], peer)
    a_out = send(al_ref, wd.at[BLOCK:, MODEL_WIDTH:], cssem.at[1], crsem.at[1], peer)

    def turn_columns(i, carry):
        start = i * 768
        both = wraw[:, :, pl.ds(pl.multiple_of(start, 768), 768)].reshape(896, 768).T
        for s in range(2):
            row = lax.broadcasted_iota(jnp.int32, (896, 448), 0)
            col = lax.broadcasted_iota(jnp.int32, (896, 448), 1)
            part_of = (row == 2 * col + s).astype(BF16)
            turned = jnp.dot(both, part_of, preferred_element_type=F32).astype(BF16)
            for g in range(48):
                n = start + 16 * g
                at = (n // BLOCK) * PAIR + s * BLOCK + lax.rem(n, BLOCK)
                wt[pl.ds(pl.multiple_of(at, 16), 16), :] = turned[16 * g:16 * g + 16]
        return carry

    load_w.wait()
    lax.fori_loop(0, 1, turn_columns, 0)
    for copy in near:
        copy.wait_recv()
    for d in (2, 1, 3):
        for h, axis in enumerate(("z", "y")):
            if h == 0:
                view = ctx_all.at[:, z_me, :, :1024]
            else:
                view = ctx_all.at[y_me, :, :, 1024:]
            copy = send(
                view, view, asem.at[h, 2 + d], arsem.at[h, 2 + d], device_at(pos, **{axis: d})
            )
            far.append(copy)
    lax.fori_loop(1, 3, turn_columns, 0)
    load_res.wait()
    load_wo.wait()

    row = lax.broadcasted_iota(jnp.int32, (128, 512), 0)
    col = lax.broadcasted_iota(jnp.int32, (128, 512), 1)
    f = x_me * 2 + c
    chosen = (col == (row // 8) * 32 + f * 4 + lax.rem(row, 4)).astype(BF16)
    stream = lax.dot_general(chosen, res[...], NT, preferred_element_type=F32)

    for copy in far:
        copy.wait_recv()
    quarter = lax.rem(lax.broadcasted_iota(jnp.int32, (HALF, 448), 0), 16) // 4
    projected = jnp.zeros((HALF, 448), F32)
    for q in range(4):
        r = lax.dot_general(
            ctx_all[...].reshape(HALF, 2048), wo[:, q * 2048:(q + 1) * 2048], NT,
            preferred_element_type=F32,
        )
        projected = jnp.where(quarter == q, r, projected)
    projected = projected.reshape(16, 16, 448)
    projected = projected[:, :8] + projected[:, 8:]
    projected = (projected + pltpu.roll(projected, 4, 1)).reshape(128, 448)
    stream = stream + projected
    normed = (stream * gain_ref[...]).astype(BF16)
    row = lax.broadcasted_iota(jnp.int32, (64, 128), 0)
    col = lax.broadcasted_iota(jnp.int32, (64, 128), 1)
    pick = (col == (row // 4) * 8 + lax.rem(row, 4)).astype(BF16)
    z[c, x_me] = jnp.dot(pick, normed, preferred_element_type=F32).astype(BF16)
    along, across = [], []
    for d in (2, 1, 3):
        view = z.at[c, x_me]
        copy = send(view, view, zsem.at[d - 1], zrsem.at[d - 1], device_at(pos, x=d))
        along.append((d, copy))
    for d in (0, 1, 3, 2):
        if d:
            dict(along)[d].wait_recv()
        view = z.at[c, lax.rem(x_me + 4 - d, 4)]
        copy = send(view, view, zsem.at[3 + d], zrsem.at[3 + d], peer)
        across.append(copy)

    squares = jnp.sum(stream * stream, axis=1, keepdims=True)
    row = lax.broadcasted_iota(jnp.int32, (128, 128), 0)
    col = lax.rem(lax.broadcasted_iota(jnp.int32, (128, 128), 1), 64)
    spread = jnp.where(row == (col // 4) * 8 + lax.rem(col, 4), squares, 0.0)
    sq[y_me, z_me] = jnp.broadcast_to(jnp.sum(spread, axis=0, keepdims=True), (8, 128))
    sums = []
    for n, (dy, dz) in enumerate(plane):
        view = sq.at[y_me, z_me]
        copy = send(view, view, qsem.at[n], qrsem.at[n], device_at(pos, y=dy, z=dz))
        sums.append(copy)
    for copy in across:
        copy.wait_recv()

    first = ("y", "z")
    me1 = [pos["y"], pos["z"]]
    me2 = [pos["z"], pos["y"]]

    def compute(h, p, lo, hi):
        def body(q, carry):
            a = p * 4 + q if h == 0 else q * 4 + p
            lhs = wt[pl.ds(pl.multiple_of(a * PAIR, PAIR), PAIR), :]
            r = lax.dot_general(
                lhs, z[h].reshape(HALF, 448), NT, preferred_element_type=F32
            )
            part[h, p, q] = r.astype(BF16)
            return carry

        lax.fori_loop(lo, hi, body, 0)

    step = [[lax.rem(me1[h] + d, 4) for d in range(4)] for h in range(2)]
    one = [[None, None], [None, None]]
    two = [[None, None], [None, None]]
    three = [[None] * 3, [None] * 3]
    for h in range(2):
        for side in range(2):
            compute(h, step[h][2], 2 * side, 2 * side + 2)
            one[h][side] = send(
                part.at[h, step[h][2], 2 * side:2 * side + 2], got_a.at[h, side],
                ssem.at[h, side], rsem.at[h, side],
                device_at(pos, **{first[h]: 1 if side == 0 else 3}),
            )
    for h in range(2):
        compute(h, step[h][1], 0, 4)
        compute(h, step[h][3], 0, 4)
    for copy in sums:
        copy.wait_recv()
    squares = jnp.sum(sq[...].reshape(16, 8, 128), axis=0)
    iv[c, x_me] = lax.rsqrt(squares / MODEL_WIDTH + 1e-06)
    scales = []
    for n, (dx, dc) in enumerate(line):
        view = iv.at[c, x_me]
        copy = send(view, view, isem.at[n], irsem.at[n], device_at(pos, x=dx, c=dc))
        scales.append(copy)
    for h in range(2):
        for side in range(2):
            to = 1 if side == 0 else 3
            p = step[h][to]
            one[h][side].wait_recv()

            def join(i, carry, h=h, side=side, p=p):
                q = 2 * side + i
                part[h, p, q] = (
                    part[h, p, q].astype(F32) + got_a[h, side, i].astype(F32)
                ).astype(BF16)
                return carry

            lax.fori_loop(0, 2, join, 0)
            two[h][side] = send(
                part.at[h, p], got_b.at[h, side], ssem.at[h, 2 + side], rsem.at[h, 2 + side],
                device_at(pos, **{first[h]: to}),
            )
    for h in range(2):
        compute(h, step[h][0], 0, 4)
    for h in range(2):
        for side in range(2):
            two[h][side].wait_recv()
        p = step[h][0]

        def total(q, h=h, p=p):
            return (
                part[h, p, q].astype(F32) + got_b[h, 0, q].astype(F32)
                + got_b[h, 1, q].astype(F32)
            )

        for d in (2, 1, 3):
            q = lax.rem(me2[h] + d, 4)
            summed[h, d - 1] = total(q).astype(BF16)
            three[h][d - 1] = send(
                summed.at[h, d - 1], got_c.at[h, d - 1], ssem.at[h, 3 + d], rsem.at[h, 3 + d],
                device_at(pos, **{first[1 - h]: d}),
            )
    for copy in scales:
        copy.wait_recv()
    left = lax.broadcasted_iota(jnp.int32, (1, 128), 1) < 64
    for h in range(2):
        inverse = jnp.concatenate(
            [jnp.where(left, iv[h, 2 * n, :1], iv[h, 2 * n + 1, :1]) for n in range(2)], axis=1
        )
        for d in range(3):
            three[h][d].wait_recv()
        p, q = step[h][0], me2[h]
        both = (
            part[h, p, q].astype(F32) + got_b[h, 0, q].astype(F32) + got_b[h, 1, q].astype(F32)
            + got_c[h, 0].astype(F32) + got_c[h, 1].astype(F32) + got_c[h, 2].astype(F32)
        ) * inverse
        gate, lift = both[:BLOCK], both[BLOCK:]
        hid[h] = (gate / (1.0 + jnp.exp(-gate)) * lift).astype(BF16)

    h_out = send(hid.at[1 - c], hb.at[BLOCK:], cssem.at[2], crsem.at[2], peer)
    hb[:BLOCK, :] = hid[c]
    for copy in (w_out, a_out, h_out):
        copy.wait_recv()
    load_wd.wait()
    load_al.wait()

    row = lax.broadcasted_iota(jnp.int32, (HALF, HALF), 0)
    col = lax.broadcasted_iota(jnp.int32, (HALF, HALF), 1)
    place = {"x": 64, "y": 16, "z": 4}
    for k, axes in enumerate(FLOWS):
        source = lax.rem(row, 4)
        for n, axis in enumerate(axes):
            source = source + lax.rem(row // (64, 16, 4)[n], 4) * place[axis]
        turn = (source == col).astype(BF16)
        ht[k] = lax.dot_general(turn, hb[...], NT, preferred_element_type=F32).astype(BF16)

    out1 = [[None] * 3 for _ in FLOWS]
    out2 = [[None] * 3 for _ in FLOWS]
    out3 = [[None] * 3 for _ in FLOWS]
    for k, axes in enumerate(FLOWS):
        def tile_of(start, width, k=k):
            r = jnp.dot(
                ht[k], wd[:, pl.ds(k * FLOW + start, width)], preferred_element_type=F32
            )
            rows1[k, :, pl.ds(start, width)] = r.astype(BF16)

        def body(i, carry, tile_of=tile_of):
            tile_of(pl.multiple_of(i * 256, 256), 256)
            return carry

        lax.fori_loop(0, 9, body, 0)
        tile_of(2304, 128)
        for d in (2, 1, 3):
            b = lax.rem(pos[axes[0]] + d, 4)
            out1[k][d - 1] = send(
                rows1.at[k, pl.ds(pl.multiple_of(b * 64, 64), 64)], got1.at[k, d - 1],
                essem.at[k, d - 1], ersem.at[k, d - 1], device_at(pos, **{axes[0]: d}),
            )
    for k, axes in enumerate(FLOWS):
        for d in range(3):
            out1[k][d].wait_recv()
        mine = pos[axes[0]] * 64

        def add1(i, carry, k=k, mine=mine):
            at = pl.multiple_of(i * 16, 16)
            r = rows1[k, pl.ds(pl.multiple_of(mine + at, 16), 16), :].astype(F32)
            for d in range(3):
                r = r + got1[k, d, pl.ds(at, 16), :].astype(F32)
            rows2[k, i] = r.astype(BF16)
            return carry

        lax.fori_loop(0, 4, add1, 0)
        for d in (2, 1, 3):
            b = lax.rem(pos[axes[1]] + d, 4)
            out2[k][d - 1] = send(
                rows2.at[k, b], got2.at[k, d - 1],
                essem.at[k, 2 + d], ersem.at[k, 2 + d], device_at(pos, **{axes[1]: d}),
            )
    wide[:, FLOW:] = jnp.zeros((16, 4 * PIECE - FLOW), F32)
    for k, axes in enumerate(FLOWS):
        for d in range(3):
            out2[k][d].wait_recv()
        r = rows2[k, pos[axes[1]]].astype(F32)
        for d in range(3):
            r = r + got2[k, d].astype(F32)
        wide[:, :FLOW] = r
        for to in range(4):
            rows3[k, to] = jnp.concatenate(
                [wide[4 * to:4 * to + 4, n * PIECE:(n + 1) * PIECE] for n in range(4)], axis=0
            ).astype(BF16)
        for d in (2, 1, 3):
            b = lax.rem(pos[axes[2]] + d, 4)
            out3[k][d - 1] = send(
                rows3.at[k, b], got3.at[k, d - 1],
                essem.at[k, 5 + d], ersem.at[k, 5 + d], device_at(pos, **{axes[2]: d}),
            )
    acc[...] = jnp.zeros(acc.shape, F32)
    for k, axes in enumerate(FLOWS):
        for d in range(3):
            out3[k][d].wait_recv()
        r = rows3[k, pos[axes[2]]].astype(F32)
        for d in range(3):
            r = r + got3[k, d].astype(F32)
        for n in range(4):
            width = min(PIECE, FLOW - n * PIECE)
            start = k * FLOW + n * PIECE
            acc[0:4, start:start + width] = r[4 * n:4 * n + 4, :width]

    low = acc[:, MODEL_WIDTH:]
    who = lax.broadcasted_iota(jnp.int32, low.shape, 0)
    owner = lax.broadcasted_iota(jnp.int32, low.shape, 1) // ADAPTER_RANK
    tenant = jnp.where(
        who == 0, tenant_ref[0],
        jnp.where(who == 1, tenant_ref[1], jnp.where(who == 2, tenant_ref[2], tenant_ref[3])),
    )
    load_up.wait()
    picked = jnp.where(owner == tenant, low, 0.0).astype(BF16)
    for n in range(7):
        cols = slice(n * 1024, (n + 1) * 1024)
        r = acc[:, cols] + jnp.dot(picked, up[:, cols], preferred_element_type=F32)
        out_ref[:, cols] = r[0:4]

    for copy in sent:
        copy.wait_send()


def feed(q, key, value, length, wo, res, gain, w, wd, al, up, tenant):
    vmem = pl.BlockSpec(memory_space=pltpu.VMEM)
    hbm = pl.BlockSpec(memory_space=pl.ANY)
    smem = pl.BlockSpec(memory_space=pltpu.SMEM)
    dma = pltpu.SemaphoreType.DMA
    return pl.pallas_call(
        feed_kernel,
        out_shape=jax.ShapeDtypeStruct((4, MODEL_WIDTH), F32),
        in_specs=[vmem, hbm, hbm, smem, hbm, hbm, vmem, hbm, hbm, hbm, hbm, smem],
        out_specs=vmem,
        scratch_shapes=[
            pltpu.VMEM((4, CACHE, HD), BF16),
            pltpu.VMEM((4, CACHE, HD), BF16),
            pltpu.VMEM((128, HD), BF16),
            pltpu.VMEM((4, 4, 16, 2048), BF16),
            pltpu.VMEM((448, 8192), BF16),
            pltpu.VMEM((448, 512), BF16),
            pltpu.VMEM((2, 4, 64, 448), BF16),
            pltpu.VMEM((4, 4, 8, 128), F32),
            pltpu.VMEM((2, 4, 8, 128), F32),
            pltpu.VMEM((448, 2, 2304), BF16),
            pltpu.VMEM((128, MODEL_WIDTH), BF16),
            pltpu.VMEM((16 * PAIR, 448), BF16),
            pltpu.VMEM((2, 4, 4, PAIR, HALF), BF16),
            pltpu.VMEM((2, 2, 2, PAIR, HALF), BF16),
            pltpu.VMEM((2, 2, 4, PAIR, HALF), BF16),
            pltpu.VMEM((2, 3, PAIR, HALF), BF16),
            pltpu.VMEM((2, 3, PAIR, HALF), BF16),
            pltpu.VMEM((2, BLOCK, HALF), BF16),
            pltpu.VMEM((PAIR, WIDE), BF16),
            pltpu.VMEM((PAIR, HALF), BF16),
            pltpu.VMEM((3, HALF, PAIR), BF16),
            pltpu.VMEM((3, HALF, FLOW), BF16),
            pltpu.VMEM((3, 3, 64, FLOW), BF16),
            pltpu.VMEM((3, 4, 16, FLOW), BF16),
            pltpu.VMEM((3, 3, 16, FLOW), BF16),
            pltpu.VMEM((16, 4 * PIECE), F32),
            pltpu.VMEM((3, 4, 16, PIECE), BF16),
            pltpu.VMEM((3, 3, 16, PIECE), BF16),
            pltpu.VMEM((8, WIDE), F32),
            dma((2, 4)), dma((6,)), dma((2, 6)), dma((2, 6)), dma((15,)), dma((15,)),
            dma((7,)), dma((7,)), dma((7,)), dma((7,)),
            dma((2, 7)), dma((2, 7)), dma((3,)), dma((3,)),
            dma((3, 9)), dma((3, 9)),
        ],
        compiler_params=pltpu.CompilerParams(
            collective_id=1, has_side_effects=True, vmem_limit_bytes=58 << 20
        ),
    )(q, key, value, length, wo, res, gain, w, wd, al, up, tenant)


def local(
    query,
    cached_key_rows,
    cached_value_rows,
    request_cache_length,
    request_tenant_index,
    residual,
    feedforward_norm_gain,
    attention_output_weight,
    gate_up_weight,
    down_projection_weight,
    adapter_down_maps,
    adapter_up_maps,
):
    result = feed(
        query.reshape(4, HQ, HD).transpose(1, 0, 2),
        cached_key_rows, cached_value_rows, request_cache_length,
        attention_output_weight.T, residual.T,
        feedforward_norm_gain.astype(F32).reshape(1, -1), gate_up_weight,
        down_projection_weight.reshape(BLOCK, MODEL_WIDTH),
        adapter_down_maps.reshape(BLOCK, TENANT_COUNT * ADAPTER_RANK),
        adapter_up_maps, request_tenant_index,
    )
    return result.astype(BF16)


def solution(mesh):
    in_specs = (
        P(("attn", "ffn"), None),
        P(("attn", "ffn"), None, None),
        P(("attn", "ffn"), None, None),
        P(("attn", "ffn")),
        P(("attn", "ffn")),
        P(None, "attn"),
        P("attn"),
        P(None, "attn"),
        P("attn", None, "ffn"),
        P("ffn", "attn", None, None),
        P("ffn", "attn", None, None),
        P(),
    )
    out_specs = P(("attn", "ffn"), None)
    return jax.shard_map(local, mesh=mesh, in_specs=in_specs, out_specs=out_specs, check_vma=False)
```

```python
import functools

import jax
import jax.numpy as jnp
from jax import lax
from jax.experimental import pallas as pl
from jax.experimental.pallas import tpu as pltpu
from jax.sharding import PartitionSpec as P

MODEL_WIDTH = 7168
HQ = 32
HD = 256
CACHE = 2048
TENANT_COUNT = 8
ADAPTER_RANK = 16
MESH = pl.DeviceIdType.MESH
BLOCK = 144
PAIR = 2 * BLOCK
HALF = 256
WIDE = MODEL_WIDTH + TENANT_COUNT * ADAPTER_RANK
FLOW = WIDE // 3
PIECE = 640
NT = (((1,), (1,)), ((), ()))
F32 = jnp.float32
BF16 = jnp.bfloat16


def position():
    a = lax.axis_index("attn")
    f = lax.axis_index("ffn")
    return {"y": a // 4, "z": lax.rem(a, 4), "x": f // 2, "c": lax.rem(f, 2)}


def device_at(pos, **steps):
    y = lax.rem(pos["y"] + steps.get("y", 0), 4)
    z = lax.rem(pos["z"] + steps.get("z", 0), 4)
    x = lax.rem(pos["x"] + steps.get("x", 0), 4)
    c = lax.rem(pos["c"] + steps.get("c", 0), 2)
    return (y * 4 + z, x * 2 + c)


def send_to(sent, src, dst, send_sem, recv_sem, where):
    copy = pltpu.make_async_remote_copy(
        src_ref=src, dst_ref=dst, send_sem=send_sem, recv_sem=recv_sem,
        device_id=where, device_id_type=MESH,
    )
    copy.start()
    sent.append(copy)
    return copy


CHUNKS = ((0, 640, 1280), (1280, 1920, FLOW))
FLOWS = (("x", "y", "z"), ("y", "z", "x"), ("z", "x", "y"))


def feed_kernel(
    q_ref, key_ref, value_ref, length_ref,
    wo_ref, res_ref, gain_ref, w_ref, wd_ref, al_ref, up_ref, tenant_ref, out_ref,
    keys, values, heads, ctx_all, wo, res, z, sq, iv, wraw, up,
    wt, part, got_a, got_b, summed, got_c, hid, wd, hb, ht,
    rows1, got1, gotb, rows2, got2, wide, rows3, got3, acc,
    kvsem, lsem, asem, arsem, qsem, qrsem, zsem, zrsem, isem, irsem,
    ssem, rsem, cssem, crsem, essem, ersem, fssem, frsem,
):
    pos = position()
    sent = []
    send = functools.partial(send_to, sent)
    c = pos["c"]
    y_me, z_me, x_me = pos["y"], pos["z"], pos["x"]
    peer = device_at(pos, c=1)
    plane = [(dy, dz) for dy in range(4) for dz in range(4) if dy or dz]
    line = [(dx, dc) for dx in range(4) for dc in range(2) if dx or dc]
    partners = [device_at(pos, y=dy, z=dz) for dy, dz in plane]
    partners += [device_at(pos, x=dx, c=dc) for dx, dc in line]
    barrier = pltpu.get_barrier_semaphore()
    for partner in partners:
        pl.semaphore_signal(barrier, inc=1, device_id=partner, device_id_type=MESH)

    streams = []
    for j in range(4):
        streams.append((
            pltpu.make_async_copy(key_ref.at[j], keys.at[j], kvsem.at[0, j]),
            pltpu.make_async_copy(value_ref.at[j], values.at[j], kvsem.at[1, j]),
        ))
        for copy in streams[j]:
            copy.start()
    loads = [
        pltpu.make_async_copy(w_ref, wraw, lsem.at[0]),
        pltpu.make_async_copy(wo_ref, wo, lsem.at[1]),
        pltpu.make_async_copy(res_ref, res, lsem.at[2]),
        pltpu.make_async_copy(wd_ref, wd.at[:BLOCK, :MODEL_WIDTH], lsem.at[3]),
        pltpu.make_async_copy(al_ref, wd.at[:BLOCK, MODEL_WIDTH:], lsem.at[4]),
        pltpu.make_async_copy(up_ref, up, lsem.at[5]),
    ]
    load_w, load_wo, load_res, load_wd, load_al, load_up = loads

    row = lax.broadcasted_iota(jnp.int32, (128, 128), 0)
    col = lax.broadcasted_iota(jnp.int32, (128, 128), 1)
    turn = (col == lax.rem(row, HQ) * 4 + row // HQ).astype(BF16)
    queries = jnp.dot(
        turn, q_ref[...].reshape(128, HD), preferred_element_type=F32
    ).astype(BF16)
    slots = lax.broadcasted_iota(jnp.int32, (HQ, CACHE), 1)
    for j in range(4):
        streams[j][0].wait()
        scores = lax.dot_general(
            queries[j * HQ:(j + 1) * HQ], keys[j], NT, preferred_element_type=F32
        ) * HD ** (-0.5)
        scores = jnp.where(slots < length_ref[j], scores, -jnp.inf)
        expo = jnp.exp(scores - jnp.max(scores, axis=1, keepdims=True))
        probs = (expo * (1.0 / jnp.sum(expo, axis=1, keepdims=True))).astype(BF16)
        streams[j][1].wait()
        heads[j * HQ:(j + 1) * HQ, :] = jnp.dot(
            probs, values[j], preferred_element_type=F32
        ).astype(BF16)
    for copy in loads:
        copy.start()
    head = lax.rem(row // 4, 4) * 8 + row // 16
    turn = (col == lax.rem(row, 4) * HQ + head).astype(BF16)
    context = jnp.dot(turn, heads[...], preferred_element_type=F32).astype(BF16)
    for n in range(8):
        ctx_all[y_me, z_me, :, n * HD:(n + 1) * HD] = context[n * 16:(n + 1) * 16]
    pl.semaphore_wait(barrier, len(partners))

    near, far = [], []
    for d in (2, 1, 3):
        for h, axis in enumerate(("y", "z")):
            view = ctx_all.at[y_me, z_me, :, h * 1024:(h + 1) * 1024]
            copy = send(
                view, view, asem.at[h, d - 1], arsem.at[h, d - 1], device_at(pos, **{axis: d})
            )
            near.append(copy)

    w_out = send(wd_ref, wd.at[BLOCK:, :MODEL_WIDTH], cssem.at[0], crsem.at[0], peer)
    a_out = send(al_ref, wd.at[BLOCK:, MODEL_WIDTH:], cssem.at[1], crsem.at[1], peer)

    def turn_columns(i, carry):
        start = i * 768
        both = wraw[:, :, pl.ds(pl.multiple_of(start, 768), 768)].reshape(896, 768).T
        for s in range(2):
            row = lax.broadcasted_iota(jnp.int32, (896, 448), 0)
            col = lax.broadcasted_iota(jnp.int32, (896, 448), 1)
            part_of = (row == 2 * col + s).astype(BF16)
            turned = jnp.dot(both, part_of, preferred_element_type=F32).astype(BF16)
            for g in range(48):
                n = start + 16 * g
                at = (n // BLOCK) * PAIR + s * BLOCK + lax.rem(n, BLOCK)
                wt[pl.ds(pl.multiple_of(at, 16), 16), :] = turned[16 * g:16 * g + 16]
        return carry

    load_w.wait()
    lax.fori_loop(0, 1, turn_columns, 0)
    for copy in near:
        copy.wait_recv()
    for d in (2, 1, 3):
        for h, axis in enumerate(("z", "y")):
            if h == 0:
                view = ctx_all.at[:, z_me, :, :1024]
            else:
                view = ctx_all.at[y_me, :, :, 1024:]
            copy = send(
                view, view, asem.at[h, 2 + d], arsem.at[h, 2 + d], device_at(pos, **{axis: d})
            )
            far.append(copy)
    lax.fori_loop(1, 3, turn_columns, 0)
    load_res.wait()
    load_wo.wait()

    row = lax.broadcasted_iota(jnp.int32, (128, 512), 0)
    col = lax.broadcasted_iota(jnp.int32, (128, 512), 1)
    f = x_me * 2 + c
    chosen = (col == (row // 8) * 32 + f * 4 + lax.rem(row, 4)).astype(BF16)
    stream = lax.dot_general(chosen, res[...], NT, preferred_element_type=F32)

    for copy in far:
        copy.wait_recv()
    quarter = lax.rem(lax.broadcasted_iota(jnp.int32, (HALF, 448), 0), 16) // 4
    projected = jnp.zeros((HALF, 448), F32)
    for q in range(4):
        r = lax.dot_general(
            ctx_all[...].reshape(HALF, 2048), wo[:, q * 2048:(q + 1) * 2048], NT,
            preferred_element_type=F32,
        )
        projected = jnp.where(quarter == q, r, projected)
    projected = projected.reshape(16, 16, 448)
    projected = projected[:, :8] + projected[:, 8:]
    projected = (projected + pltpu.roll(projected, 4, 1)).reshape(128, 448)
    stream = stream + projected
    normed = (stream * gain_ref[...].astype(F32).reshape(1, 448)).astype(BF16)
    row = lax.broadcasted_iota(jnp.int32, (64, 128), 0)
    col = lax.broadcasted_iota(jnp.int32, (64, 128), 1)
    pick = (col == (row // 4) * 8 + lax.rem(row, 4)).astype(BF16)
    z[c, x_me] = jnp.dot(pick, normed, preferred_element_type=F32).astype(BF16)
    along, across = [], []
    for d in (2, 1, 3):
        view = z.at[c, x_me]
        copy = send(view, view, zsem.at[d - 1], zrsem.at[d - 1], device_at(pos, x=d))
        along.append((d, copy))
    for d in (0, 1, 3, 2):
        if d:
            dict(along)[d].wait_recv()
        view = z.at[c, lax.rem(x_me + 4 - d, 4)]
        copy = send(view, view, zsem.at[3 + d], zrsem.at[3 + d], peer)
        across.append(copy)

    squares = jnp.sum(stream * stream, axis=1, keepdims=True)
    row = lax.broadcasted_iota(jnp.int32, (128, 128), 0)
    col = lax.rem(lax.broadcasted_iota(jnp.int32, (128, 128), 1), 64)
    spread = jnp.where(row == (col // 4) * 8 + lax.rem(col, 4), squares, 0.0)
    sq[y_me, z_me] = jnp.broadcast_to(jnp.sum(spread, axis=0, keepdims=True), (8, 128))
    sums = []
    for n, (dy, dz) in enumerate(plane):
        view = sq.at[y_me, z_me]
        copy = send(view, view, qsem.at[n], qrsem.at[n], device_at(pos, y=dy, z=dz))
        sums.append(copy)

    order = (c, 1 - c)

    def along_first(h, d):
        return device_at(pos, y=jnp.where(h == 0, d, 0), z=jnp.where(h == 0, 0, d))

    def along_second(h, d):
        return device_at(pos, y=jnp.where(h == 0, 0, d), z=jnp.where(h == 0, d, 0))

    def compute(h, p, lo, hi):
        def body(q, carry):
            a = jnp.where(h == 0, p * 4 + q, q * 4 + p)
            lhs = wt[pl.ds(pl.multiple_of(a * PAIR, PAIR), PAIR), :]
            r = lax.dot_general(
                lhs, z[h].reshape(HALF, 448), NT, preferred_element_type=F32
            ).astype(BF16)
            part[h, 0, p, q] = r[:, :128]
            part[h, 1, p, q] = r[:, 128:]
            return carry

        lax.fori_loop(lo, hi, body, 0)

    me1 = [jnp.where(h == 0, y_me, z_me) for h in order]
    me2 = [jnp.where(h == 0, z_me, y_me) for h in order]
    step = [[lax.rem(me1[n] + d, 4) for d in range(4)] for n in range(2)]
    one = [[[None] * 2 for _ in range(2)] for _ in range(2)]
    two = [[[None] * 2 for _ in range(2)] for _ in range(2)]
    three = [[[None] * 3 for _ in range(2)] for _ in range(2)]
    for n, h in enumerate(order):
        if n == 1:
            for copy in across:
                copy.wait_recv()
        for side in range(2):
            compute(h, step[n][2], 2 * side, 2 * side + 2)
            for t in range(2):
                one[n][t][side] = send(
                    part.at[h, t, step[n][2], 2 * side:2 * side + 2], got_a.at[h, t, side],
                    ssem.at[h, t, side], rsem.at[h, t, side],
                    along_first(h, 1 if side == 0 else 3),
                )
    for n, h in enumerate(order):
        compute(h, step[n][1], 0, 4)
        compute(h, step[n][3], 0, 4)
    for t in range(2):
        for n, h in enumerate(order):
            for side in range(2):
                to = 1 if side == 0 else 3
                p = step[n][to]
                one[n][t][side].wait_recv()

                def join(i, carry, h=h, t=t, side=side, p=p):
                    q = 2 * side + i
                    part[h, t, p, q] = (
                        part[h, t, p, q].astype(F32) + got_a[h, t, side, i].astype(F32)
                    ).astype(BF16)
                    return carry

                lax.fori_loop(0, 2, join, 0)
                two[n][t][side] = send(
                    part.at[h, t, p], got_b.at[h, t, side],
                    ssem.at[h, t, 2 + side], rsem.at[h, t, 2 + side], along_first(h, to),
                )
    for n, h in enumerate(order):
        compute(h, step[n][0], 0, 4)
    for copy in sums:
        copy.wait_recv()
    squares = jnp.sum(sq[...].reshape(16, 8, 128), axis=0)
    iv[c, x_me] = lax.rsqrt(squares / MODEL_WIDTH + 1e-06)
    scales = []
    for n, (dx, dc) in enumerate(line):
        view = iv.at[c, x_me]
        scales.append(send(view, view, isem.at[n], irsem.at[n], device_at(pos, x=dx, c=dc)))
    for t in range(2):
        for n, h in enumerate(order):
            for side in range(2):
                two[n][t][side].wait_recv()
            for d in (2, 1, 3):
                q = lax.rem(me2[n] + d, 4)
                summed[h, t, d - 1] = (
                    part[h, t, step[n][0], q].astype(F32) + got_b[h, t, 0, q].astype(F32)
                    + got_b[h, t, 1, q].astype(F32)
                ).astype(BF16)
                three[n][t][d - 1] = send(
                    summed.at[h, t, d - 1], got_c.at[h, t, d - 1],
                    ssem.at[h, t, 3 + d], rsem.at[h, t, 3 + d], along_second(h, d),
                )
    for copy in scales:
        copy.wait_recv()
    left = lax.broadcasted_iota(jnp.int32, (1, 128), 1) < 64
    h_out = [None, None]
    for t in range(2):
        for n, h in ((1, 1 - c), (0, c)):
            inverse = jnp.where(left, iv[h, 2 * t, :1], iv[h, 2 * t + 1, :1])
            for d in range(3):
                three[n][t][d].wait_recv()
            p, q = step[n][0], me2[n]
            both = (
                part[h, t, p, q].astype(F32)
                + got_b[h, t, 0, q].astype(F32) + got_b[h, t, 1, q].astype(F32)
                + got_c[h, t, 0].astype(F32) + got_c[h, t, 1].astype(F32)
                + got_c[h, t, 2].astype(F32)
            ) * inverse
            gate, lift = both[:BLOCK], both[BLOCK:]
            hidden = (gate / (1.0 + jnp.exp(-gate)) * lift).astype(BF16)
            if n == 1:
                hid[t] = hidden
                h_out[t] = send(
                    hid.at[t], hb.at[BLOCK:, t * 128:(t + 1) * 128],
                    cssem.at[2 + t], crsem.at[2 + t], peer,
                )
            else:
                hb[:BLOCK, t * 128:(t + 1) * 128] = hidden

    for copy in (w_out, a_out, h_out[0], h_out[1]):
        copy.wait_recv()
    load_wd.wait()
    load_al.wait()

    row = lax.broadcasted_iota(jnp.int32, (HALF, HALF), 0)
    col = lax.broadcasted_iota(jnp.int32, (HALF, HALF), 1)
    place = {"x": 64, "y": 16, "z": 4}
    for k, axes in enumerate(FLOWS):
        source = lax.rem(row, 4)
        for n, axis in enumerate(axes):
            source = source + lax.rem(row // (64, 16, 4)[n], 4) * place[axis]
        turn = (source == col).astype(BF16)
        ht[k] = lax.dot_general(turn, hb[...], NT, preferred_element_type=F32).astype(BF16)

    out1 = [[[None] * 2 for _ in CHUNKS] for _ in FLOWS]
    outb = [[[None] * 2 for _ in CHUNKS] for _ in FLOWS]
    out2 = [[[None] * 3 for _ in CHUNKS] for _ in FLOWS]
    out3 = [[None] * 3 for _ in FLOWS]

    def rows_at(k, d):
        b = lax.rem(pos[FLOWS[k][0]] + d, 4)
        return pl.ds(pl.multiple_of(b * 64, 64), 64)

    for t, (start, middle, stop) in enumerate(CHUNKS):
        for k, axes in enumerate(FLOWS):
            rows1[k, :, start:stop] = jnp.dot(
                ht[k], wd[:, k * FLOW + start:k * FLOW + stop], preferred_element_type=F32
            ).astype(BF16)
            for side, cols in enumerate((slice(start, middle), slice(middle, stop))):
                out1[k][t][side] = send(
                    rows1.at[k, rows_at(k, 2), cols], got1.at[k, :, cols],
                    essem.at[k, t, side], ersem.at[k, t, side],
                    device_at(pos, **{axes[0]: 1 if side == 0 else 3}),
                )
    for t, (start, middle, stop) in enumerate(CHUNKS):
        for k, axes in enumerate(FLOWS):
            for side, cols in enumerate((slice(start, middle), slice(middle, stop))):
                to = 1 if side == 0 else 3
                out1[k][t][side].wait_recv()
                rows1[k, rows_at(k, to), cols] = (
                    rows1[k, rows_at(k, to), cols].astype(F32) + got1[k, :, cols].astype(F32)
                ).astype(BF16)
                outb[k][t][side] = send(
                    rows1.at[k, rows_at(k, to), start:stop], gotb.at[k, side, :, start:stop],
                    essem.at[k, t, 2 + side], ersem.at[k, t, 2 + side],
                    device_at(pos, **{axes[0]: to}),
                )
    for t, (start, middle, stop) in enumerate(CHUNKS):
        for k, axes in enumerate(FLOWS):
            for side in range(2):
                outb[k][t][side].wait_recv()
            mine = pos[axes[0]] * 64
            for i in range(4):
                at = pl.multiple_of(mine + i * 16, 16)
                here = slice(i * 16, (i + 1) * 16)
                rows2[k, i, :, start:stop] = (
                    rows1[k, pl.ds(at, 16), start:stop].astype(F32)
                    + gotb[k, 0, here, start:stop].astype(F32)
                    + gotb[k, 1, here, start:stop].astype(F32)
                ).astype(BF16)
            for d in (2, 1, 3):
                b = lax.rem(pos[axes[1]] + d, 4)
                out2[k][t][d - 1] = send(
                    rows2.at[k, b, :, start:stop], got2.at[k, d - 1, :, start:stop],
                    essem.at[k, t, 3 + d], ersem.at[k, t, 3 + d],
                    device_at(pos, **{axes[1]: d}),
                )
    wide[:, FLOW:] = jnp.zeros((16, 4 * PIECE - FLOW), F32)
    for k, axes in enumerate(FLOWS):
        for t in range(len(CHUNKS)):
            for d in range(3):
                out2[k][t][d].wait_recv()
        r = rows2[k, pos[axes[1]]].astype(F32)
        for d in range(3):
            r = r + got2[k, d].astype(F32)
        wide[:, :FLOW] = r
        for to in range(4):
            rows3[k, to] = jnp.concatenate(
                [wide[4 * to:4 * to + 4, n * PIECE:(n + 1) * PIECE] for n in range(4)], axis=0
            ).astype(BF16)
        for d in (2, 1, 3):
            b = lax.rem(pos[axes[2]] + d, 4)
            out3[k][d - 1] = send(
                rows3.at[k, b], got3.at[k, d - 1],
                fssem.at[k, d - 1], frsem.at[k, d - 1], device_at(pos, **{axes[2]: d}),
            )
    acc[...] = jnp.zeros(acc.shape, F32)
    for k, axes in enumerate(FLOWS):
        for d in range(3):
            out3[k][d].wait_recv()
        r = rows3[k, pos[axes[2]]].astype(F32)
        for d in range(3):
            r = r + got3[k, d].astype(F32)
        for n in range(4):
            width = min(PIECE, FLOW - n * PIECE)
            start = k * FLOW + n * PIECE
            acc[0:4, start:start + width] = r[4 * n:4 * n + 4, :width]

    low = acc[:, MODEL_WIDTH:]
    who = lax.broadcasted_iota(jnp.int32, low.shape, 0)
    owner = lax.broadcasted_iota(jnp.int32, low.shape, 1) // ADAPTER_RANK
    tenant = jnp.where(
        who == 0, tenant_ref[0],
        jnp.where(who == 1, tenant_ref[1], jnp.where(who == 2, tenant_ref[2], tenant_ref[3])),
    )
    load_up.wait()
    picked = jnp.where(owner == tenant, low, 0.0).astype(BF16)
    for n in range(7):
        cols = slice(n * 1024, (n + 1) * 1024)
        r = acc[:, cols] + jnp.dot(picked, up[:, cols], preferred_element_type=F32)
        out_ref[:, cols] = r[0:4]

    for copy in sent:
        copy.wait_send()


def feed(q, key, value, length, wo, res, gain, w, wd, al, up, tenant):
    vmem = pl.BlockSpec(memory_space=pltpu.VMEM)
    hbm = pl.BlockSpec(memory_space=pl.ANY)
    smem = pl.BlockSpec(memory_space=pltpu.SMEM)
    dma = pltpu.SemaphoreType.DMA
    return pl.pallas_call(
        feed_kernel,
        out_shape=jax.ShapeDtypeStruct((4, MODEL_WIDTH), F32),
        in_specs=[vmem, hbm, hbm, smem, hbm, hbm, vmem, hbm, hbm, hbm, hbm, smem],
        out_specs=vmem,
        scratch_shapes=[
            pltpu.VMEM((4, CACHE, HD), BF16),
            pltpu.VMEM((4, CACHE, HD), BF16),
            pltpu.VMEM((128, HD), BF16),
            pltpu.VMEM((4, 4, 16, 2048), BF16),
            pltpu.VMEM((448, 8192), BF16),
            pltpu.VMEM((448, 512), BF16),
            pltpu.VMEM((2, 4, 64, 448), BF16),
            pltpu.VMEM((4, 4, 8, 128), F32),
            pltpu.VMEM((2, 4, 8, 128), F32),
            pltpu.VMEM((448, 2, 2304), BF16),
            pltpu.VMEM((128, MODEL_WIDTH), BF16),
            pltpu.VMEM((16 * PAIR, 448), BF16),
            pltpu.VMEM((2, 2, 4, 4, PAIR, 128), BF16),
            pltpu.VMEM((2, 2, 2, 2, PAIR, 128), BF16),
            pltpu.VMEM((2, 2, 2, 4, PAIR, 128), BF16),
            pltpu.VMEM((2, 2, 3, PAIR, 128), BF16),
            pltpu.VMEM((2, 2, 3, PAIR, 128), BF16),
            pltpu.VMEM((2, BLOCK, 128), BF16),
            pltpu.VMEM((PAIR, WIDE), BF16),
            pltpu.VMEM((PAIR, HALF), BF16),
            pltpu.VMEM((3, HALF, PAIR), BF16),
            pltpu.VMEM((3, HALF, FLOW), BF16),
            pltpu.VMEM((3, 64, FLOW), BF16),
            pltpu.VMEM((3, 2, 64, FLOW), BF16),
            pltpu.VMEM((3, 4, 16, FLOW), BF16),
            pltpu.VMEM((3, 3, 16, FLOW), BF16),
            pltpu.VMEM((16, 4 * PIECE), F32),
            pltpu.VMEM((3, 4, 16, PIECE), BF16),
            pltpu.VMEM((3, 3, 16, PIECE), BF16),
            pltpu.VMEM((8, WIDE), F32),
            dma((2, 4)), dma((6,)), dma((2, 6)), dma((2, 6)), dma((15,)), dma((15,)),
            dma((7,)), dma((7,)), dma((7,)), dma((7,)),
            dma((2, 2, 7)), dma((2, 2, 7)), dma((4,)), dma((4,)),
            dma((3, 2, 7)), dma((3, 2, 7)), dma((3, 3)), dma((3, 3)),
        ],
        compiler_params=pltpu.CompilerParams(
            collective_id=1, has_side_effects=True, vmem_limit_bytes=58 << 20
        ),
    )(q, key, value, length, wo, res, gain, w, wd, al, up, tenant)


def local(
    query,
    cached_key_rows,
    cached_value_rows,
    request_cache_length,
    request_tenant_index,
    residual,
    feedforward_norm_gain,
    attention_output_weight,
    gate_up_weight,
    down_projection_weight,
    adapter_down_maps,
    adapter_up_maps,
):
    result = feed(
        query.reshape(4, HQ, HD).transpose(1, 0, 2),
        cached_key_rows, cached_value_rows, request_cache_length,
        attention_output_weight.T, residual.T,
        feedforward_norm_gain, gate_up_weight,
        down_projection_weight.reshape(BLOCK, MODEL_WIDTH),
        adapter_down_maps.reshape(BLOCK, TENANT_COUNT * ADAPTER_RANK),
        adapter_up_maps, request_tenant_index,
    )
    return result.astype(BF16)


def solution(mesh):
    in_specs = (
        P(("attn", "ffn"), None),
        P(("attn", "ffn"), None, None),
        P(("attn", "ffn"), None, None),
        P(("attn", "ffn")),
        P(("attn", "ffn")),
        P(None, "attn"),
        P("attn"),
        P(None, "attn"),
        P("attn", None, "ffn"),
        P("ffn", "attn", None, None),
        P("ffn", "attn", None, None),
        P(),
    )
    out_specs = P(("attn", "ffn"), None)
    return jax.shard_map(local, mesh=mesh, in_specs=in_specs, out_specs=out_specs, check_vma=False)
```

```python
import functools

import jax
import jax.numpy as jnp
from jax import lax
from jax.experimental import pallas as pl
from jax.experimental.pallas import tpu as pltpu
from jax.sharding import PartitionSpec as P

MODEL_WIDTH = 7168
HQ = 32
HD = 256
CACHE = 2048
TENANT_COUNT = 8
ADAPTER_RANK = 16
MESH = pl.DeviceIdType.MESH
BLOCK = 144
PAIR = 2 * BLOCK
HALF = 256
WIDE = MODEL_WIDTH + TENANT_COUNT * ADAPTER_RANK
FLOW = WIDE // 3
PIECE = 640
NT = (((1,), (1,)), ((), ()))
F32 = jnp.float32
BF16 = jnp.bfloat16


def position():
    a = lax.axis_index("attn")
    f = lax.axis_index("ffn")
    return {"y": a // 4, "z": lax.rem(a, 4), "x": f // 2, "c": lax.rem(f, 2)}


def device_at(pos, **steps):
    y = lax.rem(pos["y"] + steps.get("y", 0), 4)
    z = lax.rem(pos["z"] + steps.get("z", 0), 4)
    x = lax.rem(pos["x"] + steps.get("x", 0), 4)
    c = lax.rem(pos["c"] + steps.get("c", 0), 2)
    return (y * 4 + z, x * 2 + c)


def send_to(sent, src, dst, send_sem, recv_sem, where):
    copy = pltpu.make_async_remote_copy(
        src_ref=src, dst_ref=dst, send_sem=send_sem, recv_sem=recv_sem,
        device_id=where, device_id_type=MESH,
    )
    copy.start()
    sent.append(copy)
    return copy


CHUNKS = ((0, 640, 1280), (1280, 1920, FLOW))
FLOWS = (("x", "y", "z"), ("y", "z", "x"), ("z", "x", "y"))


def feed_kernel(
    q_ref, key_ref, value_ref, length_ref,
    wo_ref, res_ref, gain_ref, w_ref, wd_ref, al_ref, up_ref, tenant_ref, out_ref,
    keys, values, heads, ctx_all, wo, res, z, sq, iv, wraw, up,
    wt, part, got_a, got_b, summed, got_c, hid, wd, hb, ht,
    rows1, got1, gotb, rows2, got2, wide, rows3, got3, acc,
    kvsem, lsem, asem, arsem, qsem, qrsem, zsem, zrsem, isem, irsem,
    ssem, rsem, cssem, crsem, essem, ersem, fssem, frsem,
):
    pos = position()
    sent = []
    send = functools.partial(send_to, sent)
    c = pos["c"]
    y_me, z_me, x_me = pos["y"], pos["z"], pos["x"]
    peer = device_at(pos, c=1)
    plane = [(dy, dz) for dy in range(4) for dz in range(4) if dy or dz]
    line = [(dx, dc) for dx in range(4) for dc in range(2) if dx or dc]
    partners = [device_at(pos, y=dy, z=dz) for dy, dz in plane]
    partners += [device_at(pos, x=dx, c=dc) for dx, dc in line]
    barrier = pltpu.get_barrier_semaphore()
    for partner in partners:
        pl.semaphore_signal(barrier, inc=1, device_id=partner, device_id_type=MESH)

    streams = [
        (
            pltpu.make_async_copy(key_ref.at[j], keys.at[j], kvsem.at[0, j]),
            pltpu.make_async_copy(value_ref.at[j], values.at[j], kvsem.at[1, j]),
        )
        for j in range(4)
    ]
    for j in range(2):
        for copy in streams[j]:
            copy.start()
    loads = [
        pltpu.make_async_copy(w_ref, wraw, lsem.at[0]),
        pltpu.make_async_copy(wo_ref, wo, lsem.at[1]),
        pltpu.make_async_copy(res_ref, res, lsem.at[2]),
        pltpu.make_async_copy(wd_ref, wd.at[:BLOCK, :MODEL_WIDTH], lsem.at[3]),
        pltpu.make_async_copy(al_ref, wd.at[:BLOCK, MODEL_WIDTH:], lsem.at[4]),
        pltpu.make_async_copy(up_ref, up, lsem.at[5]),
    ]
    load_w, load_wo, load_res, load_wd, load_al, load_up = loads

    row = lax.broadcasted_iota(jnp.int32, (128, 128), 0)
    col = lax.broadcasted_iota(jnp.int32, (128, 128), 1)
    turn = (col == lax.rem(row, HQ) * 4 + row // HQ).astype(BF16)
    queries = jnp.dot(
        turn, q_ref[...].reshape(128, HD), preferred_element_type=F32
    ).astype(BF16)
    slots = lax.broadcasted_iota(jnp.int32, (HQ, CACHE), 1)
    near = [[], []]
    far = [[], []]

    def attend(j):
        streams[j][0].wait()
        if j < 2:
            streams[j + 2][0].start()
        scores = lax.dot_general(
            queries[j * HQ:(j + 1) * HQ], keys[j], NT, preferred_element_type=F32
        ) * HD ** (-0.5)
        scores = jnp.where(slots < length_ref[j], scores, -jnp.inf)
        expo = jnp.exp(scores - jnp.max(scores, axis=1, keepdims=True))
        probs = (expo * (1.0 / jnp.sum(expo, axis=1, keepdims=True))).astype(BF16)
        streams[j][1].wait()
        if j < 2:
            streams[j + 2][1].start()
        return jnp.dot(probs, values[j], preferred_element_type=F32).astype(BF16)

    def place_pair(t, first, second):
        heads[:HQ, :] = first
        heads[HQ:, :] = second
        row = lax.broadcasted_iota(jnp.int32, (64, 64), 0)
        col = lax.broadcasted_iota(jnp.int32, (64, 64), 1)
        source = lax.rem(row, 2) * HQ + (lax.rem(row, 16) // 2) * 4 + row // 16
        turn = (col == source).astype(BF16)
        context = jnp.dot(turn, heads[...], preferred_element_type=F32).astype(BF16)
        for n in range(4):
            ctx_all[t, y_me, z_me, :, n * HD:(n + 1) * HD] = context[n * 16:(n + 1) * 16]

    def send_near(t):
        for d in (2, 1, 3):
            for h, axis in enumerate(("y", "z")):
                view = ctx_all.at[t, y_me, z_me, :, h * 512:(h + 1) * 512]
                near[t].append(send(
                    view, view, asem.at[t, h, d - 1], arsem.at[t, h, d - 1],
                    device_at(pos, **{axis: d}),
                ))

    def send_far(t):
        for copy in near[t]:
            copy.wait_recv()
        for d in (2, 1, 3):
            for h, axis in enumerate(("z", "y")):
                if h == 0:
                    view = ctx_all.at[t, :, z_me, :, :512]
                else:
                    view = ctx_all.at[t, y_me, :, :, 512:]
                far[t].append(send(
                    view, view, asem.at[t, h, 2 + d], arsem.at[t, h, 2 + d],
                    device_at(pos, **{axis: d}),
                ))

    place_pair(0, attend(0), attend(1))
    pl.semaphore_wait(barrier, len(partners))
    send_near(0)
    third = attend(2)
    for copy in loads:
        copy.start()
    send_far(0)
    place_pair(1, third, attend(3))
    send_near(1)
    send_far(1)
    w_out = send(wd_ref, wd.at[BLOCK:, :MODEL_WIDTH], cssem.at[0], crsem.at[0], peer)
    a_out = send(al_ref, wd.at[BLOCK:, MODEL_WIDTH:], cssem.at[1], crsem.at[1], peer)

    def turn_columns(i, carry):
        start = i * 768
        both = wraw[:, :, pl.ds(pl.multiple_of(start, 768), 768)].reshape(896, 768).T
        for s in range(2):
            row = lax.broadcasted_iota(jnp.int32, (896, 448), 0)
            col = lax.broadcasted_iota(jnp.int32, (896, 448), 1)
            part_of = (row == 2 * col + s).astype(BF16)
            turned = jnp.dot(both, part_of, preferred_element_type=F32).astype(BF16)
            for g in range(48):
                n = start + 16 * g
                at = (n // BLOCK) * PAIR + s * BLOCK + lax.rem(n, BLOCK)
                wt[pl.ds(pl.multiple_of(at, 16), 16), :] = turned[16 * g:16 * g + 16]
        return carry

    load_w.wait()
    lax.fori_loop(0, 3, turn_columns, 0)
    load_res.wait()
    load_wo.wait()

    row = lax.broadcasted_iota(jnp.int32, (128, 512), 0)
    col = lax.broadcasted_iota(jnp.int32, (128, 512), 1)
    f = x_me * 2 + c
    chosen = (col == (row // 8) * 32 + f * 4 + lax.rem(row, 4)).astype(BF16)
    stream = lax.dot_general(chosen, res[...], NT, preferred_element_type=F32)

    eighth = lax.rem(lax.broadcasted_iota(jnp.int32, (HALF, 448), 0), 16) // 2
    pairs = []
    for t in range(2):
        for copy in far[t]:
            copy.wait_recv()
        projected = jnp.zeros((HALF, 448), F32)
        for q in range(8):
            r = lax.dot_general(
                ctx_all[t].reshape(HALF, 1024), wo[:, q * 1024:(q + 1) * 1024], NT,
                preferred_element_type=F32,
            )
            projected = jnp.where(eighth == q, r, projected)
        projected = projected.reshape(16, 16, 448)
        projected = projected[:, :8] + projected[:, 8:]
        projected = projected + pltpu.roll(projected, 4, 1)
        pairs.append((projected + pltpu.roll(projected, 2, 1)).reshape(128, 448))
    request = lax.rem(lax.broadcasted_iota(jnp.int32, (128, 448), 0), 4)
    projected = jnp.where(request < 2, pairs[0], pairs[1])
    stream = stream + projected
    normed = (stream * gain_ref[...].astype(F32).reshape(1, 448)).astype(BF16)
    row = lax.broadcasted_iota(jnp.int32, (64, 128), 0)
    col = lax.broadcasted_iota(jnp.int32, (64, 128), 1)
    pick = (col == (row // 4) * 8 + lax.rem(row, 4)).astype(BF16)
    z[c, x_me] = jnp.dot(pick, normed, preferred_element_type=F32).astype(BF16)
    along, across = [], []
    for d in (2, 1, 3):
        view = z.at[c, x_me]
        copy = send(view, view, zsem.at[d - 1], zrsem.at[d - 1], device_at(pos, x=d))
        along.append((d, copy))
    squares = jnp.sum(stream * stream, axis=1, keepdims=True)
    row = lax.broadcasted_iota(jnp.int32, (128, 128), 0)
    col = lax.rem(lax.broadcasted_iota(jnp.int32, (128, 128), 1), 64)
    spread = jnp.where(row == (col // 4) * 8 + lax.rem(col, 4), squares, 0.0)
    sq[y_me, z_me] = jnp.broadcast_to(jnp.sum(spread, axis=0, keepdims=True), (8, 128))
    sums = []
    for n, (dy, dz) in enumerate(plane):
        view = sq.at[y_me, z_me]
        copy = send(view, view, qsem.at[n], qrsem.at[n], device_at(pos, y=dy, z=dz))
        sums.append(copy)

    for d in (0, 1, 3, 2):
        if d:
            dict(along)[d].wait_recv()
        view = z.at[c, lax.rem(x_me + 4 - d, 4)]
        copy = send(view, view, zsem.at[3 + d], zrsem.at[3 + d], peer)
        across.append(copy)

    order = (c, 1 - c)

    def along_first(h, d):
        return device_at(pos, y=jnp.where(h == 0, d, 0), z=jnp.where(h == 0, 0, d))

    def along_second(h, d):
        return device_at(pos, y=jnp.where(h == 0, 0, d), z=jnp.where(h == 0, d, 0))

    def compute(h, p, lo, hi):
        def body(q, carry):
            a = jnp.where(h == 0, p * 4 + q, q * 4 + p)
            lhs = wt[pl.ds(pl.multiple_of(a * PAIR, PAIR), PAIR), :]
            r = lax.dot_general(
                lhs, z[h].reshape(HALF, 448), NT, preferred_element_type=F32
            ).astype(BF16)
            part[h, 0, p, q] = r[:, :128]
            part[h, 1, p, q] = r[:, 128:]
            return carry

        lax.fori_loop(lo, hi, body, 0)

    me1 = [jnp.where(h == 0, y_me, z_me) for h in order]
    me2 = [jnp.where(h == 0, z_me, y_me) for h in order]
    step = [[lax.rem(me1[n] + d, 4) for d in range(4)] for n in range(2)]
    one = [[[None] * 2 for _ in range(2)] for _ in range(2)]
    two = [[[None] * 2 for _ in range(2)] for _ in range(2)]
    three = [[[None] * 3 for _ in range(2)] for _ in range(2)]
    for n, h in enumerate(order):
        if n == 1:
            for copy in across:
                copy.wait_recv()
        for side in range(2):
            compute(h, step[n][2], 2 * side, 2 * side + 2)
            for t in range(2):
                one[n][t][side] = send(
                    part.at[h, t, step[n][2], 2 * side:2 * side + 2], got_a.at[h, t, side],
                    ssem.at[h, t, side], rsem.at[h, t, side],
                    along_first(h, 1 if side == 0 else 3),
                )
    for n, h in enumerate(order):
        compute(h, step[n][1], 0, 4)
        compute(h, step[n][3], 0, 4)
    for t in range(2):
        for n, h in enumerate(order):
            for side in range(2):
                to = 1 if side == 0 else 3
                p = step[n][to]
                one[n][t][side].wait_recv()

                def join(i, carry, h=h, t=t, side=side, p=p):
                    q = 2 * side + i
                    part[h, t, p, q] = (
                        part[h, t, p, q].astype(F32) + got_a[h, t, side, i].astype(F32)
                    ).astype(BF16)
                    return carry

                lax.fori_loop(0, 2, join, 0)
                two[n][t][side] = send(
                    part.at[h, t, p], got_b.at[h, t, side],
                    ssem.at[h, t, 2 + side], rsem.at[h, t, 2 + side], along_first(h, to),
                )
    for n, h in enumerate(order):
        compute(h, step[n][0], 0, 4)
    for copy in sums:
        copy.wait_recv()
    squares = jnp.sum(sq[...].reshape(16, 8, 128), axis=0)
    iv[c, x_me] = lax.rsqrt(squares / MODEL_WIDTH + 1e-06)
    scales = []
    for n, (dx, dc) in enumerate(line):
        view = iv.at[c, x_me]
        scales.append(send(view, view, isem.at[n], irsem.at[n], device_at(pos, x=dx, c=dc)))
    for t in range(2):
        for n, h in enumerate(order):
            for side in range(2):
                two[n][t][side].wait_recv()
            for d in (2, 1, 3):
                q = lax.rem(me2[n] + d, 4)
                summed[h, t, d - 1] = (
                    part[h, t, step[n][0], q].astype(F32) + got_b[h, t, 0, q].astype(F32)
                    + got_b[h, t, 1, q].astype(F32)
                ).astype(BF16)
                three[n][t][d - 1] = send(
                    summed.at[h, t, d - 1], got_c.at[h, t, d - 1],
                    ssem.at[h, t, 3 + d], rsem.at[h, t, 3 + d], along_second(h, d),
                )
    for copy in scales:
        copy.wait_recv()
    left = lax.broadcasted_iota(jnp.int32, (1, 128), 1) < 64
    h_out = [None, None]
    for t in range(2):
        for n, h in ((1, 1 - c), (0, c)):
            inverse = jnp.where(left, iv[h, 2 * t, :1], iv[h, 2 * t + 1, :1])
            for d in range(3):
                three[n][t][d].wait_recv()
            p, q = step[n][0], me2[n]
            both = (
                part[h, t, p, q].astype(F32)
                + got_b[h, t, 0, q].astype(F32) + got_b[h, t, 1, q].astype(F32)
                + got_c[h, t, 0].astype(F32) + got_c[h, t, 1].astype(F32)
                + got_c[h, t, 2].astype(F32)
            ) * inverse
            gate, lift = both[:BLOCK], both[BLOCK:]
            hidden = (gate / (1.0 + jnp.exp(-gate)) * lift).astype(BF16)
            if n == 1:
                hid[t] = hidden
                h_out[t] = send(
                    hid.at[t], hb.at[BLOCK:, t * 128:(t + 1) * 128],
                    cssem.at[2 + t], crsem.at[2 + t], peer,
                )
            else:
                hb[:BLOCK, t * 128:(t + 1) * 128] = hidden

    for copy in (w_out, a_out, h_out[0], h_out[1]):
        copy.wait_recv()
    load_wd.wait()
    load_al.wait()

    row = lax.broadcasted_iota(jnp.int32, (HALF, HALF), 0)
    col = lax.broadcasted_iota(jnp.int32, (HALF, HALF), 1)
    place = {"x": 64, "y": 16, "z": 4}
    for k, axes in enumerate(FLOWS):
        source = lax.rem(row, 4)
        for n, axis in enumerate(axes):
            source = source + lax.rem(row // (64, 16, 4)[n], 4) * place[axis]
        turn = (source == col).astype(BF16)
        ht[k] = lax.dot_general(turn, hb[...], NT, preferred_element_type=F32).astype(BF16)

    out1 = [[[None] * 2 for _ in CHUNKS] for _ in FLOWS]
    outb = [[[None] * 2 for _ in CHUNKS] for _ in FLOWS]
    out2 = [[[None] * 3 for _ in CHUNKS] for _ in FLOWS]
    out3 = [[None] * 3 for _ in FLOWS]

    def rows_at(k, d):
        b = lax.rem(pos[FLOWS[k][0]] + d, 4)
        return pl.ds(pl.multiple_of(b * 64, 64), 64)

    for t, (start, middle, stop) in enumerate(CHUNKS):
        for k, axes in enumerate(FLOWS):
            rows1[k, :, start:stop] = jnp.dot(
                ht[k], wd[:, k * FLOW + start:k * FLOW + stop], preferred_element_type=F32
            ).astype(BF16)
            for side, cols in enumerate((slice(start, middle), slice(middle, stop))):
                out1[k][t][side] = send(
                    rows1.at[k, rows_at(k, 2), cols], got1.at[k, :, cols],
                    essem.at[k, t, side], ersem.at[k, t, side],
                    device_at(pos, **{axes[0]: 1 if side == 0 else 3}),
                )
    for t, (start, middle, stop) in enumerate(CHUNKS):
        for k, axes in enumerate(FLOWS):
            for side, cols in enumerate((slice(start, middle), slice(middle, stop))):
                to = 1 if side == 0 else 3
                out1[k][t][side].wait_recv()
                rows1[k, rows_at(k, to), cols] = (
                    rows1[k, rows_at(k, to), cols].astype(F32) + got1[k, :, cols].astype(F32)
                ).astype(BF16)
                outb[k][t][side] = send(
                    rows1.at[k, rows_at(k, to), start:stop], gotb.at[k, side, :, start:stop],
                    essem.at[k, t, 2 + side], ersem.at[k, t, 2 + side],
                    device_at(pos, **{axes[0]: to}),
                )
    for t, (start, middle, stop) in enumerate(CHUNKS):
        for k, axes in enumerate(FLOWS):
            for side in range(2):
                outb[k][t][side].wait_recv()
            mine = pos[axes[0]] * 64
            for i in range(4):
                at = pl.multiple_of(mine + i * 16, 16)
                here = slice(i * 16, (i + 1) * 16)
                rows2[k, i, :, start:stop] = (
                    rows1[k, pl.ds(at, 16), start:stop].astype(F32)
                    + gotb[k, 0, here, start:stop].astype(F32)
                    + gotb[k, 1, here, start:stop].astype(F32)
                ).astype(BF16)
            for d in (2, 1, 3):
                b = lax.rem(pos[axes[1]] + d, 4)
                out2[k][t][d - 1] = send(
                    rows2.at[k, b, :, start:stop], got2.at[k, d - 1, :, start:stop],
                    essem.at[k, t, 3 + d], ersem.at[k, t, 3 + d],
                    device_at(pos, **{axes[1]: d}),
                )
    wide[:, FLOW:] = jnp.zeros((16, 4 * PIECE - FLOW), F32)
    for k, axes in enumerate(FLOWS):
        for t in range(len(CHUNKS)):
            for d in range(3):
                out2[k][t][d].wait_recv()
        r = rows2[k, pos[axes[1]]].astype(F32)
        for d in range(3):
            r = r + got2[k, d].astype(F32)
        wide[:, :FLOW] = r
        for to in range(4):
            rows3[k, to] = jnp.concatenate(
                [wide[4 * to:4 * to + 4, n * PIECE:(n + 1) * PIECE] for n in range(4)], axis=0
            ).astype(BF16)
        for d in (2, 1, 3):
            b = lax.rem(pos[axes[2]] + d, 4)
            out3[k][d - 1] = send(
                rows3.at[k, b], got3.at[k, d - 1],
                fssem.at[k, d - 1], frsem.at[k, d - 1], device_at(pos, **{axes[2]: d}),
            )
    acc[...] = jnp.zeros(acc.shape, F32)
    for k, axes in enumerate(FLOWS):
        for d in range(3):
            out3[k][d].wait_recv()
        r = rows3[k, pos[axes[2]]].astype(F32)
        for d in range(3):
            r = r + got3[k, d].astype(F32)
        for n in range(4):
            width = min(PIECE, FLOW - n * PIECE)
            start = k * FLOW + n * PIECE
            acc[0:4, start:start + width] = r[4 * n:4 * n + 4, :width]

    low = acc[:, MODEL_WIDTH:]
    who = lax.broadcasted_iota(jnp.int32, low.shape, 0)
    owner = lax.broadcasted_iota(jnp.int32, low.shape, 1) // ADAPTER_RANK
    tenant = jnp.where(
        who == 0, tenant_ref[0],
        jnp.where(who == 1, tenant_ref[1], jnp.where(who == 2, tenant_ref[2], tenant_ref[3])),
    )
    load_up.wait()
    picked = jnp.where(owner == tenant, low, 0.0).astype(BF16)
    for n in range(7):
        cols = slice(n * 1024, (n + 1) * 1024)
        r = acc[:, cols] + jnp.dot(picked, up[:, cols], preferred_element_type=F32)
        out_ref[:, cols] = r[0:4]

    for copy in sent:
        copy.wait_send()


def feed(q, key, value, length, wo, res, gain, w, wd, al, up, tenant):
    vmem = pl.BlockSpec(memory_space=pltpu.VMEM)
    hbm = pl.BlockSpec(memory_space=pl.ANY)
    smem = pl.BlockSpec(memory_space=pltpu.SMEM)
    dma = pltpu.SemaphoreType.DMA
    return pl.pallas_call(
        feed_kernel,
        out_shape=jax.ShapeDtypeStruct((4, MODEL_WIDTH), F32),
        in_specs=[vmem, hbm, hbm, smem, hbm, hbm, vmem, hbm, hbm, hbm, hbm, smem],
        out_specs=vmem,
        scratch_shapes=[
            pltpu.VMEM((4, CACHE, HD), BF16),
            pltpu.VMEM((4, CACHE, HD), BF16),
            pltpu.VMEM((2 * HQ, HD), BF16),
            pltpu.VMEM((2, 4, 4, 16, 1024), BF16),
            pltpu.VMEM((448, 8192), BF16),
            pltpu.VMEM((448, 512), BF16),
            pltpu.VMEM((2, 4, 64, 448), BF16),
            pltpu.VMEM((4, 4, 8, 128), F32),
            pltpu.VMEM((2, 4, 8, 128), F32),
            pltpu.VMEM((448, 2, 2304), BF16),
            pltpu.VMEM((128, MODEL_WIDTH), BF16),
            pltpu.VMEM((16 * PAIR, 448), BF16),
            pltpu.VMEM((2, 2, 4, 4, PAIR, 128), BF16),
            pltpu.VMEM((2, 2, 2, 2, PAIR, 128), BF16),
            pltpu.VMEM((2, 2, 2, 4, PAIR, 128), BF16),
            pltpu.VMEM((2, 2, 3, PAIR, 128), BF16),
            pltpu.VMEM((2, 2, 3, PAIR, 128), BF16),
            pltpu.VMEM((2, BLOCK, 128), BF16),
            pltpu.VMEM((PAIR, WIDE), BF16),
            pltpu.VMEM((PAIR, HALF), BF16),
            pltpu.VMEM((3, HALF, PAIR), BF16),
            pltpu.VMEM((3, HALF, FLOW), BF16),
            pltpu.VMEM((3, 64, FLOW), BF16),
            pltpu.VMEM((3, 2, 64, FLOW), BF16),
            pltpu.VMEM((3, 4, 16, FLOW), BF16),
            pltpu.VMEM((3, 3, 16, FLOW), BF16),
            pltpu.VMEM((16, 4 * PIECE), F32),
            pltpu.VMEM((3, 4, 16, PIECE), BF16),
            pltpu.VMEM((3, 3, 16, PIECE), BF16),
            pltpu.VMEM((8, WIDE), F32),
            dma((2, 4)), dma((6,)), dma((2, 2, 6)), dma((2, 2, 6)), dma((15,)), dma((15,)),
            dma((7,)), dma((7,)), dma((7,)), dma((7,)),
            dma((2, 2, 7)), dma((2, 2, 7)), dma((4,)), dma((4,)),
            dma((3, 2, 7)), dma((3, 2, 7)), dma((3, 3)), dma((3, 3)),
        ],
        compiler_params=pltpu.CompilerParams(
            collective_id=1, has_side_effects=True, vmem_limit_bytes=58 << 20
        ),
    )(q, key, value, length, wo, res, gain, w, wd, al, up, tenant)


def local(
    query,
    cached_key_rows,
    cached_value_rows,
    request_cache_length,
    request_tenant_index,
    residual,
    feedforward_norm_gain,
    attention_output_weight,
    gate_up_weight,
    down_projection_weight,
    adapter_down_maps,
    adapter_up_maps,
):
    result = feed(
        query.reshape(4, HQ, HD).transpose(1, 0, 2),
        cached_key_rows, cached_value_rows, request_cache_length,
        attention_output_weight.T, residual.T,
        feedforward_norm_gain, gate_up_weight,
        down_projection_weight.reshape(BLOCK, MODEL_WIDTH),
        adapter_down_maps.reshape(BLOCK, TENANT_COUNT * ADAPTER_RANK),
        adapter_up_maps, request_tenant_index,
    )
    return result.astype(BF16)


def solution(mesh):
    in_specs = (
        P(("attn", "ffn"), None),
        P(("attn", "ffn"), None, None),
        P(("attn", "ffn"), None, None),
        P(("attn", "ffn")),
        P(("attn", "ffn")),
        P(None, "attn"),
        P("attn"),
        P(None, "attn"),
        P("attn", None, "ffn"),
        P("ffn", "attn", None, None),
        P("ffn", "attn", None, None),
        P(),
    )
    out_specs = P(("attn", "ffn"), None)
    return jax.shard_map(local, mesh=mesh, in_specs=in_specs, out_specs=out_specs, check_vma=False)
```

```python
import functools

import jax
import jax.numpy as jnp
from jax import lax
from jax.experimental import pallas as pl
from jax.experimental.pallas import tpu as pltpu
from jax.sharding import PartitionSpec as P

MODEL_WIDTH = 7168
HQ = 32
HD = 256
CACHE = 2048
TENANT_COUNT = 8
ADAPTER_RANK = 16
MESH = pl.DeviceIdType.MESH
BLOCK = 144
PAIR = 2 * BLOCK
HALF = 256
WIDE = MODEL_WIDTH + TENANT_COUNT * ADAPTER_RANK
FLOW = WIDE // 3
PIECE = 640
NT = (((1,), (1,)), ((), ()))
F32 = jnp.float32
BF16 = jnp.bfloat16


def position():
    a = lax.axis_index("attn")
    f = lax.axis_index("ffn")
    return {"y": a // 4, "z": lax.rem(a, 4), "x": f // 2, "c": lax.rem(f, 2)}


def device_at(pos, **steps):
    y = lax.rem(pos["y"] + steps.get("y", 0), 4)
    z = lax.rem(pos["z"] + steps.get("z", 0), 4)
    x = lax.rem(pos["x"] + steps.get("x", 0), 4)
    c = lax.rem(pos["c"] + steps.get("c", 0), 2)
    return (y * 4 + z, x * 2 + c)


def send_to(sent, src, dst, send_sem, recv_sem, where):
    copy = pltpu.make_async_remote_copy(
        src_ref=src, dst_ref=dst, send_sem=send_sem, recv_sem=recv_sem,
        device_id=where, device_id_type=MESH,
    )
    copy.start()
    sent.append(copy)
    return copy


SPLIT = 1280
FLOWS = (("x", "y", "z"), ("y", "z", "x"), ("z", "x", "y"))


def feed_kernel(
    q_ref, key_ref, value_ref, length_ref,
    wo_ref, res_ref, gain_ref, w_ref, wd_ref, al_ref, up_ref, tenant_ref, out_ref,
    keys, values, heads, ctx_all, wo, res, z, sq, iv, wraw, up,
    wt, part, got_a, got_b, summed, got_c, hid, wd, hb,
    rows1, got1, gotb, early, rows2, got2, wide, rows3, got3, acc,
    kvsem, lsem, asem, arsem, qsem, qrsem, zsem, zrsem, isem, irsem,
    ssem, rsem, cssem, crsem, essem, ersem, gssem, grsem, fssem, frsem,
):
    pos = position()
    sent = []
    send = functools.partial(send_to, sent)
    c = pos["c"]
    y_me, z_me, x_me = pos["y"], pos["z"], pos["x"]
    peer = device_at(pos, c=1)
    plane = [(dy, dz) for dy in range(4) for dz in range(4) if dy or dz]
    line = [(dx, dc) for dx in range(4) for dc in range(2) if dx or dc]
    partners = [device_at(pos, y=dy, z=dz) for dy, dz in plane]
    partners += [device_at(pos, x=dx, c=dc) for dx, dc in line]
    barrier = pltpu.get_barrier_semaphore()
    for partner in partners:
        pl.semaphore_signal(barrier, inc=1, device_id=partner, device_id_type=MESH)

    streams = [
        (
            pltpu.make_async_copy(key_ref.at[j], keys.at[j], kvsem.at[0, j]),
            pltpu.make_async_copy(value_ref.at[j], values.at[j], kvsem.at[1, j]),
        )
        for j in range(4)
    ]
    for j in range(2):
        for copy in streams[j]:
            copy.start()
    loads = [
        pltpu.make_async_copy(w_ref, wraw, lsem.at[0]),
        pltpu.make_async_copy(wo_ref, wo, lsem.at[1]),
        pltpu.make_async_copy(res_ref, res, lsem.at[2]),
        pltpu.make_async_copy(wd_ref, wd.at[:BLOCK, :MODEL_WIDTH], lsem.at[3]),
        pltpu.make_async_copy(al_ref, wd.at[:BLOCK, MODEL_WIDTH:], lsem.at[4]),
        pltpu.make_async_copy(up_ref, up, lsem.at[5]),
    ]
    load_w, load_wo, load_res, load_wd, load_al, load_up = loads

    row = lax.broadcasted_iota(jnp.int32, (128, 128), 0)
    col = lax.broadcasted_iota(jnp.int32, (128, 128), 1)
    turn = (col == lax.rem(row, HQ) * 4 + row // HQ).astype(BF16)
    queries = jnp.dot(
        turn, q_ref[...].reshape(128, HD), preferred_element_type=F32
    ).astype(BF16)
    slots = lax.broadcasted_iota(jnp.int32, (HQ, CACHE), 1)
    near = [[], []]
    far = [[], []]

    def attend(j):
        streams[j][0].wait()
        if j < 2:
            streams[j + 2][0].start()
        scores = lax.dot_general(
            queries[j * HQ:(j + 1) * HQ], keys[j], NT, preferred_element_type=F32
        ) * HD ** (-0.5)
        scores = jnp.where(slots < length_ref[j], scores, -jnp.inf)
        expo = jnp.exp(scores - jnp.max(scores, axis=1, keepdims=True))
        probs = (expo * (1.0 / jnp.sum(expo, axis=1, keepdims=True))).astype(BF16)
        streams[j][1].wait()
        if j < 2:
            streams[j + 2][1].start()
        return jnp.dot(probs, values[j], preferred_element_type=F32).astype(BF16)

    def place_pair(t, first, second):
        heads[:HQ, :] = first
        heads[HQ:, :] = second
        row = lax.broadcasted_iota(jnp.int32, (64, 64), 0)
        col = lax.broadcasted_iota(jnp.int32, (64, 64), 1)
        source = lax.rem(row, 2) * HQ + (lax.rem(row, 16) // 2) * 4 + row // 16
        turn = (col == source).astype(BF16)
        context = jnp.dot(turn, heads[...], preferred_element_type=F32).astype(BF16)
        for n in range(4):
            ctx_all[t, y_me, z_me, :, n * HD:(n + 1) * HD] = context[n * 16:(n + 1) * 16]

    def send_near(t):
        for d in (2, 1, 3):
            for h, axis in enumerate(("y", "z")):
                view = ctx_all.at[t, y_me, z_me, :, h * 512:(h + 1) * 512]
                near[t].append(send(
                    view, view, asem.at[t, h, d - 1], arsem.at[t, h, d - 1],
                    device_at(pos, **{axis: d}),
                ))

    def send_far(t):
        for copy in near[t]:
            copy.wait_recv()
        for d in (2, 1, 3):
            for h, axis in enumerate(("z", "y")):
                if h == 0:
                    view = ctx_all.at[t, :, z_me, :, :512]
                else:
                    view = ctx_all.at[t, y_me, :, :, 512:]
                far[t].append(send(
                    view, view, asem.at[t, h, 2 + d], arsem.at[t, h, 2 + d],
                    device_at(pos, **{axis: d}),
                ))

    place_pair(0, attend(0), attend(1))
    pl.semaphore_wait(barrier, len(partners))
    send_near(0)
    third = attend(2)
    for copy in loads:
        copy.start()
    send_far(0)
    place_pair(1, third, attend(3))
    send_near(1)
    send_far(1)
    w_out = send(wd_ref, wd.at[BLOCK:, :MODEL_WIDTH], cssem.at[0], crsem.at[0], peer)
    a_out = send(al_ref, wd.at[BLOCK:, MODEL_WIDTH:], cssem.at[1], crsem.at[1], peer)

    row = lax.broadcasted_iota(jnp.int32, (256, 256), 0)
    col = lax.broadcasted_iota(jnp.int32, (256, 256), 1)
    split = (row == 2 * lax.rem(col, 128) + col // 128).astype(BF16)

    def turn_columns(i):
        start = i * 768
        for group in range(4):
            count = min(128, 448 - group * 128)
            lanes = slice(group * 128, group * 128 + count)
            both = wraw[lanes, :, start:start + 768].reshape(2 * count, 768).T
            turned = jnp.dot(
                both, split[:2 * count], preferred_element_type=F32
            ).astype(BF16)
            for s in range(2):
                for g in range(48):
                    n = start + 16 * g
                    at = (n // BLOCK) * PAIR + s * BLOCK + n % BLOCK
                    wt[at:at + 16, lanes] = turned[
                        16 * g:16 * g + 16, s * 128:s * 128 + count
                    ]

    load_w.wait()
    turn_columns(0)
    load_res.wait()
    load_wo.wait()

    row = lax.broadcasted_iota(jnp.int32, (128, 512), 0)
    col = lax.broadcasted_iota(jnp.int32, (128, 512), 1)
    f = x_me * 2 + c
    chosen = (col == (row // 8) * 32 + f * 4 + lax.rem(row, 4)).astype(BF16)
    stream = lax.dot_general(chosen, res[...], NT, preferred_element_type=F32)

    eighth = lax.rem(lax.broadcasted_iota(jnp.int32, (HALF, 448), 0), 16) // 2
    pairs = []
    for t in range(2):
        for copy in far[t]:
            copy.wait_recv()
        projected = jnp.zeros((HALF, 448), F32)
        for q in range(8):
            r = lax.dot_general(
                ctx_all[t].reshape(HALF, 1024), wo[:, q * 1024:(q + 1) * 1024], NT,
                preferred_element_type=F32,
            )
            projected = jnp.where(eighth == q, r, projected)
        projected = projected.reshape(16, 16, 448)
        projected = projected[:, :8] + projected[:, 8:]
        projected = projected + pltpu.roll(projected, 4, 1)
        pairs.append((projected + pltpu.roll(projected, 2, 1)).reshape(128, 448))
        if t == 0:
            turn_columns(1)
    request = lax.rem(lax.broadcasted_iota(jnp.int32, (128, 448), 0), 4)
    projected = jnp.where(request < 2, pairs[0], pairs[1])
    stream = stream + projected
    normed = (stream * gain_ref[...].astype(F32).reshape(1, 448)).astype(BF16)
    row = lax.broadcasted_iota(jnp.int32, (64, 128), 0)
    col = lax.broadcasted_iota(jnp.int32, (64, 128), 1)
    source = (lax.rem(row, 32) // 2) * 8 + 2 * (row // 32) + lax.rem(row, 2)
    picked = jnp.dot((col == source).astype(BF16), normed, preferred_element_type=F32)
    z[c, :, x_me] = picked.astype(BF16).reshape(2, 32, 448)
    along, across = [], []
    for d in (2, 1, 3):
        view = z.at[c, :, x_me]
        copy = send(view, view, zsem.at[d - 1], zrsem.at[d - 1], device_at(pos, x=d))
        along.append((d, copy))
    view = z.at[c, :, x_me]
    across.append(send(view, view, zsem.at[3], zrsem.at[3], peer))
    squares = jnp.sum(stream * stream, axis=1, keepdims=True)
    row = lax.broadcasted_iota(jnp.int32, (128, 128), 0)
    col = lax.rem(lax.broadcasted_iota(jnp.int32, (128, 128), 1), 32)
    lanes = []
    for t in range(2):
        spread = jnp.where(row == (col // 2) * 8 + 2 * t + lax.rem(col, 2), squares, 0.0)
        lanes.append(jnp.sum(spread, axis=0, keepdims=True))
    even = lax.rem(lax.broadcasted_iota(jnp.int32, (8, 128), 0), 2) == 0
    sq[y_me, z_me] = jnp.where(even, lanes[0], lanes[1])
    sums = []
    for n, (dy, dz) in enumerate(plane):
        view = sq.at[y_me, z_me]
        copy = send(view, view, qsem.at[n], qrsem.at[n], device_at(pos, y=dy, z=dz))
        sums.append(copy)

    turn_columns(2)
    for d in (1, 3, 2):
        dict(along)[d].wait_recv()
        view = z.at[c, :, lax.rem(x_me + 4 - d, 4)]
        copy = send(view, view, zsem.at[3 + d], zrsem.at[3 + d], peer)
        across.append(copy)

    order = (c, 1 - c)

    def along_first(h, d):
        return device_at(pos, y=jnp.where(h == 0, d, 0), z=jnp.where(h == 0, 0, d))

    def along_second(h, d):
        return device_at(pos, y=jnp.where(h == 0, 0, d), z=jnp.where(h == 0, d, 0))

    def compute(h, p, lo, hi):
        def body(q, carry):
            a = jnp.where(h == 0, p * 4 + q, q * 4 + p)
            lhs = wt[pl.ds(pl.multiple_of(a * PAIR, PAIR), PAIR), :]
            r = lax.dot_general(
                lhs, z[h].reshape(HALF, 448), NT, preferred_element_type=F32
            ).astype(BF16)
            part[h, 0, p, q] = r[:, :128]
            part[h, 1, p, q] = r[:, 128:]
            return carry

        lax.fori_loop(lo, hi, body, 0)

    me1 = [jnp.where(h == 0, y_me, z_me) for h in order]
    me2 = [jnp.where(h == 0, z_me, y_me) for h in order]
    step = [[lax.rem(me1[n] + d, 4) for d in range(4)] for n in range(2)]
    one = [[[None] * 2 for _ in range(2)] for _ in range(2)]
    two = [[[None] * 2 for _ in range(2)] for _ in range(2)]
    three = [[[None] * 3 for _ in range(2)] for _ in range(2)]
    for n, h in enumerate(order):
        if n == 1:
            for copy in across:
                copy.wait_recv()
        for side in range(2):
            compute(h, step[n][2], 2 * side, 2 * side + 2)
            for t in range(2):
                one[n][t][side] = send(
                    part.at[h, t, step[n][2], 2 * side:2 * side + 2], got_a.at[h, t, side],
                    ssem.at[h, t, side], rsem.at[h, t, side],
                    along_first(h, 1 if side == 0 else 3),
                )
    for n, h in enumerate(order):
        compute(h, step[n][1], 0, 4)
        compute(h, step[n][3], 0, 4)
    for t in range(2):
        for n, h in enumerate(order):
            for side in range(2):
                to = 1 if side == 0 else 3
                p = step[n][to]
                one[n][t][side].wait_recv()

                def join(i, carry, h=h, t=t, side=side, p=p):
                    q = 2 * side + i
                    part[h, t, p, q] = (
                        part[h, t, p, q].astype(F32) + got_a[h, t, side, i].astype(F32)
                    ).astype(BF16)
                    return carry

                lax.fori_loop(0, 2, join, 0)
                two[n][t][side] = send(
                    part.at[h, t, p], got_b.at[h, t, side],
                    ssem.at[h, t, 2 + side], rsem.at[h, t, 2 + side], along_first(h, to),
                )
    for n, h in enumerate(order):
        compute(h, step[n][0], 0, 4)
    for copy in sums:
        copy.wait_recv()
    squares = jnp.sum(sq[...].reshape(16, 8, 128), axis=0)
    iv[c, x_me] = lax.rsqrt(squares / MODEL_WIDTH + 1e-06)
    scales = []
    for n, (dx, dc) in enumerate(line):
        view = iv.at[c, x_me]
        scales.append(send(view, view, isem.at[n], irsem.at[n], device_at(pos, x=dx, c=dc)))
    def second_axis(t):
        for n, h in enumerate(order):
            for side in range(2):
                two[n][t][side].wait_recv()
            for d in (2, 1, 3):
                q = lax.rem(me2[n] + d, 4)
                summed[h, t, d - 1] = (
                    part[h, t, step[n][0], q].astype(F32) + got_b[h, t, 0, q].astype(F32)
                    + got_b[h, t, 1, q].astype(F32)
                ).astype(BF16)
                three[n][t][d - 1] = send(
                    summed.at[h, t, d - 1], got_c.at[h, t, d - 1],
                    ssem.at[h, t, 3 + d], rsem.at[h, t, 3 + d], along_second(h, d),
                )

    lane = lax.broadcasted_iota(jnp.int32, (1, 128), 1) // 32
    h_out = [None, None]

    def activate(t):
        for n, h in ((1, 1 - c), (0, c)):
            inverse = iv[h, 0, t:t + 1]
            for x in range(1, 4):
                inverse = jnp.where(lane == x, iv[h, x, t:t + 1], inverse)
            for d in range(3):
                three[n][t][d].wait_recv()
            p, q = step[n][0], me2[n]
            both = (
                part[h, t, p, q].astype(F32)
                + got_b[h, t, 0, q].astype(F32) + got_b[h, t, 1, q].astype(F32)
                + got_c[h, t, 0].astype(F32) + got_c[h, t, 1].astype(F32)
                + got_c[h, t, 2].astype(F32)
            ) * inverse
            gate, lift = both[:BLOCK], both[BLOCK:]
            hidden = (gate / (1.0 + jnp.exp(-gate)) * lift).astype(BF16)
            if n == 1:
                hid[t] = hidden
                h_out[t] = send(
                    hid.at[t], hb.at[t, BLOCK:], cssem.at[2 + t], crsem.at[2 + t], peer
                )
            else:
                hb[t, :BLOCK] = hidden

    row = lax.broadcasted_iota(jnp.int32, (128, 128), 0)
    col = lax.broadcasted_iota(jnp.int32, (128, 128), 1)
    place = {"x": 32, "y": 8, "z": 2}
    turns = []
    for axes in FLOWS:
        source = lax.rem(row, 2)
        for n, axis in enumerate(axes):
            source = source + lax.rem(row // (32, 8, 2)[n], 4) * place[axis]
        turns.append((source == col).astype(BF16))

    out1 = [[[None] * 2 for _ in range(2)] for _ in FLOWS]
    outb = [[[None] * 2 for _ in range(2)] for _ in FLOWS]
    out2 = [[None] * 3 for _ in FLOWS]
    out3 = [[None] * 3 for _ in FLOWS]
    sides = (slice(0, SPLIT), slice(SPLIT, FLOW))

    def rows_at(k, d):
        b = lax.rem(pos[FLOWS[k][0]] + d, 4)
        return pl.ds(pl.multiple_of(b * 32, 32), 32)

    def project_down(t):
        h_out[t].wait_recv()
        for k, axes in enumerate(FLOWS):
            ht = lax.dot_general(turns[k], hb[t], NT, preferred_element_type=F32).astype(BF16)
            rows1[k, t] = jnp.dot(
                ht, wd[:, k * FLOW:(k + 1) * FLOW], preferred_element_type=F32
            ).astype(BF16)
            for side, cols in enumerate(sides):
                out1[k][t][side] = send(
                    rows1.at[k, t, rows_at(k, 2), cols], got1.at[k, t, :, cols],
                    essem.at[k, t, side], ersem.at[k, t, side],
                    device_at(pos, **{axes[0]: 1 if side == 0 else 3}),
                )

    def join_down(t):
        for k, axes in enumerate(FLOWS):
            for side, cols in enumerate(sides):
                to = 1 if side == 0 else 3
                out1[k][t][side].wait_recv()
                rows1[k, t, rows_at(k, to), cols] = (
                    rows1[k, t, rows_at(k, to), cols].astype(F32)
                    + got1[k, t, :, cols].astype(F32)
                ).astype(BF16)
                outb[k][t][side] = send(
                    rows1.at[k, t, rows_at(k, to)], gotb.at[k, t, side],
                    essem.at[k, t, 2 + side], ersem.at[k, t, 2 + side],
                    device_at(pos, **{axes[0]: to}),
                )

    def own_rows(k, t):
        for side in range(2):
            outb[k][t][side].wait_recv()
        return (
            rows1[k, t, rows_at(k, 0)].astype(F32)
            + gotb[k, t, 0].astype(F32) + gotb[k, t, 1].astype(F32)
        )

    second_axis(0)
    for copy in scales:
        copy.wait_recv()
    activate(0)
    second_axis(1)
    for copy in (w_out, a_out):
        copy.wait_recv()
    load_wd.wait()
    load_al.wait()
    project_down(0)
    activate(1)
    join_down(0)
    project_down(1)
    for k in range(3):
        early[k] = own_rows(k, 0)
    join_down(1)
    for k, axes in enumerate(FLOWS):
        late = own_rows(k, 1)
        for i in range(4):
            rows2[k, i] = jnp.concatenate(
                [early[k, 8 * i:8 * i + 8], late[8 * i:8 * i + 8]], axis=0
            ).astype(BF16)
        for d in (2, 1, 3):
            b = lax.rem(pos[axes[1]] + d, 4)
            out2[k][d - 1] = send(
                rows2.at[k, b], got2.at[k, d - 1], gssem.at[k, d - 1], grsem.at[k, d - 1],
                device_at(pos, **{axes[1]: d}),
            )
    wide[:, FLOW:] = jnp.zeros((16, 4 * PIECE - FLOW), F32)
    for k, axes in enumerate(FLOWS):
        for d in range(3):
            out2[k][d].wait_recv()
        r = rows2[k, pos[axes[1]]].astype(F32)
        for d in range(3):
            r = r + got2[k, d].astype(F32)
        for to in range(4):
            wide[4 * to:4 * to + 2, :FLOW] = r[2 * to:2 * to + 2]
            wide[4 * to + 2:4 * to + 4, :FLOW] = r[8 + 2 * to:8 + 2 * to + 2]
        for to in range(4):
            rows3[k, to] = jnp.concatenate(
                [wide[4 * to:4 * to + 4, n * PIECE:(n + 1) * PIECE] for n in range(4)], axis=0
            ).astype(BF16)
        for d in (2, 1, 3):
            b = lax.rem(pos[axes[2]] + d, 4)
            out3[k][d - 1] = send(
                rows3.at[k, b], got3.at[k, d - 1],
                fssem.at[k, d - 1], frsem.at[k, d - 1], device_at(pos, **{axes[2]: d}),
            )
    acc[...] = jnp.zeros(acc.shape, F32)
    for k, axes in enumerate(FLOWS):
        for d in range(3):
            out3[k][d].wait_recv()
        r = rows3[k, pos[axes[2]]].astype(F32)
        for d in range(3):
            r = r + got3[k, d].astype(F32)
        for n in range(4):
            width = min(PIECE, FLOW - n * PIECE)
            start = k * FLOW + n * PIECE
            acc[0:4, start:start + width] = r[4 * n:4 * n + 4, :width]

    low = acc[:, MODEL_WIDTH:]
    who = lax.broadcasted_iota(jnp.int32, low.shape, 0)
    owner = lax.broadcasted_iota(jnp.int32, low.shape, 1) // ADAPTER_RANK
    tenant = jnp.where(
        who == 0, tenant_ref[0],
        jnp.where(who == 1, tenant_ref[1], jnp.where(who == 2, tenant_ref[2], tenant_ref[3])),
    )
    load_up.wait()
    picked = jnp.where(owner == tenant, low, 0.0).astype(BF16)
    for n in range(7):
        cols = slice(n * 1024, (n + 1) * 1024)
        r = acc[:, cols] + jnp.dot(picked, up[:, cols], preferred_element_type=F32)
        out_ref[:, cols] = r[0:4]

    for copy in sent:
        copy.wait_send()


def feed(q, key, value, length, wo, res, gain, w, wd, al, up, tenant):
    vmem = pl.BlockSpec(memory_space=pltpu.VMEM)
    hbm = pl.BlockSpec(memory_space=pl.ANY)
    smem = pl.BlockSpec(memory_space=pltpu.SMEM)
    dma = pltpu.SemaphoreType.DMA
    return pl.pallas_call(
        feed_kernel,
        out_shape=jax.ShapeDtypeStruct((4, MODEL_WIDTH), F32),
        in_specs=[vmem, hbm, hbm, smem, hbm, hbm, vmem, hbm, hbm, hbm, hbm, smem],
        out_specs=vmem,
        scratch_shapes=[
            pltpu.VMEM((4, CACHE, HD), BF16),
            pltpu.VMEM((4, CACHE, HD), BF16),
            pltpu.VMEM((2 * HQ, HD), BF16),
            pltpu.VMEM((2, 4, 4, 16, 1024), BF16),
            pltpu.VMEM((448, 8192), BF16),
            pltpu.VMEM((448, 512), BF16),
            pltpu.VMEM((2, 2, 4, 32, 448), BF16),
            pltpu.VMEM((4, 4, 8, 128), F32),
            pltpu.VMEM((2, 4, 8, 128), F32),
            pltpu.VMEM((448, 2, 2304), BF16),
            pltpu.VMEM((128, MODEL_WIDTH), BF16),
            pltpu.VMEM((16 * PAIR, 448), BF16),
            pltpu.VMEM((2, 2, 4, 4, PAIR, 128), BF16),
            pltpu.VMEM((2, 2, 2, 2, PAIR, 128), BF16),
            pltpu.VMEM((2, 2, 2, 4, PAIR, 128), BF16),
            pltpu.VMEM((2, 2, 3, PAIR, 128), BF16),
            pltpu.VMEM((2, 2, 3, PAIR, 128), BF16),
            pltpu.VMEM((2, BLOCK, 128), BF16),
            pltpu.VMEM((PAIR, WIDE), BF16),
            pltpu.VMEM((2, PAIR, 128), BF16),
            pltpu.VMEM((3, 2, 128, FLOW), BF16),
            pltpu.VMEM((3, 2, 32, FLOW), BF16),
            pltpu.VMEM((3, 2, 2, 32, FLOW), BF16),
            pltpu.VMEM((3, 32, FLOW), F32),
            pltpu.VMEM((3, 4, 16, FLOW), BF16),
            pltpu.VMEM((3, 3, 16, FLOW), BF16),
            pltpu.VMEM((16, 4 * PIECE), F32),
            pltpu.VMEM((3, 4, 16, PIECE), BF16),
            pltpu.VMEM((3, 3, 16, PIECE), BF16),
            pltpu.VMEM((8, WIDE), F32),
            dma((2, 4)), dma((6,)), dma((2, 2, 6)), dma((2, 2, 6)), dma((15,)), dma((15,)),
            dma((7,)), dma((7,)), dma((7,)), dma((7,)),
            dma((2, 2, 7)), dma((2, 2, 7)), dma((4,)), dma((4,)),
            dma((3, 2, 4)), dma((3, 2, 4)), dma((3, 3)), dma((3, 3)), dma((3, 3)), dma((3, 3)),
        ],
        compiler_params=pltpu.CompilerParams(
            collective_id=1, has_side_effects=True, vmem_limit_bytes=58 << 20
        ),
    )(q, key, value, length, wo, res, gain, w, wd, al, up, tenant)


def local(
    query,
    cached_key_rows,
    cached_value_rows,
    request_cache_length,
    request_tenant_index,
    residual,
    feedforward_norm_gain,
    attention_output_weight,
    gate_up_weight,
    down_projection_weight,
    adapter_down_maps,
    adapter_up_maps,
):
    result = feed(
        query.reshape(4, HQ, HD).transpose(1, 0, 2),
        cached_key_rows, cached_value_rows, request_cache_length,
        attention_output_weight.T, residual.T,
        feedforward_norm_gain, gate_up_weight,
        down_projection_weight.reshape(BLOCK, MODEL_WIDTH),
        adapter_down_maps.reshape(BLOCK, TENANT_COUNT * ADAPTER_RANK),
        adapter_up_maps, request_tenant_index,
    )
    return result.astype(BF16)


def solution(mesh):
    in_specs = (
        P(("attn", "ffn"), None),
        P(("attn", "ffn"), None, None),
        P(("attn", "ffn"), None, None),
        P(("attn", "ffn")),
        P(("attn", "ffn")),
        P(None, "attn"),
        P("attn"),
        P(None, "attn"),
        P("attn", None, "ffn"),
        P("ffn", "attn", None, None),
        P("ffn", "attn", None, None),
        P(),
    )
    out_specs = P(("attn", "ffn"), None)
    return jax.shard_map(local, mesh=mesh, in_specs=in_specs, out_specs=out_specs, check_vma=False)
```

```python
import functools

import jax
import jax.numpy as jnp
from jax import lax
from jax.experimental import pallas as pl
from jax.experimental.pallas import tpu as pltpu
from jax.sharding import PartitionSpec as P

MODEL_WIDTH = 7168
HQ = 32
HD = 256
CACHE = 2048
TENANT_COUNT = 8
ADAPTER_RANK = 16
MESH = pl.DeviceIdType.MESH
BLOCK = 144
PAIR = 2 * BLOCK
CUT = 80
ROWS = (slice(0, 2 * CUT), slice(2 * CUT, PAIR))
UNITS = (slice(0, CUT), slice(CUT, BLOCK))
PARTS = ((0, 0), (0, 1), (1, 0), (1, 1))
HALF = 256
WIDE = MODEL_WIDTH + TENANT_COUNT * ADAPTER_RANK
FLOW = WIDE // 3
PIECE = 640
NT = (((1,), (1,)), ((), ()))
F32 = jnp.float32
BF16 = jnp.bfloat16


def position():
    a = lax.axis_index("attn")
    f = lax.axis_index("ffn")
    return {"y": a // 4, "z": lax.rem(a, 4), "x": f // 2, "c": lax.rem(f, 2)}


def device_at(pos, **steps):
    y = lax.rem(pos["y"] + steps.get("y", 0), 4)
    z = lax.rem(pos["z"] + steps.get("z", 0), 4)
    x = lax.rem(pos["x"] + steps.get("x", 0), 4)
    c = lax.rem(pos["c"] + steps.get("c", 0), 2)
    return (y * 4 + z, x * 2 + c)


def send_to(sent, src, dst, send_sem, recv_sem, where):
    copy = pltpu.make_async_remote_copy(
        src_ref=src, dst_ref=dst, send_sem=send_sem, recv_sem=recv_sem,
        device_id=where, device_id_type=MESH,
    )
    copy.start()
    sent.append(copy)
    return copy


CHUNKS = ((0, 640, 1280), (1280, 1920, FLOW))
FLOWS = (("x", "y", "z"), ("y", "z", "x"), ("z", "x", "y"))


def feed_kernel(
    q_ref, key_ref, value_ref, length_ref,
    wo_ref, res_ref, gain_ref, w_ref, wd_ref, al_ref, up_ref, tenant_ref, out_ref,
    keys, values, heads, ctx_all, wo, res, z, sq, iv, wraw, up,
    wt, part, got_a, got_b, summed, got_c, hid, wd, hb, ht,
    rows1, got1, gotb, rows2, got2, wide, rows3, got3, acc,
    kvsem, lsem, asem, arsem, qsem, qrsem, zsem, zrsem, isem, irsem,
    ssem, rsem, cssem, crsem, essem, ersem, fssem, frsem,
):
    pos = position()
    sent = []
    send = functools.partial(send_to, sent)
    c = pos["c"]
    y_me, z_me, x_me = pos["y"], pos["z"], pos["x"]
    peer = device_at(pos, c=1)
    plane = [(dy, dz) for dy in range(4) for dz in range(4) if dy or dz]
    line = [(dx, dc) for dx in range(4) for dc in range(2) if dx or dc]
    partners = [device_at(pos, y=dy, z=dz) for dy, dz in plane]
    partners += [device_at(pos, x=dx, c=dc) for dx, dc in line]
    barrier = pltpu.get_barrier_semaphore()
    for partner in partners:
        pl.semaphore_signal(barrier, inc=1, device_id=partner, device_id_type=MESH)

    streams = [
        (
            pltpu.make_async_copy(key_ref.at[j], keys.at[j], kvsem.at[0, j]),
            pltpu.make_async_copy(value_ref.at[j], values.at[j], kvsem.at[1, j]),
        )
        for j in range(4)
    ]
    for j in range(2):
        for copy in streams[j]:
            copy.start()
    loads = [
        pltpu.make_async_copy(w_ref, wraw, lsem.at[0]),
        pltpu.make_async_copy(wo_ref, wo, lsem.at[1]),
        pltpu.make_async_copy(res_ref, res, lsem.at[2]),
        pltpu.make_async_copy(wd_ref, wd.at[:BLOCK, :MODEL_WIDTH], lsem.at[3]),
        pltpu.make_async_copy(al_ref, wd.at[:BLOCK, MODEL_WIDTH:], lsem.at[4]),
        pltpu.make_async_copy(up_ref, up, lsem.at[5]),
    ]
    load_w, load_wo, load_res, load_wd, load_al, load_up = loads

    row = lax.broadcasted_iota(jnp.int32, (128, 128), 0)
    col = lax.broadcasted_iota(jnp.int32, (128, 128), 1)
    turn = (col == lax.rem(row, HQ) * 4 + row // HQ).astype(BF16)
    queries = jnp.dot(
        turn, q_ref[...].reshape(128, HD), preferred_element_type=F32
    ).astype(BF16)
    slots = lax.broadcasted_iota(jnp.int32, (HQ, CACHE), 1)
    near = [[], []]
    far = [[], []]

    def attend(j):
        streams[j][0].wait()
        if j < 2:
            streams[j + 2][0].start()
        scores = lax.dot_general(
            queries[j * HQ:(j + 1) * HQ], keys[j], NT, preferred_element_type=F32
        ) * HD ** (-0.5)
        scores = jnp.where(slots < length_ref[j], scores, -jnp.inf)
        expo = jnp.exp(scores - jnp.max(scores, axis=1, keepdims=True))
        probs = (expo * (1.0 / jnp.sum(expo, axis=1, keepdims=True))).astype(BF16)
        streams[j][1].wait()
        if j < 2:
            streams[j + 2][1].start()
        return jnp.dot(probs, values[j], preferred_element_type=F32).astype(BF16)

    def place_pair(t, first, second):
        heads[:HQ, :] = first
        heads[HQ:, :] = second
        row = lax.broadcasted_iota(jnp.int32, (64, 64), 0)
        col = lax.broadcasted_iota(jnp.int32, (64, 64), 1)
        source = lax.rem(row, 2) * HQ + (lax.rem(row, 16) // 2) * 4 + row // 16
        turn = (col == source).astype(BF16)
        context = jnp.dot(turn, heads[...], preferred_element_type=F32).astype(BF16)
        for n in range(4):
            ctx_all[t, y_me, z_me, :, n * HD:(n + 1) * HD] = context[n * 16:(n + 1) * 16]

    def send_near(t):
        for d in (2, 1, 3):
            for h, axis in enumerate(("y", "z")):
                view = ctx_all.at[t, y_me, z_me, :, h * 512:(h + 1) * 512]
                near[t].append(send(
                    view, view, asem.at[t, h, d - 1], arsem.at[t, h, d - 1],
                    device_at(pos, **{axis: d}),
                ))

    def send_far(t):
        for copy in near[t]:
            copy.wait_recv()
        for d in (2, 1, 3):
            for h, axis in enumerate(("z", "y")):
                if h == 0:
                    view = ctx_all.at[t, :, z_me, :, :512]
                else:
                    view = ctx_all.at[t, y_me, :, :, 512:]
                far[t].append(send(
                    view, view, asem.at[t, h, 2 + d], arsem.at[t, h, 2 + d],
                    device_at(pos, **{axis: d}),
                ))

    place_pair(0, attend(0), attend(1))
    pl.semaphore_wait(barrier, len(partners))
    send_near(0)
    third = attend(2)
    for copy in loads:
        copy.start()
    send_far(0)
    place_pair(1, third, attend(3))
    send_near(1)
    send_far(1)
    w_out = send(wd_ref, wd.at[BLOCK:, :MODEL_WIDTH], cssem.at[0], crsem.at[0], peer)
    a_out = send(al_ref, wd.at[BLOCK:, MODEL_WIDTH:], cssem.at[1], crsem.at[1], peer)

    row = lax.broadcasted_iota(jnp.int32, (256, 256), 0)
    col = lax.broadcasted_iota(jnp.int32, (256, 256), 1)
    split = (row == 2 * lax.rem(col, 128) + col // 128).astype(BF16)

    def turn_columns(i):
        start = i * 768
        for group in range(4):
            count = min(128, 448 - group * 128)
            lanes = slice(group * 128, group * 128 + count)
            both = wraw[lanes, :, start:start + 768].reshape(2 * count, 768).T
            turned = jnp.dot(
                both, split[:2 * count], preferred_element_type=F32
            ).astype(BF16)
            for s in range(2):
                for g in range(48):
                    n = start + 16 * g
                    k = n % BLOCK
                    at = (n // BLOCK) * PAIR
                    if k < CUT:
                        at += s * CUT + k
                    else:
                        at += 2 * CUT + s * (BLOCK - CUT) + k - CUT
                    wt[at:at + 16, lanes] = turned[
                        16 * g:16 * g + 16, s * 128:s * 128 + count
                    ]

    load_w.wait()
    turn_columns(0)
    load_res.wait()
    load_wo.wait()

    row = lax.broadcasted_iota(jnp.int32, (128, 512), 0)
    col = lax.broadcasted_iota(jnp.int32, (128, 512), 1)
    f = x_me * 2 + c
    chosen = (col == (row // 8) * 32 + f * 4 + lax.rem(row, 4)).astype(BF16)
    stream = lax.dot_general(chosen, res[...], NT, preferred_element_type=F32)

    eighth = lax.rem(lax.broadcasted_iota(jnp.int32, (HALF, 448), 0), 16) // 2
    pairs = []
    for t in range(2):
        for copy in far[t]:
            copy.wait_recv()
        projected = jnp.zeros((HALF, 448), F32)
        for q in range(8):
            r = lax.dot_general(
                ctx_all[t].reshape(HALF, 1024), wo[:, q * 1024:(q + 1) * 1024], NT,
                preferred_element_type=F32,
            )
            projected = jnp.where(eighth == q, r, projected)
        projected = projected.reshape(16, 16, 448)
        projected = projected[:, :8] + projected[:, 8:]
        projected = projected + pltpu.roll(projected, 4, 1)
        pairs.append((projected + pltpu.roll(projected, 2, 1)).reshape(128, 448))
        if t == 0:
            turn_columns(1)
    request = lax.rem(lax.broadcasted_iota(jnp.int32, (128, 448), 0), 4)
    projected = jnp.where(request < 2, pairs[0], pairs[1])
    stream = stream + projected
    normed = (stream * gain_ref[...].astype(F32).reshape(1, 448)).astype(BF16)
    row = lax.broadcasted_iota(jnp.int32, (64, 128), 0)
    col = lax.broadcasted_iota(jnp.int32, (64, 128), 1)
    pick = (col == (row // 4) * 8 + lax.rem(row, 4)).astype(BF16)
    z[c, x_me] = jnp.dot(pick, normed, preferred_element_type=F32).astype(BF16)
    along, across = [], []
    for d in (2, 1, 3):
        view = z.at[c, x_me]
        copy = send(view, view, zsem.at[d - 1], zrsem.at[d - 1], device_at(pos, x=d))
        along.append((d, copy))
    view = z.at[c, x_me]
    across.append(send(view, view, zsem.at[3], zrsem.at[3], peer))
    squares = jnp.sum(stream * stream, axis=1, keepdims=True)
    row = lax.broadcasted_iota(jnp.int32, (128, 128), 0)
    col = lax.rem(lax.broadcasted_iota(jnp.int32, (128, 128), 1), 64)
    spread = jnp.where(row == (col // 4) * 8 + lax.rem(col, 4), squares, 0.0)
    sq[y_me, z_me] = jnp.broadcast_to(jnp.sum(spread, axis=0, keepdims=True), (8, 128))
    sums = []
    for n, (dy, dz) in enumerate(plane):
        view = sq.at[y_me, z_me]
        copy = send(view, view, qsem.at[n], qrsem.at[n], device_at(pos, y=dy, z=dz))
        sums.append(copy)

    turn_columns(2)
    for d in (1, 3, 2):
        dict(along)[d].wait_recv()
        view = z.at[c, lax.rem(x_me + 4 - d, 4)]
        copy = send(view, view, zsem.at[3 + d], zrsem.at[3 + d], peer)
        across.append(copy)

    order = (c, 1 - c)

    def along_first(h, d):
        return device_at(pos, y=jnp.where(h == 0, d, 0), z=jnp.where(h == 0, 0, d))

    def along_second(h, d):
        return device_at(pos, y=jnp.where(h == 0, 0, d), z=jnp.where(h == 0, d, 0))

    def compute(h, p, lo, hi):
        def body(q, carry):
            a = jnp.where(h == 0, p * 4 + q, q * 4 + p)
            lhs = wt[pl.ds(pl.multiple_of(a * PAIR, PAIR), PAIR), :]
            r = lax.dot_general(
                lhs, z[h].reshape(HALF, 448), NT, preferred_element_type=F32
            ).astype(BF16)
            part[h, 0, p, q] = r[:, :128]
            part[h, 1, p, q] = r[:, 128:]
            return carry

        lax.fori_loop(lo, hi, body, 0)

    me1 = [jnp.where(h == 0, y_me, z_me) for h in order]
    me2 = [jnp.where(h == 0, z_me, y_me) for h in order]
    step = [[lax.rem(me1[n] + d, 4) for d in range(4)] for n in range(2)]
    one, two, three = {}, {}, {}
    for n, h in enumerate(order):
        if n == 1:
            for copy in across:
                copy.wait_recv()
        for side in range(2):
            compute(h, step[n][2], 2 * side, 2 * side + 2)
            for t, u in PARTS:
                one[n, t, u, side] = send(
                    part.at[h, t, step[n][2], 2 * side:2 * side + 2, ROWS[u]],
                    got_a.at[h, t, side, :, ROWS[u]],
                    ssem.at[h, t, u, side], rsem.at[h, t, u, side],
                    along_first(h, 1 if side == 0 else 3),
                )
    for n, h in enumerate(order):
        compute(h, step[n][1], 0, 4)
        compute(h, step[n][3], 0, 4)
    for t, u in PARTS:
        for n, h in enumerate(order):
            for side in range(2):
                to = 1 if side == 0 else 3
                p = step[n][to]
                one[n, t, u, side].wait_recv()
                for i in range(2):
                    q = 2 * side + i
                    part[h, t, p, q, ROWS[u]] = (
                        part[h, t, p, q, ROWS[u]].astype(F32)
                        + got_a[h, t, side, i, ROWS[u]].astype(F32)
                    ).astype(BF16)
                two[n, t, u, side] = send(
                    part.at[h, t, p, :, ROWS[u]], got_b.at[h, t, side, :, ROWS[u]],
                    ssem.at[h, t, u, 2 + side], rsem.at[h, t, u, 2 + side], along_first(h, to),
                )
    for n, h in enumerate(order):
        compute(h, step[n][0], 0, 4)
    for copy in sums:
        copy.wait_recv()
    squares = jnp.sum(sq[...].reshape(16, 8, 128), axis=0)
    iv[c, x_me] = lax.rsqrt(squares / MODEL_WIDTH + 1e-06)
    scales = []
    for n, (dx, dc) in enumerate(line):
        view = iv.at[c, x_me]
        scales.append(send(view, view, isem.at[n], irsem.at[n], device_at(pos, x=dx, c=dc)))
    for t, u in PARTS:
        for n, h in enumerate(order):
            for side in range(2):
                two[n, t, u, side].wait_recv()
            for d in (2, 1, 3):
                q = lax.rem(me2[n] + d, 4)
                summed[h, t, d - 1, ROWS[u]] = (
                    part[h, t, step[n][0], q, ROWS[u]].astype(F32)
                    + got_b[h, t, 0, q, ROWS[u]].astype(F32)
                    + got_b[h, t, 1, q, ROWS[u]].astype(F32)
                ).astype(BF16)
                three[n, t, u, d] = send(
                    summed.at[h, t, d - 1, ROWS[u]], got_c.at[h, t, d - 1, ROWS[u]],
                    ssem.at[h, t, u, 3 + d], rsem.at[h, t, u, 3 + d], along_second(h, d),
                )
    for copy in scales:
        copy.wait_recv()
    left = lax.broadcasted_iota(jnp.int32, (1, 128), 1) < 64
    h_out = []
    for t, u in PARTS:
        for n, h in ((1, 1 - c), (0, c)):
            inverse = jnp.where(left, iv[h, 2 * t, :1], iv[h, 2 * t + 1, :1])
            for d in (1, 2, 3):
                three[n, t, u, d].wait_recv()
            p, q = step[n][0], me2[n]
            both = (
                part[h, t, p, q, ROWS[u]].astype(F32)
                + got_b[h, t, 0, q, ROWS[u]].astype(F32)
                + got_b[h, t, 1, q, ROWS[u]].astype(F32)
                + got_c[h, t, 0, ROWS[u]].astype(F32) + got_c[h, t, 1, ROWS[u]].astype(F32)
                + got_c[h, t, 2, ROWS[u]].astype(F32)
            ) * inverse
            half = both.shape[0] // 2
            gate, lift = both[:half], both[half:]
            hidden = (gate / (1.0 + jnp.exp(-gate)) * lift).astype(BF16)
            if n == 1:
                hid[t, UNITS[u]] = hidden
                far_rows = slice(BLOCK + UNITS[u].start, BLOCK + UNITS[u].stop)
                h_out.append(send(
                    hid.at[t, UNITS[u]], hb.at[far_rows, t * 128:(t + 1) * 128],
                    cssem.at[2 + 2 * t + u], crsem.at[2 + 2 * t + u], peer,
                ))
            else:
                hb[UNITS[u], t * 128:(t + 1) * 128] = hidden

    for copy in (w_out, a_out, *h_out):
        copy.wait_recv()
    load_wd.wait()
    load_al.wait()

    row = lax.broadcasted_iota(jnp.int32, (HALF, HALF), 0)
    col = lax.broadcasted_iota(jnp.int32, (HALF, HALF), 1)
    place = {"x": 64, "y": 16, "z": 4}
    for k, axes in enumerate(FLOWS):
        source = lax.rem(row, 4)
        for n, axis in enumerate(axes):
            source = source + lax.rem(row // (64, 16, 4)[n], 4) * place[axis]
        turn = (source == col).astype(BF16)
        ht[k] = lax.dot_general(turn, hb[...], NT, preferred_element_type=F32).astype(BF16)

    out1 = [[[None] * 2 for _ in CHUNKS] for _ in FLOWS]
    outb = [[[None] * 2 for _ in CHUNKS] for _ in FLOWS]
    out2 = [[[None] * 3 for _ in CHUNKS] for _ in FLOWS]
    out3 = [[None] * 3 for _ in FLOWS]

    def rows_at(k, d):
        b = lax.rem(pos[FLOWS[k][0]] + d, 4)
        return pl.ds(pl.multiple_of(b * 64, 64), 64)

    for t, (start, middle, stop) in enumerate(CHUNKS):
        for k, axes in enumerate(FLOWS):
            rows1[k, :, start:stop] = jnp.dot(
                ht[k], wd[:, k * FLOW + start:k * FLOW + stop], preferred_element_type=F32
            ).astype(BF16)
            for side, cols in enumerate((slice(start, middle), slice(middle, stop))):
                out1[k][t][side] = send(
                    rows1.at[k, rows_at(k, 2), cols], got1.at[k, :, cols],
                    essem.at[k, t, side], ersem.at[k, t, side],
                    device_at(pos, **{axes[0]: 1 if side == 0 else 3}),
                )
    for t, (start, middle, stop) in enumerate(CHUNKS):
        for k, axes in enumerate(FLOWS):
            for side, cols in enumerate((slice(start, middle), slice(middle, stop))):
                to = 1 if side == 0 else 3
                out1[k][t][side].wait_recv()
                rows1[k, rows_at(k, to), cols] = (
                    rows1[k, rows_at(k, to), cols].astype(F32) + got1[k, :, cols].astype(F32)
                ).astype(BF16)
                outb[k][t][side] = send(
                    rows1.at[k, rows_at(k, to), start:stop], gotb.at[k, side, :, start:stop],
                    essem.at[k, t, 2 + side], ersem.at[k, t, 2 + side],
                    device_at(pos, **{axes[0]: to}),
                )
    for t, (start, middle, stop) in enumerate(CHUNKS):
        for k, axes in enumerate(FLOWS):
            for side in range(2):
                outb[k][t][side].wait_recv()
            mine = pos[axes[0]] * 64
            for i in range(4):
                at = pl.multiple_of(mine + i * 16, 16)
                here = slice(i * 16, (i + 1) * 16)
                rows2[k, i, :, start:stop] = (
                    rows1[k, pl.ds(at, 16), start:stop].astype(F32)
                    + gotb[k, 0, here, start:stop].astype(F32)
                    + gotb[k, 1, here, start:stop].astype(F32)
                ).astype(BF16)
            for d in (2, 1, 3):
                b = lax.rem(pos[axes[1]] + d, 4)
                out2[k][t][d - 1] = send(
                    rows2.at[k, b, :, start:stop], got2.at[k, d - 1, :, start:stop],
                    essem.at[k, t, 3 + d], ersem.at[k, t, 3 + d],
                    device_at(pos, **{axes[1]: d}),
                )
    wide[:, FLOW:] = jnp.zeros((16, 4 * PIECE - FLOW), F32)
    for k, axes in enumerate(FLOWS):
        for t in range(len(CHUNKS)):
            for d in range(3):
                out2[k][t][d].wait_recv()
        r = rows2[k, pos[axes[1]]].astype(F32)
        for d in range(3):
            r = r + got2[k, d].astype(F32)
        wide[:, :FLOW] = r
        for to in range(4):
            rows3[k, to] = jnp.concatenate(
                [wide[4 * to:4 * to + 4, n * PIECE:(n + 1) * PIECE] for n in range(4)], axis=0
            ).astype(BF16)
        for d in (2, 1, 3):
            b = lax.rem(pos[axes[2]] + d, 4)
            out3[k][d - 1] = send(
                rows3.at[k, b], got3.at[k, d - 1],
                fssem.at[k, d - 1], frsem.at[k, d - 1], device_at(pos, **{axes[2]: d}),
            )
    acc[...] = jnp.zeros(acc.shape, F32)
    for k, axes in enumerate(FLOWS):
        for d in range(3):
            out3[k][d].wait_recv()
        r = rows3[k, pos[axes[2]]].astype(F32)
        for d in range(3):
            r = r + got3[k, d].astype(F32)
        for n in range(4):
            width = min(PIECE, FLOW - n * PIECE)
            start = k * FLOW + n * PIECE
            acc[0:4, start:start + width] = r[4 * n:4 * n + 4, :width]

    low = acc[:, MODEL_WIDTH:]
    who = lax.broadcasted_iota(jnp.int32, low.shape, 0)
    owner = lax.broadcasted_iota(jnp.int32, low.shape, 1) // ADAPTER_RANK
    tenant = jnp.where(
        who == 0, tenant_ref[0],
        jnp.where(who == 1, tenant_ref[1], jnp.where(who == 2, tenant_ref[2], tenant_ref[3])),
    )
    load_up.wait()
    picked = jnp.where(owner == tenant, low, 0.0).astype(BF16)
    for n in range(7):
        cols = slice(n * 1024, (n + 1) * 1024)
        r = acc[:, cols] + jnp.dot(picked, up[:, cols], preferred_element_type=F32)
        out_ref[:, cols] = r[0:4]

    for copy in sent:
        copy.wait_send()


def feed(q, key, value, length, wo, res, gain, w, wd, al, up, tenant):
    vmem = pl.BlockSpec(memory_space=pltpu.VMEM)
    hbm = pl.BlockSpec(memory_space=pl.ANY)
    smem = pl.BlockSpec(memory_space=pltpu.SMEM)
    dma = pltpu.SemaphoreType.DMA
    return pl.pallas_call(
        feed_kernel,
        out_shape=jax.ShapeDtypeStruct((4, MODEL_WIDTH), F32),
        in_specs=[vmem, hbm, hbm, smem, hbm, hbm, vmem, hbm, hbm, hbm, hbm, smem],
        out_specs=vmem,
        scratch_shapes=[
            pltpu.VMEM((4, CACHE, HD), BF16),
            pltpu.VMEM((4, CACHE, HD), BF16),
            pltpu.VMEM((2 * HQ, HD), BF16),
            pltpu.VMEM((2, 4, 4, 16, 1024), BF16),
            pltpu.VMEM((448, 8192), BF16),
            pltpu.VMEM((448, 512), BF16),
            pltpu.VMEM((2, 4, 64, 448), BF16),
            pltpu.VMEM((4, 4, 8, 128), F32),
            pltpu.VMEM((2, 4, 8, 128), F32),
            pltpu.VMEM((448, 2, 2304), BF16),
            pltpu.VMEM((128, MODEL_WIDTH), BF16),
            pltpu.VMEM((16 * PAIR, 448), BF16),
            pltpu.VMEM((2, 2, 4, 4, PAIR, 128), BF16),
            pltpu.VMEM((2, 2, 2, 2, PAIR, 128), BF16),
            pltpu.VMEM((2, 2, 2, 4, PAIR, 128), BF16),
            pltpu.VMEM((2, 2, 3, PAIR, 128), BF16),
            pltpu.VMEM((2, 2, 3, PAIR, 128), BF16),
            pltpu.VMEM((2, BLOCK, 128), BF16),
            pltpu.VMEM((PAIR, WIDE), BF16),
            pltpu.VMEM((PAIR, HALF), BF16),
            pltpu.VMEM((3, HALF, PAIR), BF16),
            pltpu.VMEM((3, HALF, FLOW), BF16),
            pltpu.VMEM((3, 64, FLOW), BF16),
            pltpu.VMEM((3, 2, 64, FLOW), BF16),
            pltpu.VMEM((3, 4, 16, FLOW), BF16),
            pltpu.VMEM((3, 3, 16, FLOW), BF16),
            pltpu.VMEM((16, 4 * PIECE), F32),
            pltpu.VMEM((3, 4, 16, PIECE), BF16),
            pltpu.VMEM((3, 3, 16, PIECE), BF16),
            pltpu.VMEM((8, WIDE), F32),
            dma((2, 4)), dma((6,)), dma((2, 2, 6)), dma((2, 2, 6)), dma((15,)), dma((15,)),
            dma((7,)), dma((7,)), dma((7,)), dma((7,)),
            dma((2, 2, 2, 7)), dma((2, 2, 2, 7)), dma((6,)), dma((6,)),
            dma((3, 2, 7)), dma((3, 2, 7)), dma((3, 3)), dma((3, 3)),
        ],
        compiler_params=pltpu.CompilerParams(
            collective_id=1, has_side_effects=True, vmem_limit_bytes=58 << 20
        ),
    )(q, key, value, length, wo, res, gain, w, wd, al, up, tenant)


def local(
    query,
    cached_key_rows,
    cached_value_rows,
    request_cache_length,
    request_tenant_index,
    residual,
    feedforward_norm_gain,
    attention_output_weight,
    gate_up_weight,
    down_projection_weight,
    adapter_down_maps,
    adapter_up_maps,
):
    result = feed(
        query.reshape(4, HQ, HD).transpose(1, 0, 2),
        cached_key_rows, cached_value_rows, request_cache_length,
        attention_output_weight.T, residual.T,
        feedforward_norm_gain, gate_up_weight,
        down_projection_weight.reshape(BLOCK, MODEL_WIDTH),
        adapter_down_maps.reshape(BLOCK, TENANT_COUNT * ADAPTER_RANK),
        adapter_up_maps, request_tenant_index,
    )
    return result.astype(BF16)


def solution(mesh):
    in_specs = (
        P(("attn", "ffn"), None),
        P(("attn", "ffn"), None, None),
        P(("attn", "ffn"), None, None),
        P(("attn", "ffn")),
        P(("attn", "ffn")),
        P(None, "attn"),
        P("attn"),
        P(None, "attn"),
        P("attn", None, "ffn"),
        P("ffn", "attn", None, None),
        P("ffn", "attn", None, None),
        P(),
    )
    out_specs = P(("attn", "ffn"), None)
    return jax.shard_map(local, mesh=mesh, in_specs=in_specs, out_specs=out_specs, check_vma=False)
```

```python
import functools

import jax
import jax.numpy as jnp
from jax import lax
from jax.experimental import pallas as pl
from jax.experimental.pallas import tpu as pltpu
from jax.sharding import PartitionSpec as P

MODEL_WIDTH = 7168
HQ = 32
HD = 256
CACHE = 2048
TENANT_COUNT = 8
ADAPTER_RANK = 16
MESH = pl.DeviceIdType.MESH
BLOCK = 144
PAIR = 2 * BLOCK
CUT = 80
ROWS = (slice(0, 2 * CUT), slice(2 * CUT, PAIR))
UNITS = (slice(0, CUT), slice(CUT, BLOCK))
PARTS = ((0, 0), (0, 1), (1, 0), (1, 1))
HALF = 256
WIDE = MODEL_WIDTH + TENANT_COUNT * ADAPTER_RANK
FLOW = WIDE // 3
PIECE = 640
NT = (((1,), (1,)), ((), ()))
F32 = jnp.float32
BF16 = jnp.bfloat16


def position():
    a = lax.axis_index("attn")
    f = lax.axis_index("ffn")
    return {"y": a // 4, "z": lax.rem(a, 4), "x": f // 2, "c": lax.rem(f, 2)}


def device_at(pos, **steps):
    y = lax.rem(pos["y"] + steps.get("y", 0), 4)
    z = lax.rem(pos["z"] + steps.get("z", 0), 4)
    x = lax.rem(pos["x"] + steps.get("x", 0), 4)
    c = lax.rem(pos["c"] + steps.get("c", 0), 2)
    return (y * 4 + z, x * 2 + c)


def send_to(sent, src, dst, send_sem, recv_sem, where):
    copy = pltpu.make_async_remote_copy(
        src_ref=src, dst_ref=dst, send_sem=send_sem, recv_sem=recv_sem,
        device_id=where, device_id_type=MESH,
    )
    copy.start()
    sent.append(copy)
    return copy


CHUNKS = ((0, 384, 768), (768, 1152, 1536), (1536, 2048, FLOW))
FLOWS = (("x", "y", "z"), ("y", "z", "x"), ("z", "x", "y"))


def feed_kernel(
    q_ref, key_ref, value_ref, length_ref,
    wo_ref, res_ref, gain_ref, w_ref, wd_ref, al_ref, up_ref, tenant_ref, out_ref,
    keys, values, heads, ctx_all, wo, res, z, sq, iv, wraw, up,
    wt, part, got_a, got_b, summed, got_c, hid, wd, hb, ht,
    rows1, got1, gotb, rows2, got2, wide, rows3, got3, acc,
    kvsem, lsem, asem, arsem, qsem, qrsem, zsem, zrsem, isem, irsem,
    ssem, rsem, cssem, crsem, essem, ersem, fssem, frsem,
):
    pos = position()
    sent = []
    send = functools.partial(send_to, sent)
    c = pos["c"]
    y_me, z_me, x_me = pos["y"], pos["z"], pos["x"]
    peer = device_at(pos, c=1)
    plane = [(dy, dz) for dy in range(4) for dz in range(4) if dy or dz]
    line = [(dx, dc) for dx in range(4) for dc in range(2) if dx or dc]
    partners = [device_at(pos, y=dy, z=dz) for dy, dz in plane]
    partners += [device_at(pos, x=dx, c=dc) for dx, dc in line]
    barrier = pltpu.get_barrier_semaphore()
    for partner in partners:
        pl.semaphore_signal(barrier, inc=1, device_id=partner, device_id_type=MESH)

    streams = [
        (
            pltpu.make_async_copy(key_ref.at[j], keys.at[j], kvsem.at[0, j]),
            pltpu.make_async_copy(value_ref.at[j], values.at[j], kvsem.at[1, j]),
        )
        for j in range(4)
    ]
    for j in range(2):
        for copy in streams[j]:
            copy.start()
    loads = [
        pltpu.make_async_copy(w_ref, wraw, lsem.at[0]),
        pltpu.make_async_copy(wo_ref, wo, lsem.at[1]),
        pltpu.make_async_copy(res_ref, res, lsem.at[2]),
        pltpu.make_async_copy(wd_ref, wd.at[:BLOCK, :MODEL_WIDTH], lsem.at[3]),
        pltpu.make_async_copy(al_ref, wd.at[:BLOCK, MODEL_WIDTH:], lsem.at[4]),
        pltpu.make_async_copy(up_ref, up, lsem.at[5]),
    ]
    load_w, load_wo, load_res, load_wd, load_al, load_up = loads

    row = lax.broadcasted_iota(jnp.int32, (128, 128), 0)
    col = lax.broadcasted_iota(jnp.int32, (128, 128), 1)
    turn = (col == lax.rem(row, HQ) * 4 + row // HQ).astype(BF16)
    queries = jnp.dot(
        turn, q_ref[...].reshape(128, HD), preferred_element_type=F32
    ).astype(BF16)
    slots = lax.broadcasted_iota(jnp.int32, (HQ, CACHE), 1)
    near = [[], []]
    far = [[], []]

    def attend(j):
        streams[j][0].wait()
        if j < 2:
            streams[j + 2][0].start()
        scores = lax.dot_general(
            queries[j * HQ:(j + 1) * HQ], keys[j], NT, preferred_element_type=F32
        ) * HD ** (-0.5)
        scores = jnp.where(slots < length_ref[j], scores, -jnp.inf)
        expo = jnp.exp(scores - jnp.max(scores, axis=1, keepdims=True))
        probs = (expo * (1.0 / jnp.sum(expo, axis=1, keepdims=True))).astype(BF16)
        streams[j][1].wait()
        if j < 2:
            streams[j + 2][1].start()
        return jnp.dot(probs, values[j], preferred_element_type=F32).astype(BF16)

    def place_pair(t, first, second):
        heads[:HQ, :] = first
        heads[HQ:, :] = second
        row = lax.broadcasted_iota(jnp.int32, (64, 64), 0)
        col = lax.broadcasted_iota(jnp.int32, (64, 64), 1)
        source = lax.rem(row, 2) * HQ + (lax.rem(row, 16) // 2) * 4 + row // 16
        turn = (col == source).astype(BF16)
        context = jnp.dot(turn, heads[...], preferred_element_type=F32).astype(BF16)
        for n in range(4):
            ctx_all[t, y_me, z_me, :, n * HD:(n + 1) * HD] = context[n * 16:(n + 1) * 16]

    def send_near(t):
        for d in (2, 1, 3):
            for h, axis in enumerate(("y", "z")):
                view = ctx_all.at[t, y_me, z_me, :, h * 512:(h + 1) * 512]
                near[t].append(send(
                    view, view, asem.at[t, h, d - 1], arsem.at[t, h, d - 1],
                    device_at(pos, **{axis: d}),
                ))

    def send_far(t):
        for copy in near[t]:
            copy.wait_recv()
        for d in (2, 1, 3):
            for h, axis in enumerate(("z", "y")):
                if h == 0:
                    view = ctx_all.at[t, :, z_me, :, :512]
                else:
                    view = ctx_all.at[t, y_me, :, :, 512:]
                far[t].append(send(
                    view, view, asem.at[t, h, 2 + d], arsem.at[t, h, 2 + d],
                    device_at(pos, **{axis: d}),
                ))

    place_pair(0, attend(0), attend(1))
    pl.semaphore_wait(barrier, len(partners))
    send_near(0)
    third = attend(2)
    for copy in loads:
        copy.start()
    send_far(0)
    place_pair(1, third, attend(3))
    send_near(1)
    send_far(1)
    w_out = send(wd_ref, wd.at[BLOCK:, :MODEL_WIDTH], cssem.at[0], crsem.at[0], peer)
    a_out = send(al_ref, wd.at[BLOCK:, MODEL_WIDTH:], cssem.at[1], crsem.at[1], peer)

    row = lax.broadcasted_iota(jnp.int32, (256, 256), 0)
    col = lax.broadcasted_iota(jnp.int32, (256, 256), 1)
    split = (row == 2 * lax.rem(col, 128) + col // 128).astype(BF16)

    def turn_columns(i):
        start = i * 768
        for group in range(4):
            count = min(128, 448 - group * 128)
            lanes = slice(group * 128, group * 128 + count)
            both = wraw[lanes, :, start:start + 768].reshape(2 * count, 768).T
            turned = jnp.dot(
                both, split[:2 * count], preferred_element_type=F32
            ).astype(BF16)
            for s in range(2):
                for g in range(48):
                    n = start + 16 * g
                    k = n % BLOCK
                    at = (n // BLOCK) * PAIR
                    if k < CUT:
                        at += s * CUT + k
                    else:
                        at += 2 * CUT + s * (BLOCK - CUT) + k - CUT
                    wt[at:at + 16, lanes] = turned[
                        16 * g:16 * g + 16, s * 128:s * 128 + count
                    ]

    load_w.wait()
    turn_columns(0)
    load_res.wait()
    load_wo.wait()

    row = lax.broadcasted_iota(jnp.int32, (128, 512), 0)
    col = lax.broadcasted_iota(jnp.int32, (128, 512), 1)
    f = x_me * 2 + c
    chosen = (col == (row // 8) * 32 + f * 4 + lax.rem(row, 4)).astype(BF16)
    stream = lax.dot_general(chosen, res[...], NT, preferred_element_type=F32)

    eighth = lax.rem(lax.broadcasted_iota(jnp.int32, (HALF, 448), 0), 16) // 2
    pairs = []
    for t in range(2):
        for copy in far[t]:
            copy.wait_recv()
        projected = jnp.zeros((HALF, 448), F32)
        for q in range(8):
            r = lax.dot_general(
                ctx_all[t].reshape(HALF, 1024), wo[:, q * 1024:(q + 1) * 1024], NT,
                preferred_element_type=F32,
            )
            projected = jnp.where(eighth == q, r, projected)
        projected = projected.reshape(16, 16, 448)
        projected = projected[:, :8] + projected[:, 8:]
        projected = projected + pltpu.roll(projected, 4, 1)
        pairs.append((projected + pltpu.roll(projected, 2, 1)).reshape(128, 448))
        if t == 0:
            turn_columns(1)
    request = lax.rem(lax.broadcasted_iota(jnp.int32, (128, 448), 0), 4)
    projected = jnp.where(request < 2, pairs[0], pairs[1])
    stream = stream + projected
    normed = (stream * gain_ref[...].astype(F32).reshape(1, 448)).astype(BF16)
    row = lax.broadcasted_iota(jnp.int32, (64, 128), 0)
    col = lax.broadcasted_iota(jnp.int32, (64, 128), 1)
    pick = (col == (row // 4) * 8 + lax.rem(row, 4)).astype(BF16)
    z[c, x_me] = jnp.dot(pick, normed, preferred_element_type=F32).astype(BF16)
    along, across = [], []
    for d in (2, 1, 3):
        view = z.at[c, x_me]
        copy = send(view, view, zsem.at[d - 1], zrsem.at[d - 1], device_at(pos, x=d))
        along.append((d, copy))
    view = z.at[c, x_me]
    across.append(send(view, view, zsem.at[3], zrsem.at[3], peer))
    squares = jnp.sum(stream * stream, axis=1, keepdims=True)
    row = lax.broadcasted_iota(jnp.int32, (128, 128), 0)
    col = lax.rem(lax.broadcasted_iota(jnp.int32, (128, 128), 1), 64)
    spread = jnp.where(row == (col // 4) * 8 + lax.rem(col, 4), squares, 0.0)
    sq[y_me, z_me] = jnp.broadcast_to(jnp.sum(spread, axis=0, keepdims=True), (8, 128))
    sums = []
    for n, (dy, dz) in enumerate(plane):
        view = sq.at[y_me, z_me]
        copy = send(view, view, qsem.at[n], qrsem.at[n], device_at(pos, y=dy, z=dz))
        sums.append(copy)

    turn_columns(2)
    for d in (1, 3, 2):
        dict(along)[d].wait_recv()
        view = z.at[c, lax.rem(x_me + 4 - d, 4)]
        copy = send(view, view, zsem.at[3 + d], zrsem.at[3 + d], peer)
        across.append(copy)

    order = (c, 1 - c)

    def along_first(h, d):
        return device_at(pos, y=jnp.where(h == 0, d, 0), z=jnp.where(h == 0, 0, d))

    def along_second(h, d):
        return device_at(pos, y=jnp.where(h == 0, 0, d), z=jnp.where(h == 0, d, 0))

    def compute(h, p, lo, hi):
        def body(q, carry):
            a = jnp.where(h == 0, p * 4 + q, q * 4 + p)
            lhs = wt[pl.ds(pl.multiple_of(a * PAIR, PAIR), PAIR), :]
            r = lax.dot_general(
                lhs, z[h].reshape(HALF, 448), NT, preferred_element_type=F32
            ).astype(BF16)
            part[h, 0, p, q] = r[:, :128]
            part[h, 1, p, q] = r[:, 128:]
            return carry

        lax.fori_loop(lo, hi, body, 0)

    me1 = [jnp.where(h == 0, y_me, z_me) for h in order]
    me2 = [jnp.where(h == 0, z_me, y_me) for h in order]
    step = [[lax.rem(me1[n] + d, 4) for d in range(4)] for n in range(2)]
    one, two, three = {}, {}, {}
    for n, h in enumerate(order):
        if n == 1:
            for copy in across:
                copy.wait_recv()
        for side in range(2):
            compute(h, step[n][2], 2 * side, 2 * side + 2)
            for t, u in PARTS:
                one[n, t, u, side] = send(
                    part.at[h, t, step[n][2], 2 * side:2 * side + 2, ROWS[u]],
                    got_a.at[h, t, side, :, ROWS[u]],
                    ssem.at[h, t, u, side], rsem.at[h, t, u, side],
                    along_first(h, 1 if side == 0 else 3),
                )
    for n, h in enumerate(order):
        compute(h, step[n][1], 0, 4)
        compute(h, step[n][3], 0, 4)
    for t, u in PARTS:
        for n, h in enumerate(order):
            for side in range(2):
                to = 1 if side == 0 else 3
                p = step[n][to]
                one[n, t, u, side].wait_recv()
                for i in range(2):
                    q = 2 * side + i
                    part[h, t, p, q, ROWS[u]] = (
                        part[h, t, p, q, ROWS[u]].astype(F32)
                        + got_a[h, t, side, i, ROWS[u]].astype(F32)
                    ).astype(BF16)
                two[n, t, u, side] = send(
                    part.at[h, t, p, :, ROWS[u]], got_b.at[h, t, side, :, ROWS[u]],
                    ssem.at[h, t, u, 2 + side], rsem.at[h, t, u, 2 + side], along_first(h, to),
                )
    for n, h in enumerate(order):
        compute(h, step[n][0], 0, 4)
    for copy in sums:
        copy.wait_recv()
    squares = jnp.sum(sq[...].reshape(16, 8, 128), axis=0)
    iv[c, x_me] = lax.rsqrt(squares / MODEL_WIDTH + 1e-06)
    scales = []
    for n, (dx, dc) in enumerate(line):
        view = iv.at[c, x_me]
        scales.append(send(view, view, isem.at[n], irsem.at[n], device_at(pos, x=dx, c=dc)))
    for t, u in PARTS:
        for n, h in enumerate(order):
            for side in range(2):
                two[n, t, u, side].wait_recv()
            for d in (2, 1, 3):
                q = lax.rem(me2[n] + d, 4)
                summed[h, t, d - 1, ROWS[u]] = (
                    part[h, t, step[n][0], q, ROWS[u]].astype(F32)
                    + got_b[h, t, 0, q, ROWS[u]].astype(F32)
                    + got_b[h, t, 1, q, ROWS[u]].astype(F32)
                ).astype(BF16)
                three[n, t, u, d] = send(
                    summed.at[h, t, d - 1, ROWS[u]], got_c.at[h, t, d - 1, ROWS[u]],
                    ssem.at[h, t, u, 3 + d], rsem.at[h, t, u, 3 + d], along_second(h, d),
                )
    for copy in scales:
        copy.wait_recv()
    left = lax.broadcasted_iota(jnp.int32, (1, 128), 1) < 64
    h_out = []
    for t, u in PARTS:
        for n, h in ((1, 1 - c), (0, c)):
            inverse = jnp.where(left, iv[h, 2 * t, :1], iv[h, 2 * t + 1, :1])
            for d in (1, 2, 3):
                three[n, t, u, d].wait_recv()
            p, q = step[n][0], me2[n]
            both = (
                part[h, t, p, q, ROWS[u]].astype(F32)
                + got_b[h, t, 0, q, ROWS[u]].astype(F32)
                + got_b[h, t, 1, q, ROWS[u]].astype(F32)
                + got_c[h, t, 0, ROWS[u]].astype(F32) + got_c[h, t, 1, ROWS[u]].astype(F32)
                + got_c[h, t, 2, ROWS[u]].astype(F32)
            ) * inverse
            half = both.shape[0] // 2
            gate, lift = both[:half], both[half:]
            hidden = (gate / (1.0 + jnp.exp(-gate)) * lift).astype(BF16)
            if n == 1:
                hid[t, UNITS[u]] = hidden
                far_rows = slice(BLOCK + UNITS[u].start, BLOCK + UNITS[u].stop)
                h_out.append(send(
                    hid.at[t, UNITS[u]], hb.at[far_rows, t * 128:(t + 1) * 128],
                    cssem.at[2 + 2 * t + u], crsem.at[2 + 2 * t + u], peer,
                ))
            else:
                hb[UNITS[u], t * 128:(t + 1) * 128] = hidden

    for copy in (w_out, a_out, *h_out):
        copy.wait_recv()
    load_wd.wait()
    load_al.wait()

    row = lax.broadcasted_iota(jnp.int32, (HALF, HALF), 0)
    col = lax.broadcasted_iota(jnp.int32, (HALF, HALF), 1)
    place = {"x": 64, "y": 16, "z": 4}
    for k, axes in enumerate(FLOWS):
        source = lax.rem(row, 4)
        for n, axis in enumerate(axes):
            source = source + lax.rem(row // (64, 16, 4)[n], 4) * place[axis]
        turn = (source == col).astype(BF16)
        ht[k] = lax.dot_general(turn, hb[...], NT, preferred_element_type=F32).astype(BF16)

    out1 = [[[None] * 2 for _ in CHUNKS] for _ in FLOWS]
    outb = [[[None] * 2 for _ in CHUNKS] for _ in FLOWS]
    out2 = [[[None] * 3 for _ in CHUNKS] for _ in FLOWS]
    out3 = [[None] * 3 for _ in FLOWS]

    def rows_at(k, d):
        b = lax.rem(pos[FLOWS[k][0]] + d, 4)
        return pl.ds(pl.multiple_of(b * 64, 64), 64)

    for t, (start, middle, stop) in enumerate(CHUNKS):
        for k, axes in enumerate(FLOWS):
            rows1[k, :, start:stop] = jnp.dot(
                ht[k], wd[:, k * FLOW + start:k * FLOW + stop], preferred_element_type=F32
            ).astype(BF16)
            for side, cols in enumerate((slice(start, middle), slice(middle, stop))):
                out1[k][t][side] = send(
                    rows1.at[k, rows_at(k, 2), cols], got1.at[k, :, cols],
                    essem.at[k, t, side], ersem.at[k, t, side],
                    device_at(pos, **{axes[0]: 1 if side == 0 else 3}),
                )
    for t, (start, middle, stop) in enumerate(CHUNKS):
        for k, axes in enumerate(FLOWS):
            for side, cols in enumerate((slice(start, middle), slice(middle, stop))):
                to = 1 if side == 0 else 3
                out1[k][t][side].wait_recv()
                rows1[k, rows_at(k, to), cols] = (
                    rows1[k, rows_at(k, to), cols].astype(F32) + got1[k, :, cols].astype(F32)
                ).astype(BF16)
                outb[k][t][side] = send(
                    rows1.at[k, rows_at(k, to), start:stop], gotb.at[k, side, :, start:stop],
                    essem.at[k, t, 2 + side], ersem.at[k, t, 2 + side],
                    device_at(pos, **{axes[0]: to}),
                )
    for t, (start, middle, stop) in enumerate(CHUNKS):
        for k, axes in enumerate(FLOWS):
            for side in range(2):
                outb[k][t][side].wait_recv()
            mine = pos[axes[0]] * 64
            for i in range(4):
                at = pl.multiple_of(mine + i * 16, 16)
                here = slice(i * 16, (i + 1) * 16)
                rows2[k, i, :, start:stop] = (
                    rows1[k, pl.ds(at, 16), start:stop].astype(F32)
                    + gotb[k, 0, here, start:stop].astype(F32)
                    + gotb[k, 1, here, start:stop].astype(F32)
                ).astype(BF16)
            for d in (2, 1, 3):
                b = lax.rem(pos[axes[1]] + d, 4)
                out2[k][t][d - 1] = send(
                    rows2.at[k, b, :, start:stop], got2.at[k, d - 1, :, start:stop],
                    essem.at[k, t, 3 + d], ersem.at[k, t, 3 + d],
                    device_at(pos, **{axes[1]: d}),
                )
    wide[:, FLOW:] = jnp.zeros((16, 4 * PIECE - FLOW), F32)
    for k, axes in enumerate(FLOWS):
        for t in range(len(CHUNKS)):
            for d in range(3):
                out2[k][t][d].wait_recv()
        r = rows2[k, pos[axes[1]]].astype(F32)
        for d in range(3):
            r = r + got2[k, d].astype(F32)
        wide[:, :FLOW] = r
        for to in range(4):
            rows3[k, to] = jnp.concatenate(
                [wide[4 * to:4 * to + 4, n * PIECE:(n + 1) * PIECE] for n in range(4)], axis=0
            ).astype(BF16)
        for d in (2, 1, 3):
            b = lax.rem(pos[axes[2]] + d, 4)
            out3[k][d - 1] = send(
                rows3.at[k, b], got3.at[k, d - 1],
                fssem.at[k, d - 1], frsem.at[k, d - 1], device_at(pos, **{axes[2]: d}),
            )
    acc[...] = jnp.zeros(acc.shape, F32)
    for k, axes in enumerate(FLOWS):
        for d in range(3):
            out3[k][d].wait_recv()
        r = rows3[k, pos[axes[2]]].astype(F32)
        for d in range(3):
            r = r + got3[k, d].astype(F32)
        for n in range(4):
            width = min(PIECE, FLOW - n * PIECE)
            start = k * FLOW + n * PIECE
            acc[0:4, start:start + width] = r[4 * n:4 * n + 4, :width]

    low = acc[:, MODEL_WIDTH:]
    who = lax.broadcasted_iota(jnp.int32, low.shape, 0)
    owner = lax.broadcasted_iota(jnp.int32, low.shape, 1) // ADAPTER_RANK
    tenant = jnp.where(
        who == 0, tenant_ref[0],
        jnp.where(who == 1, tenant_ref[1], jnp.where(who == 2, tenant_ref[2], tenant_ref[3])),
    )
    load_up.wait()
    picked = jnp.where(owner == tenant, low, 0.0).astype(BF16)
    for n in range(7):
        cols = slice(n * 1024, (n + 1) * 1024)
        r = acc[:, cols] + jnp.dot(picked, up[:, cols], preferred_element_type=F32)
        out_ref[:, cols] = r[0:4]

    for copy in sent:
        copy.wait_send()


def feed(q, key, value, length, wo, res, gain, w, wd, al, up, tenant):
    vmem = pl.BlockSpec(memory_space=pltpu.VMEM)
    hbm = pl.BlockSpec(memory_space=pl.ANY)
    smem = pl.BlockSpec(memory_space=pltpu.SMEM)
    dma = pltpu.SemaphoreType.DMA
    return pl.pallas_call(
        feed_kernel,
        out_shape=jax.ShapeDtypeStruct((4, MODEL_WIDTH), F32),
        in_specs=[vmem, hbm, hbm, smem, hbm, hbm, vmem, hbm, hbm, hbm, hbm, smem],
        out_specs=vmem,
        scratch_shapes=[
            pltpu.VMEM((4, CACHE, HD), BF16),
            pltpu.VMEM((4, CACHE, HD), BF16),
            pltpu.VMEM((2 * HQ, HD), BF16),
            pltpu.VMEM((2, 4, 4, 16, 1024), BF16),
            pltpu.VMEM((448, 8192), BF16),
            pltpu.VMEM((448, 512), BF16),
            pltpu.VMEM((2, 4, 64, 448), BF16),
            pltpu.VMEM((4, 4, 8, 128), F32),
            pltpu.VMEM((2, 4, 8, 128), F32),
            pltpu.VMEM((448, 2, 2304), BF16),
            pltpu.VMEM((128, MODEL_WIDTH), BF16),
            pltpu.VMEM((16 * PAIR, 448), BF16),
            pltpu.VMEM((2, 2, 4, 4, PAIR, 128), BF16),
            pltpu.VMEM((2, 2, 2, 2, PAIR, 128), BF16),
            pltpu.VMEM((2, 2, 2, 4, PAIR, 128), BF16),
            pltpu.VMEM((2, 2, 3, PAIR, 128), BF16),
            pltpu.VMEM((2, 2, 3, PAIR, 128), BF16),
            pltpu.VMEM((2, BLOCK, 128), BF16),
            pltpu.VMEM((PAIR, WIDE), BF16),
            pltpu.VMEM((PAIR, HALF), BF16),
            pltpu.VMEM((3, HALF, PAIR), BF16),
            pltpu.VMEM((3, HALF, FLOW), BF16),
            pltpu.VMEM((3, 64, FLOW), BF16),
            pltpu.VMEM((3, 2, 64, FLOW), BF16),
            pltpu.VMEM((3, 4, 16, FLOW), BF16),
            pltpu.VMEM((3, 3, 16, FLOW), BF16),
            pltpu.VMEM((16, 4 * PIECE), F32),
            pltpu.VMEM((3, 4, 16, PIECE), BF16),
            pltpu.VMEM((3, 3, 16, PIECE), BF16),
            pltpu.VMEM((8, WIDE), F32),
            dma((2, 4)), dma((6,)), dma((2, 2, 6)), dma((2, 2, 6)), dma((15,)), dma((15,)),
            dma((7,)), dma((7,)), dma((7,)), dma((7,)),
            dma((2, 2, 2, 7)), dma((2, 2, 2, 7)), dma((6,)), dma((6,)),
            dma((3, 3, 7)), dma((3, 3, 7)), dma((3, 3)), dma((3, 3)),
        ],
        compiler_params=pltpu.CompilerParams(
            collective_id=1, has_side_effects=True, vmem_limit_bytes=58 << 20
        ),
    )(q, key, value, length, wo, res, gain, w, wd, al, up, tenant)


def local(
    query,
    cached_key_rows,
    cached_value_rows,
    request_cache_length,
    request_tenant_index,
    residual,
    feedforward_norm_gain,
    attention_output_weight,
    gate_up_weight,
    down_projection_weight,
    adapter_down_maps,
    adapter_up_maps,
):
    result = feed(
        query.reshape(4, HQ, HD).transpose(1, 0, 2),
        cached_key_rows, cached_value_rows, request_cache_length,
        attention_output_weight.T, residual.T,
        feedforward_norm_gain, gate_up_weight,
        down_projection_weight.reshape(BLOCK, MODEL_WIDTH),
        adapter_down_maps.reshape(BLOCK, TENANT_COUNT * ADAPTER_RANK),
        adapter_up_maps, request_tenant_index,
    )
    return result.astype(BF16)


def solution(mesh):
    in_specs = (
        P(("attn", "ffn"), None),
        P(("attn", "ffn"), None, None),
        P(("attn", "ffn"), None, None),
        P(("attn", "ffn")),
        P(("attn", "ffn")),
        P(None, "attn"),
        P("attn"),
        P(None, "attn"),
        P("attn", None, "ffn"),
        P("ffn", "attn", None, None),
        P("ffn", "attn", None, None),
        P(),
    )
    out_specs = P(("attn", "ffn"), None)
    return jax.shard_map(local, mesh=mesh, in_specs=in_specs, out_specs=out_specs, check_vma=False)
```

```python
import functools

import jax
import jax.numpy as jnp
from jax import lax
from jax.experimental import pallas as pl
from jax.experimental.pallas import tpu as pltpu
from jax.sharding import PartitionSpec as P

MODEL_WIDTH = 7168
HQ = 32
HD = 256
CACHE = 2048
TENANT_COUNT = 8
ADAPTER_RANK = 16
MESH = pl.DeviceIdType.MESH
BLOCK = 144
PAIR = 2 * BLOCK
CUT = 80
ROWS = (slice(0, 2 * CUT), slice(2 * CUT, PAIR))
UNITS = (slice(0, CUT), slice(CUT, BLOCK))
PARTS = ((0, 0), (0, 1), (1, 0), (1, 1))
HALF = 256
WIDE = MODEL_WIDTH + TENANT_COUNT * ADAPTER_RANK
FLOW = WIDE // 3
PIECE = 640
NT = (((1,), (1,)), ((), ()))
F32 = jnp.float32
BF16 = jnp.bfloat16


def position():
    a = lax.axis_index("attn")
    f = lax.axis_index("ffn")
    return {"y": a // 4, "z": lax.rem(a, 4), "x": f // 2, "c": lax.rem(f, 2)}


def device_at(pos, **steps):
    y = lax.rem(pos["y"] + steps.get("y", 0), 4)
    z = lax.rem(pos["z"] + steps.get("z", 0), 4)
    x = lax.rem(pos["x"] + steps.get("x", 0), 4)
    c = lax.rem(pos["c"] + steps.get("c", 0), 2)
    return (y * 4 + z, x * 2 + c)


def send_to(sent, src, dst, send_sem, recv_sem, where):
    copy = pltpu.make_async_remote_copy(
        src_ref=src, dst_ref=dst, send_sem=send_sem, recv_sem=recv_sem,
        device_id=where, device_id_type=MESH,
    )
    copy.start()
    sent.append(copy)
    return copy


CHUNKS = ((0, 256, 512), (512, 768, 1024), (1024, 1408, 1792), (1792, 2176, FLOW))
FLOWS = (("x", "y", "z"), ("y", "z", "x"), ("z", "x", "y"))


def feed_kernel(
    q_ref, key_ref, value_ref, length_ref,
    wo_ref, res_ref, gain_ref, w_ref, wd_ref, al_ref, up_ref, tenant_ref, out_ref,
    keys, values, heads, ctx_all, wo, res, z, sq, iv, wraw, up,
    wt, part, got_a, got_b, summed, got_c, hid, wd, hb, ht,
    rows1, got1, gotb, rows2, got2, wide, rows3, got3, acc,
    kvsem, lsem, asem, arsem, qsem, qrsem, zsem, zrsem, isem, irsem,
    ssem, rsem, cssem, crsem, essem, ersem, fssem, frsem,
):
    pos = position()
    sent = []
    send = functools.partial(send_to, sent)
    c = pos["c"]
    y_me, z_me, x_me = pos["y"], pos["z"], pos["x"]
    peer = device_at(pos, c=1)
    plane = [(dy, dz) for dy in range(4) for dz in range(4) if dy or dz]
    line = [(dx, dc) for dx in range(4) for dc in range(2) if dx or dc]
    partners = [device_at(pos, y=dy, z=dz) for dy, dz in plane]
    partners += [device_at(pos, x=dx, c=dc) for dx, dc in line]
    barrier = pltpu.get_barrier_semaphore()
    for partner in partners:
        pl.semaphore_signal(barrier, inc=1, device_id=partner, device_id_type=MESH)

    streams = [
        (
            pltpu.make_async_copy(key_ref.at[j], keys.at[j], kvsem.at[0, j]),
            pltpu.make_async_copy(value_ref.at[j], values.at[j], kvsem.at[1, j]),
        )
        for j in range(4)
    ]
    for j in range(2):
        for copy in streams[j]:
            copy.start()
    loads = [
        pltpu.make_async_copy(w_ref, wraw, lsem.at[0]),
        pltpu.make_async_copy(wo_ref, wo, lsem.at[1]),
        pltpu.make_async_copy(res_ref, res, lsem.at[2]),
        pltpu.make_async_copy(wd_ref, wd.at[:BLOCK, :MODEL_WIDTH], lsem.at[3]),
        pltpu.make_async_copy(al_ref, wd.at[:BLOCK, MODEL_WIDTH:], lsem.at[4]),
        pltpu.make_async_copy(up_ref, up, lsem.at[5]),
    ]
    load_w, load_wo, load_res, load_wd, load_al, load_up = loads

    row = lax.broadcasted_iota(jnp.int32, (128, 128), 0)
    col = lax.broadcasted_iota(jnp.int32, (128, 128), 1)
    turn = (col == lax.rem(row, HQ) * 4 + row // HQ).astype(BF16)
    queries = jnp.dot(
        turn, q_ref[...].reshape(128, HD), preferred_element_type=F32
    ).astype(BF16)
    slots = lax.broadcasted_iota(jnp.int32, (HQ, CACHE), 1)
    near = [[], []]
    far = [[], []]

    def attend(j):
        streams[j][0].wait()
        if j < 2:
            streams[j + 2][0].start()
        scores = lax.dot_general(
            queries[j * HQ:(j + 1) * HQ], keys[j], NT, preferred_element_type=F32
        ) * HD ** (-0.5)
        scores = jnp.where(slots < length_ref[j], scores, -jnp.inf)
        expo = jnp.exp(scores - jnp.max(scores, axis=1, keepdims=True))
        probs = (expo * (1.0 / jnp.sum(expo, axis=1, keepdims=True))).astype(BF16)
        streams[j][1].wait()
        if j < 2:
            streams[j + 2][1].start()
        return jnp.dot(probs, values[j], preferred_element_type=F32).astype(BF16)

    def place_pair(t, first, second):
        heads[:HQ, :] = first
        heads[HQ:, :] = second
        row = lax.broadcasted_iota(jnp.int32, (64, 64), 0)
        col = lax.broadcasted_iota(jnp.int32, (64, 64), 1)
        source = lax.rem(row, 2) * HQ + (lax.rem(row, 16) // 2) * 4 + row // 16
        turn = (col == source).astype(BF16)
        context = jnp.dot(turn, heads[...], preferred_element_type=F32).astype(BF16)
        for n in range(4):
            ctx_all[t, y_me, z_me, :, n * HD:(n + 1) * HD] = context[n * 16:(n + 1) * 16]

    def send_near(t):
        for d in (2, 1, 3):
            for h, axis in enumerate(("y", "z")):
                view = ctx_all.at[t, y_me, z_me, :, h * 512:(h + 1) * 512]
                near[t].append(send(
                    view, view, asem.at[t, h, d - 1], arsem.at[t, h, d - 1],
                    device_at(pos, **{axis: d}),
                ))

    def send_far(t):
        for copy in near[t]:
            copy.wait_recv()
        for d in (2, 1, 3):
            for h, axis in enumerate(("z", "y")):
                if h == 0:
                    view = ctx_all.at[t, :, z_me, :, :512]
                else:
                    view = ctx_all.at[t, y_me, :, :, 512:]
                far[t].append(send(
                    view, view, asem.at[t, h, 2 + d], arsem.at[t, h, 2 + d],
                    device_at(pos, **{axis: d}),
                ))

    place_pair(0, attend(0), attend(1))
    pl.semaphore_wait(barrier, len(partners))
    send_near(0)
    third = attend(2)
    for copy in loads:
        copy.start()
    send_far(0)
    place_pair(1, third, attend(3))
    send_near(1)
    send_far(1)
    w_out = send(wd_ref, wd.at[BLOCK:, :MODEL_WIDTH], cssem.at[0], crsem.at[0], peer)
    a_out = send(al_ref, wd.at[BLOCK:, MODEL_WIDTH:], cssem.at[1], crsem.at[1], peer)

    row = lax.broadcasted_iota(jnp.int32, (256, 256), 0)
    col = lax.broadcasted_iota(jnp.int32, (256, 256), 1)
    split = (row == 2 * lax.rem(col, 128) + col // 128).astype(BF16)

    def turn_columns(i):
        start = i * 768
        for group in range(4):
            count = min(128, 448 - group * 128)
            lanes = slice(group * 128, group * 128 + count)
            both = wraw[lanes, :, start:start + 768].reshape(2 * count, 768).T
            turned = jnp.dot(
                both, split[:2 * count], preferred_element_type=F32
            ).astype(BF16)
            for s in range(2):
                for g in range(48):
                    n = start + 16 * g
                    k = n % BLOCK
                    at = (n // BLOCK) * PAIR
                    if k < CUT:
                        at += s * CUT + k
                    else:
                        at += 2 * CUT + s * (BLOCK - CUT) + k - CUT
                    wt[at:at + 16, lanes] = turned[
                        16 * g:16 * g + 16, s * 128:s * 128 + count
                    ]

    load_w.wait()
    turn_columns(0)
    load_res.wait()
    load_wo.wait()

    row = lax.broadcasted_iota(jnp.int32, (128, 512), 0)
    col = lax.broadcasted_iota(jnp.int32, (128, 512), 1)
    f = x_me * 2 + c
    chosen = (col == (row // 8) * 32 + f * 4 + lax.rem(row, 4)).astype(BF16)
    stream = lax.dot_general(chosen, res[...], NT, preferred_element_type=F32)

    eighth = lax.rem(lax.broadcasted_iota(jnp.int32, (HALF, 448), 0), 16) // 2
    pairs = []
    for t in range(2):
        for copy in far[t]:
            copy.wait_recv()
        projected = jnp.zeros((HALF, 448), F32)
        for q in range(8):
            r = lax.dot_general(
                ctx_all[t].reshape(HALF, 1024), wo[:, q * 1024:(q + 1) * 1024], NT,
                preferred_element_type=F32,
            )
            projected = jnp.where(eighth == q, r, projected)
        projected = projected.reshape(16, 16, 448)
        projected = projected[:, :8] + projected[:, 8:]
        projected = projected + pltpu.roll(projected, 4, 1)
        pairs.append((projected + pltpu.roll(projected, 2, 1)).reshape(128, 448))
        if t == 0:
            turn_columns(1)
    request = lax.rem(lax.broadcasted_iota(jnp.int32, (128, 448), 0), 4)
    projected = jnp.where(request < 2, pairs[0], pairs[1])
    stream = stream + projected
    normed = (stream * gain_ref[...].astype(F32).reshape(1, 448)).astype(BF16)
    row = lax.broadcasted_iota(jnp.int32, (64, 128), 0)
    col = lax.broadcasted_iota(jnp.int32, (64, 128), 1)
    pick = (col == (row // 4) * 8 + lax.rem(row, 4)).astype(BF16)
    z[c, x_me] = jnp.dot(pick, normed, preferred_element_type=F32).astype(BF16)
    along, across = [], []
    for d in (2, 1, 3):
        view = z.at[c, x_me]
        copy = send(view, view, zsem.at[d - 1], zrsem.at[d - 1], device_at(pos, x=d))
        along.append((d, copy))
    view = z.at[c, x_me]
    across.append(send(view, view, zsem.at[3], zrsem.at[3], peer))
    squares = jnp.sum(stream * stream, axis=1, keepdims=True)
    row = lax.broadcasted_iota(jnp.int32, (128, 128), 0)
    col = lax.rem(lax.broadcasted_iota(jnp.int32, (128, 128), 1), 64)
    spread = jnp.where(row == (col // 4) * 8 + lax.rem(col, 4), squares, 0.0)
    sq[y_me, z_me] = jnp.broadcast_to(jnp.sum(spread, axis=0, keepdims=True), (8, 128))
    sums = []
    for n, (dy, dz) in enumerate(plane):
        view = sq.at[y_me, z_me]
        copy = send(view, view, qsem.at[n], qrsem.at[n], device_at(pos, y=dy, z=dz))
        sums.append(copy)

    turn_columns(2)
    for d in (1, 3, 2):
        dict(along)[d].wait_recv()
        view = z.at[c, lax.rem(x_me + 4 - d, 4)]
        copy = send(view, view, zsem.at[3 + d], zrsem.at[3 + d], peer)
        across.append(copy)

    order = (c, 1 - c)

    def along_first(h, d):
        return device_at(pos, y=jnp.where(h == 0, d, 0), z=jnp.where(h == 0, 0, d))

    def along_second(h, d):
        return device_at(pos, y=jnp.where(h == 0, 0, d), z=jnp.where(h == 0, d, 0))

    def compute(h, p, lo, hi):
        def body(q, carry):
            a = jnp.where(h == 0, p * 4 + q, q * 4 + p)
            lhs = wt[pl.ds(pl.multiple_of(a * PAIR, PAIR), PAIR), :]
            r = lax.dot_general(
                lhs, z[h].reshape(HALF, 448), NT, preferred_element_type=F32
            ).astype(BF16)
            part[h, 0, p, q] = r[:, :128]
            part[h, 1, p, q] = r[:, 128:]
            return carry

        lax.fori_loop(lo, hi, body, 0)

    me1 = [jnp.where(h == 0, y_me, z_me) for h in order]
    me2 = [jnp.where(h == 0, z_me, y_me) for h in order]
    step = [[lax.rem(me1[n] + d, 4) for d in range(4)] for n in range(2)]
    one, two, three = {}, {}, {}
    for n, h in enumerate(order):
        if n == 1:
            for copy in across:
                copy.wait_recv()
        for side in range(2):
            compute(h, step[n][2], 2 * side, 2 * side + 2)
            for t, u in PARTS:
                one[n, t, u, side] = send(
                    part.at[h, t, step[n][2], 2 * side:2 * side + 2, ROWS[u]],
                    got_a.at[h, t, side, :, ROWS[u]],
                    ssem.at[h, t, u, side], rsem.at[h, t, u, side],
                    along_first(h, 1 if side == 0 else 3),
                )
    for n, h in enumerate(order):
        compute(h, step[n][1], 0, 4)
        compute(h, step[n][3], 0, 4)
    for t, u in PARTS:
        for n, h in enumerate(order):
            for side in range(2):
                to = 1 if side == 0 else 3
                p = step[n][to]
                one[n, t, u, side].wait_recv()
                for i in range(2):
                    q = 2 * side + i
                    part[h, t, p, q, ROWS[u]] = (
                        part[h, t, p, q, ROWS[u]].astype(F32)
                        + got_a[h, t, side, i, ROWS[u]].astype(F32)
                    ).astype(BF16)
                two[n, t, u, side] = send(
                    part.at[h, t, p, :, ROWS[u]], got_b.at[h, t, side, :, ROWS[u]],
                    ssem.at[h, t, u, 2 + side], rsem.at[h, t, u, 2 + side], along_first(h, to),
                )
    for n, h in enumerate(order):
        compute(h, step[n][0], 0, 4)
    for copy in sums:
        copy.wait_recv()
    squares = jnp.sum(sq[...].reshape(16, 8, 128), axis=0)
    iv[c, x_me] = lax.rsqrt(squares / MODEL_WIDTH + 1e-06)
    scales = []
    for n, (dx, dc) in enumerate(line):
        view = iv.at[c, x_me]
        scales.append(send(view, view, isem.at[n], irsem.at[n], device_at(pos, x=dx, c=dc)))
    for t, u in PARTS:
        for n, h in enumerate(order):
            for side in range(2):
                two[n, t, u, side].wait_recv()
            for d in (2, 1, 3):
                q = lax.rem(me2[n] + d, 4)
                summed[h, t, d - 1, ROWS[u]] = (
                    part[h, t, step[n][0], q, ROWS[u]].astype(F32)
                    + got_b[h, t, 0, q, ROWS[u]].astype(F32)
                    + got_b[h, t, 1, q, ROWS[u]].astype(F32)
                ).astype(BF16)
                three[n, t, u, d] = send(
                    summed.at[h, t, d - 1, ROWS[u]], got_c.at[h, t, d - 1, ROWS[u]],
                    ssem.at[h, t, u, 3 + d], rsem.at[h, t, u, 3 + d], along_second(h, d),
                )
    for copy in scales:
        copy.wait_recv()
    left = lax.broadcasted_iota(jnp.int32, (1, 128), 1) < 64
    h_out = []
    for t, u in PARTS:
        for n, h in ((1, 1 - c), (0, c)):
            inverse = jnp.where(left, iv[h, 2 * t, :1], iv[h, 2 * t + 1, :1])
            for d in (1, 2, 3):
                three[n, t, u, d].wait_recv()
            p, q = step[n][0], me2[n]
            both = (
                part[h, t, p, q, ROWS[u]].astype(F32)
                + got_b[h, t, 0, q, ROWS[u]].astype(F32)
                + got_b[h, t, 1, q, ROWS[u]].astype(F32)
                + got_c[h, t, 0, ROWS[u]].astype(F32) + got_c[h, t, 1, ROWS[u]].astype(F32)
                + got_c[h, t, 2, ROWS[u]].astype(F32)
            ) * inverse
            half = both.shape[0] // 2
            gate, lift = both[:half], both[half:]
            hidden = (gate / (1.0 + jnp.exp(-gate)) * lift).astype(BF16)
            if n == 1:
                hid[t, UNITS[u]] = hidden
                far_rows = slice(BLOCK + UNITS[u].start, BLOCK + UNITS[u].stop)
                h_out.append(send(
                    hid.at[t, UNITS[u]], hb.at[far_rows, t * 128:(t + 1) * 128],
                    cssem.at[2 + 2 * t + u], crsem.at[2 + 2 * t + u], peer,
                ))
            else:
                hb[UNITS[u], t * 128:(t + 1) * 128] = hidden

    for copy in (w_out, a_out, *h_out):
        copy.wait_recv()
    load_wd.wait()
    load_al.wait()

    row = lax.broadcasted_iota(jnp.int32, (HALF, HALF), 0)
    col = lax.broadcasted_iota(jnp.int32, (HALF, HALF), 1)
    place = {"x": 64, "y": 16, "z": 4}
    for k, axes in enumerate(FLOWS):
        source = lax.rem(row, 4)
        for n, axis in enumerate(axes):
            source = source + lax.rem(row // (64, 16, 4)[n], 4) * place[axis]
        turn = (source == col).astype(BF16)
        ht[k] = lax.dot_general(turn, hb[...], NT, preferred_element_type=F32).astype(BF16)

    out1 = [[[None] * 2 for _ in CHUNKS] for _ in FLOWS]
    outb = [[[None] * 2 for _ in CHUNKS] for _ in FLOWS]
    out2 = [[[None] * 3 for _ in CHUNKS] for _ in FLOWS]
    out3 = [[None] * 3 for _ in FLOWS]

    def rows_at(k, d):
        b = lax.rem(pos[FLOWS[k][0]] + d, 4)
        return pl.ds(pl.multiple_of(b * 64, 64), 64)

    for t, (start, middle, stop) in enumerate(CHUNKS):
        for k, axes in enumerate(FLOWS):
            rows1[k, :, start:stop] = jnp.dot(
                ht[k], wd[:, k * FLOW + start:k * FLOW + stop], preferred_element_type=F32
            ).astype(BF16)
            for side, cols in enumerate((slice(start, middle), slice(middle, stop))):
                out1[k][t][side] = send(
                    rows1.at[k, rows_at(k, 2), cols], got1.at[k, :, cols],
                    essem.at[k, t, side], ersem.at[k, t, side],
                    device_at(pos, **{axes[0]: 1 if side == 0 else 3}),
                )
    for t, (start, middle, stop) in enumerate(CHUNKS):
        for k, axes in enumerate(FLOWS):
            for side, cols in enumerate((slice(start, middle), slice(middle, stop))):
                to = 1 if side == 0 else 3
                out1[k][t][side].wait_recv()
                rows1[k, rows_at(k, to), cols] = (
                    rows1[k, rows_at(k, to), cols].astype(F32) + got1[k, :, cols].astype(F32)
                ).astype(BF16)
                outb[k][t][side] = send(
                    rows1.at[k, rows_at(k, to), start:stop], gotb.at[k, side, :, start:stop],
                    essem.at[k, t, 2 + side], ersem.at[k, t, 2 + side],
                    device_at(pos, **{axes[0]: to}),
                )
    for t, (start, middle, stop) in enumerate(CHUNKS):
        for k, axes in enumerate(FLOWS):
            for side in range(2):
                outb[k][t][side].wait_recv()
            mine = pos[axes[0]] * 64
            for i in range(4):
                at = pl.multiple_of(mine + i * 16, 16)
                here = slice(i * 16, (i + 1) * 16)
                rows2[k, i, :, start:stop] = (
                    rows1[k, pl.ds(at, 16), start:stop].astype(F32)
                    + gotb[k, 0, here, start:stop].astype(F32)
                    + gotb[k, 1, here, start:stop].astype(F32)
                ).astype(BF16)
            for d in (2, 1, 3):
                b = lax.rem(pos[axes[1]] + d, 4)
                out2[k][t][d - 1] = send(
                    rows2.at[k, b, :, start:stop], got2.at[k, d - 1, :, start:stop],
                    essem.at[k, t, 3 + d], ersem.at[k, t, 3 + d],
                    device_at(pos, **{axes[1]: d}),
                )
    wide[:, FLOW:] = jnp.zeros((16, 4 * PIECE - FLOW), F32)
    for k, axes in enumerate(FLOWS):
        for t in range(len(CHUNKS)):
            for d in range(3):
                out2[k][t][d].wait_recv()
        r = rows2[k, pos[axes[1]]].astype(F32)
        for d in range(3):
            r = r + got2[k, d].astype(F32)
        wide[:, :FLOW] = r
        for to in range(4):
            rows3[k, to] = jnp.concatenate(
                [wide[4 * to:4 * to + 4, n * PIECE:(n + 1) * PIECE] for n in range(4)], axis=0
            ).astype(BF16)
        for d in (2, 1, 3):
            b = lax.rem(pos[axes[2]] + d, 4)
            out3[k][d - 1] = send(
                rows3.at[k, b], got3.at[k, d - 1],
                fssem.at[k, d - 1], frsem.at[k, d - 1], device_at(pos, **{axes[2]: d}),
            )
    acc[...] = jnp.zeros(acc.shape, F32)
    for k, axes in enumerate(FLOWS):
        for d in range(3):
            out3[k][d].wait_recv()
        r = rows3[k, pos[axes[2]]].astype(F32)
        for d in range(3):
            r = r + got3[k, d].astype(F32)
        for n in range(4):
            width = min(PIECE, FLOW - n * PIECE)
            start = k * FLOW + n * PIECE
            acc[0:4, start:start + width] = r[4 * n:4 * n + 4, :width]

    low = acc[:, MODEL_WIDTH:]
    who = lax.broadcasted_iota(jnp.int32, low.shape, 0)
    owner = lax.broadcasted_iota(jnp.int32, low.shape, 1) // ADAPTER_RANK
    tenant = jnp.where(
        who == 0, tenant_ref[0],
        jnp.where(who == 1, tenant_ref[1], jnp.where(who == 2, tenant_ref[2], tenant_ref[3])),
    )
    load_up.wait()
    picked = jnp.where(owner == tenant, low, 0.0).astype(BF16)
    for n in range(7):
        cols = slice(n * 1024, (n + 1) * 1024)
        r = acc[:, cols] + jnp.dot(picked, up[:, cols], preferred_element_type=F32)
        out_ref[:, cols] = r[0:4]

    for copy in sent:
        copy.wait_send()


def feed(q, key, value, length, wo, res, gain, w, wd, al, up, tenant):
    vmem = pl.BlockSpec(memory_space=pltpu.VMEM)
    hbm = pl.BlockSpec(memory_space=pl.ANY)
    smem = pl.BlockSpec(memory_space=pltpu.SMEM)
    dma = pltpu.SemaphoreType.DMA
    return pl.pallas_call(
        feed_kernel,
        out_shape=jax.ShapeDtypeStruct((4, MODEL_WIDTH), F32),
        in_specs=[vmem, hbm, hbm, smem, hbm, hbm, vmem, hbm, hbm, hbm, hbm, smem],
        out_specs=vmem,
        scratch_shapes=[
            pltpu.VMEM((4, CACHE, HD), BF16),
            pltpu.VMEM((4, CACHE, HD), BF16),
            pltpu.VMEM((2 * HQ, HD), BF16),
            pltpu.VMEM((2, 4, 4, 16, 1024), BF16),
            pltpu.VMEM((448, 8192), BF16),
            pltpu.VMEM((448, 512), BF16),
            pltpu.VMEM((2, 4, 64, 448), BF16),
            pltpu.VMEM((4, 4, 8, 128), F32),
            pltpu.VMEM((2, 4, 8, 128), F32),
            pltpu.VMEM((448, 2, 2304), BF16),
            pltpu.VMEM((128, MODEL_WIDTH), BF16),
            pltpu.VMEM((16 * PAIR, 448), BF16),
            pltpu.VMEM((2, 2, 4, 4, PAIR, 128), BF16),
            pltpu.VMEM((2, 2, 2, 2, PAIR, 128), BF16),
            pltpu.VMEM((2, 2, 2, 4, PAIR, 128), BF16),
            pltpu.VMEM((2, 2, 3, PAIR, 128), BF16),
            pltpu.VMEM((2, 2, 3, PAIR, 128), BF16),
            pltpu.VMEM((2, BLOCK, 128), BF16),
            pltpu.VMEM((PAIR, WIDE), BF16),
            pltpu.VMEM((PAIR, HALF), BF16),
            pltpu.VMEM((3, HALF, PAIR), BF16),
            pltpu.VMEM((3, HALF, FLOW), BF16),
            pltpu.VMEM((3, 64, FLOW), BF16),
            pltpu.VMEM((3, 2, 64, FLOW), BF16),
            pltpu.VMEM((3, 4, 16, FLOW), BF16),
            pltpu.VMEM((3, 3, 16, FLOW), BF16),
            pltpu.VMEM((16, 4 * PIECE), F32),
            pltpu.VMEM((3, 4, 16, PIECE), BF16),
            pltpu.VMEM((3, 3, 16, PIECE), BF16),
            pltpu.VMEM((8, WIDE), F32),
            dma((2, 4)), dma((6,)), dma((2, 2, 6)), dma((2, 2, 6)), dma((15,)), dma((15,)),
            dma((7,)), dma((7,)), dma((7,)), dma((7,)),
            dma((2, 2, 2, 7)), dma((2, 2, 2, 7)), dma((6,)), dma((6,)),
            dma((3, 4, 7)), dma((3, 4, 7)), dma((3, 3)), dma((3, 3)),
        ],
        compiler_params=pltpu.CompilerParams(
            collective_id=1, has_side_effects=True, vmem_limit_bytes=58 << 20
        ),
    )(q, key, value, length, wo, res, gain, w, wd, al, up, tenant)


def local(
    query,
    cached_key_rows,
    cached_value_rows,
    request_cache_length,
    request_tenant_index,
    residual,
    feedforward_norm_gain,
    attention_output_weight,
    gate_up_weight,
    down_projection_weight,
    adapter_down_maps,
    adapter_up_maps,
):
    result = feed(
        query.reshape(4, HQ, HD).transpose(1, 0, 2),
        cached_key_rows, cached_value_rows, request_cache_length,
        attention_output_weight.T, residual.T,
        feedforward_norm_gain, gate_up_weight,
        down_projection_weight.reshape(BLOCK, MODEL_WIDTH),
        adapter_down_maps.reshape(BLOCK, TENANT_COUNT * ADAPTER_RANK),
        adapter_up_maps, request_tenant_index,
    )
    return result.astype(BF16)


def solution(mesh):
    in_specs = (
        P(("attn", "ffn"), None),
        P(("attn", "ffn"), None, None),
        P(("attn", "ffn"), None, None),
        P(("attn", "ffn")),
        P(("attn", "ffn")),
        P(None, "attn"),
        P("attn"),
        P(None, "attn"),
        P("attn", None, "ffn"),
        P("ffn", "attn", None, None),
        P("ffn", "attn", None, None),
        P(),
    )
    out_specs = P(("attn", "ffn"), None)
    return jax.shard_map(local, mesh=mesh, in_specs=in_specs, out_specs=out_specs, check_vma=False)
```
